32 devices in a mesh: ga: 8 (over z, y), pair: 4 (over x, core).
Axes of the slice: x: 2, y: 2, z: 4, core: 2. Of those that a mesh axis runs over, the one named last changes fastest.
Arguments:
- val_density: bfloat16 [256, 3, 2, 8192], P('pair', None, None, 'ga'), may hold values from -0.0625 to 0.0625
- con_density: bfloat16 [576, 3, 2, 8192], P('ga', None, None, 'pair'), may hold values from -6 to 6
- screened: bfloat16 [3, 2, 8192, 8192], P(None, None, 'ga', 'pair'), may hold values from -0.0625 to 0.0625
- coulomb: float32 [3, 8192], P(None, 'ga'), may hold values from 0.2 to 2
- trans_here: bfloat16 [384, 2, 8192], P('pair', None, 'ga'), may hold values from -6 to 6
- trans_there: bfloat16 [384, 3, 2, 8192], P('pair', None, None, 'ga'), may hold values from -0.0625 to 0.0625
- shift_map: int32 [3, 8192], P(None, 'pair'), may hold values from 0 to 8191, as said below
- ordering: int32 [384], replicated, may hold values from 0 to 383, each once
Outputs:
- kernel: float32 [3, 2, 384, 384], P(None, None, 'pair', 'ga')
The draws below stay inside these ranges and needn't reach their ends.
Inputs may be any that keep to these rules, and one draw needn't show every extreme that they name: `shift_map`: each aligned block of 128 entries of a row is a permutation of that block's own G-vector indices.
All inputs are finite; a program needn't handle non-finite values.
Results may differ from the reference program's by a relative error of at most 0.0003.
Values may be sent and summed in bfloat16 or wider, within the bound.
No kernel may reach another device: no remote copies, remote signals or barrier semaphores. Data moves between devices by JAX's collectives and lax.ppermute only.
A program may use at most 192 MiB of HBM per device.

```python
import math
import jax
import jax.numpy as jnp
from jax import lax

NV = 16
NC = 24
NG = 8192
GBLK = 128
KSEL = 3
VV = 256
CC = 576
NT = 384


def draw_shift_map(key, part):
    scores = jax.random.randint(jax.random.fold_in(key, 11), (KSEL, NG // GBLK, GBLK), 0, 1 << 20)
    scores = scores * GBLK + jnp.arange(GBLK, dtype=jnp.int32)
    within = jnp.argsort(scores, axis=-1, stable=True).astype(jnp.int32)
    offsets = (jnp.arange(NG // GBLK, dtype=jnp.int32) * GBLK)[None, :, None]
    return (within + offsets).reshape(KSEL, NG)


def level_of(key, dims, cuts, least, largest):
    factor_of, own = 1.0, jax.random.fold_in(key, 6)
    for position, parts in cuts:
        steps = jnp.exp(jax.random.uniform(jax.random.fold_in(own, position), (parts,), jnp.float32, least / len(cuts), largest / len(cuts)))
        factor_of = factor_of * jnp.repeat(steps, dims[position] // parts).reshape([-1 if axis == position else 1 for axis in range(len(dims))])
    return factor_of


def normal_values(key, shape, scale, most, cuts=(), kind=jnp.bfloat16):
    level = level_of(key, shape, cuts, -0.22, 0.18) if cuts else 1.0
    array = jax.random.normal(key, shape, jnp.float32) * scale * level
    return jnp.minimum(jnp.maximum(array, -most), most).astype(kind)


def setup_inputs(seed: int = 0) -> dict:
    arg_keys = jax.random.split(jax.random.key(seed), 9)
    val_density = normal_values(arg_keys[0], (VV, KSEL, 2, NG), NG ** -0.5, 0.0625, ((0, 4), (3, 8)))
    con_density = normal_values(arg_keys[1], (CC, KSEL, 2, NG), 1.0, 6.0, ((0, 8), (3, 4)))
    screened = normal_values(arg_keys[2], (KSEL, 2, NG, NG), NG ** -0.5, 0.0625, ((2, 8), (3, 4)))
    coulomb = jnp.clip(jnp.exp(math.log(2.0) - 2.3025851 * jax.random.uniform(arg_keys[3], (KSEL, NG), jnp.float32) ** level_of(arg_keys[3], (KSEL, NG), ((1, 8),), -0.2, 0.2)), 0.2, 2.0)
    trans_here = normal_values(arg_keys[4], (NT, 2, NG), 1.0, 6.0, ((0, 4), (2, 8)))
    trans_there = normal_values(arg_keys[5], (NT, KSEL, 2, NG), NG ** -0.5, 0.0625, ((0, 4), (3, 8)))
    shift_map = draw_shift_map(jax.random.fold_in(arg_keys[8], 71), 0)
    ordering = jax.random.permutation(arg_keys[7], NT).astype(jnp.int32)
    return dict(val_density=val_density, con_density=con_density, screened=screened, coulomb=coulomb, trans_here=trans_here, trans_there=trans_there, shift_map=shift_map, ordering=ordering)


def complex_rows(left, right):
    high = lax.Precision.HIGHEST
    real_part = jnp.dot(left[0], right[0].T, precision=high) - jnp.dot(left[1], right[1].T, precision=high)
    imag_part = jnp.dot(left[0], right[1].T, precision=high) + jnp.dot(left[1], right[0].T, precision=high)
    return jnp.stack([real_part, imag_part], axis=0)


def reference(val_density, con_density, screened, coulomb, trans_here, trans_there, shift_map, ordering):
    lookup = jnp.broadcast_to(shift_map[None, :, None, :], con_density.shape).astype(jnp.int32)
    shifted = jnp.take_along_axis(con_density, lookup, axis=3).astype(jnp.float32)
    valence = val_density.astype(jnp.float32)
    here = trans_here.astype(jnp.float32)
    there = trans_there.astype(jnp.float32) * coulomb[None, :, None, :]

    def one_point(point):
        weights = screened[point].astype(jnp.float32)
        conduct = jnp.transpose(shifted[:, point], (1, 0, 2))
        screened_rows = jnp.stack([
            jnp.dot(conduct[0], weights[0].T, precision=lax.Precision.HIGHEST) - jnp.dot(conduct[1], weights[1].T, precision=lax.Precision.HIGHEST),
            jnp.dot(conduct[0], weights[1].T, precision=lax.Precision.HIGHEST) + jnp.dot(conduct[1], weights[0].T, precision=lax.Precision.HIGHEST)], axis=0)
        left = jnp.transpose(valence[:, point], (1, 0, 2))
        direct = complex_rows(left, screened_rows)
        outer = jnp.transpose(there[:, point], (1, 0, 2))
        exchange = complex_rows(jnp.transpose(here, (1, 0, 2)), outer)
        return direct, exchange

    direct, exchange = lax.map(one_point, jnp.arange(KSEL, dtype=jnp.int32))
    trans = jnp.arange(NT, dtype=jnp.int32)
    valence_band = trans // NC
    conduct_band = trans % NC
    row_pairs = valence_band[:, None] * NV + valence_band[None, :]
    col_pairs = conduct_band[:, None] * NC + conduct_band[None, :]
    regrouped = direct[:, :, row_pairs, col_pairs]
    natural = 2.0 * exchange - regrouped
    natural = natural[:, :, ordering, :]
    return natural[:, :, :, ordering]
```

```python
import math

import jax
import jax.numpy as jnp
from jax import lax
from jax.experimental import pallas as pl
from jax.experimental.pallas import tpu as pltpu
from jax.sharding import PartitionSpec as P

NV = 16
NC = 24
GBLK = 128
NT = 384

GROUP = 64
EXP_ROWS = 16
STEPS = 128.0
TOP = 32700.0
NT_DIMS = (((1,), (1,)), ((), ()))
VMEM = 56 * 1024 * 1024


def params():
    return pltpu.CompilerParams(vmem_limit_bytes=VMEM)


def cost(flops, moved):
    return pl.CostEstimate(flops=int(flops), bytes_accessed=int(moved), transcendentals=0)


def mm(left, right):
    return jnp.dot(left, right, preferred_element_type=jnp.float32)


def mm_nt(left, right):
    return lax.dot_general(left, right, NT_DIMS, preferred_element_type=jnp.float32)


def halves(value):
    high = value.astype(jnp.bfloat16)
    low = (value - high.astype(jnp.float32)).astype(jnp.bfloat16)
    return high, low


def encode(value, out_ref):
    rows, width = value.shape
    groups = rows // GROUP
    parts = value.reshape(groups, GROUP, width)
    largest = jnp.maximum(jnp.max(jnp.abs(parts), axis=1), 1e-30)
    level = jnp.ceil(jnp.log2(largest) * STEPS) + 1.0
    factor = TOP * jnp.exp2(level * (-1.0 / STEPS))
    coded = jnp.round(parts * factor[:, None, :]).astype(jnp.int32)
    out_ref[0:rows, :] = coded.reshape(rows, width).astype(jnp.int16)
    pad = jnp.zeros((EXP_ROWS - groups, width), jnp.int32)
    out_ref[rows : rows + EXP_ROWS, :] = jnp.concatenate(
        [level.astype(jnp.int32), pad], axis=0
    ).astype(jnp.int16)


def decode(ref):
    rows = ref.shape[0] - EXP_ROWS
    width = ref.shape[1]
    groups = rows // GROUP
    level = ref[rows : rows + EXP_ROWS, :].astype(jnp.int32).astype(jnp.float32)[0:groups]
    factor = jnp.exp2(level * (1.0 / STEPS)) * (1.0 / TOP)
    parts = ref[0:rows, :].astype(jnp.int32).astype(jnp.float32).reshape(groups, GROUP, width)
    return (parts * factor[:, None, :]).reshape(rows, width)


def shift_kernel(dest_ref, con_ref, map_ref, out_ref):
    rows, width = con_ref.shape[2], con_ref.shape[3]
    for block in range(width // GBLK):
        cols = slice(block * GBLK, (block + 1) * GBLK)
        within = jnp.bitwise_and(map_ref[0, 0:1, cols], GBLK - 1)
        source = lax.broadcasted_iota(jnp.int32, (GBLK, GBLK), 0)
        pick = (source == within).astype(jnp.float32).astype(jnp.bfloat16)
        for part in range(2):
            out_ref[0, 0, part, :, cols] = mm(con_ref[0, part, :, cols], pick).astype(jnp.bfloat16)


def shift_call(con, shift_map, dests, width):
    points, _, rows, _ = con.shape
    slots = dests.shape[0]
    grid_spec = pltpu.PrefetchScalarGridSpec(
        num_scalar_prefetch=1,
        grid=(points, slots),
        in_specs=[
            pl.BlockSpec((1, 2, rows, width), lambda q, k, dest: (q, 0, 0, dest[k])),
            pl.BlockSpec((1, 1, width), lambda q, k, dest: (q, 0, dest[k])),
        ],
        out_specs=pl.BlockSpec((1, 1, 2, rows, width), lambda q, k, dest: (k, q, 0, 0, 0)),
    )
    return pl.pallas_call(
        shift_kernel,
        grid_spec=grid_spec,
        out_shape=jax.ShapeDtypeStruct((slots, points, 2, rows, width), jnp.bfloat16),
        compiler_params=params(),
        cost_estimate=cost(2 * con.size * GBLK, 4 * con.size),
    )(dests, con, shift_map.reshape(points, 1, -1))


def x_kernel(coded, slots, base_ref, *refs):
    val_refs, (weight_ref, out_ref, left_ref) = refs[:slots], refs[slots:]
    rows, depth = val_refs[0].shape[1], val_refs[0].shape[2]
    half = slots * rows

    @pl.when(pl.program_id(0) == 0)
    def _():
        for slot in range(slots):
            real, imag = val_refs[slot][0], val_refs[slot][1]
            top = slice(slot * rows, (slot + 1) * rows)
            low = slice(half + slot * rows, half + (slot + 1) * rows)
            left_ref[top, 0:depth] = real
            left_ref[top, depth : 2 * depth] = -imag
            left_ref[low, 0:depth] = imag
            left_ref[low, depth : 2 * depth] = real

    weight = weight_ref[0].reshape(2 * depth, weight_ref.shape[3])
    product = mm(left_ref[...], weight)
    if coded:
        encode(product, out_ref)
    else:
        out_ref[...] = product


def x_call(vals, screened, point, base, width, tiles, coded):
    slots = len(vals)
    rows, depth = vals[0].shape[1], vals[0].shape[2]
    height = 2 * slots * rows
    out_rows, kind = (height + EXP_ROWS, jnp.int16) if coded else (height, jnp.float32)
    grid_spec = pltpu.PrefetchScalarGridSpec(
        num_scalar_prefetch=1,
        grid=(tiles,),
        in_specs=[pl.BlockSpec(v.shape, lambda j, b: (0, 0, 0)) for v in vals]
        + [pl.BlockSpec((1, 2, depth, width), lambda j, b: (point, 0, 0, b[0] + j))],
        out_specs=pl.BlockSpec((out_rows, width), lambda j, b: (0, j)),
        scratch_shapes=[pltpu.VMEM((height, 2 * depth), jnp.bfloat16)],
    )
    return pl.pallas_call(
        lambda *refs: x_kernel(coded, slots, *refs),
        grid_spec=grid_spec,
        out_shape=jax.ShapeDtypeStruct((out_rows, width * tiles), kind),
        compiler_params=params(),
        cost_estimate=cost(
            2 * height * 2 * depth * width * tiles,
            4 * depth * width * tiles + out_rows * width * tiles * 3,
        ),
    )(base, *vals, screened)


def hop_kernel(have, index_ref, *refs):
    if have:
        keep_up, near_up, got_up, keep_down, near_down, got_down, out_up, out_down = refs
    else:
        keep_up, near_up, keep_down, near_down, out_up, out_down = refs
        got_up = got_down = None
    for keep, near, got, out in (
        (keep_up, near_up, got_up, out_up),
        (keep_down, near_down, got_down, out_down),
    ):
        total = keep[...] + decode(near)
        if got is not None:
            total = total + decode(got)
        encode(total, out)


def hop_call(keep, near, got, index, width):
    height, tall = keep.shape[0], near.shape[0]
    in_specs, operands = [], []
    for way in range(2):
        in_specs += [
            pl.BlockSpec((height, width), lambda i, at, way=way: (0, at[way])),
            pl.BlockSpec((tall, width), lambda i, at, way=way: (0, at[way])),
        ]
        operands += [keep, near]
        if got is not None:
            in_specs.append(pl.BlockSpec((tall, width), lambda i, at: (0, 0)))
            operands.append(got[way])
    grid_spec = pltpu.PrefetchScalarGridSpec(
        num_scalar_prefetch=1,
        grid=(1,),
        in_specs=in_specs,
        out_specs=[pl.BlockSpec((tall, width), lambda i, at: (0, 0))] * 2,
    )
    return pl.pallas_call(
        lambda *refs: hop_kernel(got is not None, *refs),
        grid_spec=grid_spec,
        out_shape=[jax.ShapeDtypeStruct((tall, width), jnp.int16)] * 2,
        compiler_params=params(),
        cost_estimate=cost(40 * height * width, 16 * height * width),
    )(index, *operands)


def exchange_kernel(slots, *refs):
    here_refs, (there_ref, coulomb_ref, out_ref, left_ref) = refs[:slots], refs[slots:]
    rows, depth = here_refs[0].shape[1], here_refs[0].shape[2]

    @pl.when(pl.program_id(0) == 0)
    def _():
        for slot in range(slots):
            for part in range(2):
                left_ref[
                    slot * rows : (slot + 1) * rows, part * depth : (part + 1) * depth
                ] = here_refs[slot][part]

    factor = coulomb_ref[0]
    real = there_ref[0, 0].astype(jnp.float32) * factor
    imag = there_ref[0, 1].astype(jnp.float32) * factor
    right = jnp.concatenate(
        [jnp.concatenate([real, -imag], axis=1), jnp.concatenate([imag, real], axis=1)], axis=0
    )
    high, low = halves(right)
    left = left_ref[...]
    out_ref[0] = mm_nt(left, high) + mm_nt(left, low)


def exchange_call(heres, there, coulomb):
    slots = len(heres)
    points, _, cols, depth = there.shape
    rows = heres[0].shape[1]
    height = slots * rows
    return pl.pallas_call(
        lambda *refs: exchange_kernel(slots, *refs),
        grid=(points,),
        in_specs=[pl.BlockSpec(h.shape, lambda q: (0, 0, 0)) for h in heres]
        + [
            pl.BlockSpec((1, 2, cols, depth), lambda q: (q, 0, 0, 0)),
            pl.BlockSpec((1, 1, depth), lambda q: (q, 0, 0)),
        ],
        out_specs=pl.BlockSpec((1, height, 2 * cols), lambda q: (q, 0, 0)),
        out_shape=jax.ShapeDtypeStruct((points, height, 2 * cols), jnp.float32),
        scratch_shapes=[pltpu.VMEM((height, 2 * depth), jnp.bfloat16)],
        compiler_params=params(),
        cost_estimate=cost(2 * points * height * 2 * cols * 2 * depth * 2, 8 * points * cols * depth),
    )(*heres, there, coulomb.reshape(points, 1, depth))


def tile_kernel(slots, index_ref, *refs):
    con_refs = refs[:slots]
    (keep_ref, near_ref, up_ref, down_ref, exch_ref, row_ref, col_direct_ref, col_exch_ref) = refs[
        slots : slots + 8
    ]
    out_ref, con_all, direct_ref, natural_ref = refs[slots + 8 :]
    total = keep_ref[...] + decode(near_ref) + decode(up_ref) + decode(down_ref)
    pairs, width = total.shape[0] // 2, total.shape[1]
    rows = con_refs[0].shape[2]
    pitch = con_all.shape[0] // slots
    for slot in range(slots):
        for part in range(2):
            con_all[
                slot * pitch : slot * pitch + rows, part * width : (part + 1) * width
            ] = con_refs[slot][0, part]
    real, imag = total[:pairs], total[pairs:]
    right = jnp.concatenate(
        [jnp.concatenate([real, -imag], axis=1), jnp.concatenate([imag, real], axis=1)], axis=0
    )
    high, low = halves(right)
    left = con_all[...]
    direct = mm_nt(left, high) + mm_nt(left, low)
    lanes = direct_ref.shape[0]
    for slot in range(slots):
        start = pl.multiple_of(index_ref[1 + slot] * rows, 8)
        for lane in range(lanes):
            direct_ref[lane, pl.ds(start, rows), :] = direct[
                slot * pitch : slot * pitch + rows, lane * 128 : (lane + 1) * 128
            ]
    group = 128 // NV
    place = lax.broadcasted_iota(jnp.int32, (NC, 128), 1) // NV
    per_part = lanes // 2
    for part in range(2):
        for chunk in range(NC // group):
            for band in range(NV):
                block = jnp.zeros((NC, 128), jnp.float32)
                for step in range(group):
                    e = chunk * group + step
                    piece = direct_ref[part * per_part + band // group, pl.ds(e, NC, stride=NC), :]
                    turn = (NV * (step - band)) % 128
                    if turn:
                        piece = pltpu.roll(piece, turn, 1)
                    block = jnp.where(place == step, piece, block)
                at = part * NC * NV + chunk * 128
                natural_ref[band * NC : (band + 1) * NC, at : at + 128] = block
    pick_rows = row_ref[...]
    result = None
    for source, pick_cols in ((natural_ref[...], col_direct_ref), (exch_ref[0], col_exch_ref)):
        for piece in halves(source):
            moved = mm(pick_rows, piece).astype(jnp.bfloat16)
            term = mm(moved, pick_cols[...])
            result = term if result is None else result + term
    out_ref[...] = result


def tile_call(cons, point, keep, near, got, exch, index, pick_rows, col_direct, col_exch):
    slots = len(cons)
    _, _, rows, width = cons[0].shape
    height, tall = keep.shape[0], near.shape[0]
    pitch = -(-rows // 16) * 16
    out_cols = col_direct.shape[1]
    whole = lambda a: pl.BlockSpec(a.shape, lambda i, at: (0,) * a.ndim)
    grid_spec = pltpu.PrefetchScalarGridSpec(
        num_scalar_prefetch=1,
        grid=(1,),
        in_specs=[pl.BlockSpec((1, 2, rows, width), lambda i, at: (point, 0, 0, 0))] * slots
        + [
            pl.BlockSpec((height, width), lambda i, at: (0, at[0])),
            pl.BlockSpec((tall, width), lambda i, at: (0, at[0])),
            whole(got[0]),
            whole(got[1]),
            pl.BlockSpec((1,) + exch.shape[1:], lambda i, at: (point, 0, 0)),
            whole(pick_rows),
            whole(col_direct),
            whole(col_exch),
        ],
        out_specs=pl.BlockSpec((NT, out_cols), lambda i, at: (0, 0)),
        scratch_shapes=[
            pltpu.VMEM((slots * pitch, 2 * width), jnp.bfloat16),
            pltpu.VMEM((height // 128, NC * NC, 128), jnp.float32),
            pltpu.VMEM((NT, 2 * NT), jnp.float32),
        ],
    )
    return pl.pallas_call(
        lambda *refs: tile_kernel(slots, *refs),
        grid_spec=grid_spec,
        out_shape=jax.ShapeDtypeStruct((NT, out_cols), jnp.float32),
        compiler_params=params(),
        cost_estimate=cost(2.8e9, 8e6),
    )(index, *cons, keep, near, got[0], got[1], exch, pick_rows, col_direct, col_exch)


def swap(value, axis, size, bit):
    return lax.ppermute(value, axis, [(i, i ^ bit) for i in range(size)])


def gather_slots(value, axis, size):
    slots = [value]
    bit = size // 2
    found = {0: value}
    while bit:
        for known in sorted(found):
            found[known ^ bit] = swap(found[known], axis, size, bit)
        bit //= 2
    return [found[r] for r in range(size)]


def halving_order(bits):
    order = [0]
    for bit in reversed(bits):
        order = order + [o ^ bit for o in order]
    return order


def on_device(outer, inner, *args):
    (val_density, con_density, screened, coulomb, trans_here, trans_there, shift_map, ordering) = args
    ga, pair = outer * inner, lax.axis_size("pair")
    points = con_density.shape[1]
    slab = con_density.shape[3]
    width = slab // ga
    me_ga, me_pair = lax.axis_index("ga"), lax.axis_index("pair")
    me_outer, me_inner = me_ga // inner, me_ga % inner
    as_index = lambda *items: jnp.stack([jnp.asarray(i, jnp.int32) for i in items])

    val = jnp.transpose(val_density, (1, 2, 0, 3))
    vals = [gather_slots(val[q], "pair", pair) for q in range(points)]

    con = jnp.transpose(con_density, (1, 2, 0, 3))
    dests = me_ga ^ jnp.arange(ga, dtype=jnp.int32)
    dest_blocks = (dests % inner) * outer + dests // inner
    sends = shift_call(con, shift_map, dest_blocks, width)
    cons = [sends[0]] + [swap(sends[k], "ga", ga, k) for k in range(1, ga)]

    other, mine = as_index((1 - me_inner) * outer), as_index(me_inner * outer)
    gone = [x_call(vals[q], screened, q, other, width, outer, True) for q in range(points)]
    near = [swap(gone[q], "ga", ga, 1) for q in range(points)]
    keep = [x_call(vals[q], screened, q, mine, width, outer, False) for q in range(points)]

    here = jnp.transpose(trans_here, (1, 0, 2))
    heres = gather_slots(here, "pair", pair)
    there = jnp.transpose(trans_there, (1, 2, 0, 3))
    exch = exchange_call(heres, there, coulomb)

    row_bits, col_bits = [1 << b for b in range(pair.bit_length() - 1)], [1]
    col_bits += [1 << b for b in reversed(range(1, ga.bit_length() - 1))]
    row_count, col_count = NT // pair, NT // ga
    row_slots = jnp.asarray(halving_order(row_bits), jnp.int32)
    col_slots = jnp.asarray(halving_order(col_bits), jnp.int32)
    row_trans = ordering.reshape(pair, row_count)[me_pair ^ row_slots].reshape(-1)
    at_row = ((row_trans // row_count) ^ me_pair) * row_count + row_trans % row_count
    pick_rows = (at_row[:, None] == jnp.arange(NT, dtype=jnp.int32)[None, :]).astype(jnp.bfloat16)
    col_trans = ordering.reshape(ga, col_count)[me_ga ^ col_slots]
    fill = jnp.full((ga, 64 - col_count), -1, jnp.int32)
    at_direct = (col_trans % NC) * NV + col_trans // NC
    at_exch = jnp.where(col_trans // row_count == me_pair, col_trans % row_count, -1)

    def pick_cols(at, size, scale):
        real = jnp.concatenate([at, fill], axis=1)
        imag = jnp.where(real >= 0, real + size, -1)
        lanes = jnp.stack([real, imag], axis=1).reshape(1, -1)
        hot = lanes == jnp.arange(2 * size, dtype=jnp.int32)[:, None]
        return jnp.where(hot, scale, 0.0).astype(jnp.bfloat16)

    col_direct, col_exch = pick_cols(at_direct, NT, -1.0), pick_cols(at_exch, row_count, 2.0)

    up_pairs = [
        [(p * inner + y, (p + 1) * inner + y) for p in range(step) for y in range(inner)]
        for step in range(outer)
    ]
    last = outer - 1
    down_pairs = [
        [((last - p) * inner + y, (last - p - 1) * inner + y) for p in range(step) for y in range(inner)]
        for step in range(outer)
    ]
    hop_index = [
        as_index(
            jnp.clip(outer - step + me_outer, 0, last), jnp.clip(step - outer + me_outer, 0, last)
        )
        for step in range(outer)
    ]
    got = [None] * points
    for step in range(1, outer):
        for q in range(points):
            up, down = hop_call(keep[q], near[q], got[q], hop_index[step], width)
            got[q] = (
                lax.ppermute(up, "ga", up_pairs[step]),
                lax.ppermute(down, "ga", down_pairs[step]),
            )
    tile_index = jnp.concatenate([as_index(me_outer), dests])
    outs = []
    for q in range(points):
        part = tile_call(
            cons, q, keep[q], near[q], got[q], exch, tile_index, pick_rows, col_direct, col_exch
        )
        for bit in row_bits:
            half = part.shape[0] // 2
            part = part[:half] + swap(part[half:], "pair", pair, bit)
        for bit in col_bits:
            half = part.shape[1] // 2
            part = part[:, :half] + swap(part[:, half:], "ga", ga, bit)
        outs.append(jnp.stack([part[:, :col_count], part[:, 64 : 64 + col_count]]))
    return jnp.stack(outs)


def contract_float(left, right):
    high = lax.Precision.HIGHEST
    real_part = jnp.einsum(
        "nkg,mkg->nkm", left[:, :, 0], right[:, :, 0], precision=high
    ) - jnp.einsum("nkg,mkg->nkm", left[:, :, 1], right[:, :, 1], precision=high)
    imag_part = jnp.einsum(
        "nkg,mkg->nkm", left[:, :, 0], right[:, :, 1], precision=high
    ) + jnp.einsum("nkg,mkg->nkm", left[:, :, 1], right[:, :, 0], precision=high)
    return jnp.stack([real_part, imag_part], axis=2)


def times_cols(rows, weights):
    first = jnp.einsum(
        "nkh,kgh->nkg", rows[:, :, 0], weights[:, 0], preferred_element_type=jnp.float32
    ) - jnp.einsum("nkh,kgh->nkg", rows[:, :, 1], weights[:, 1], preferred_element_type=jnp.float32)
    second = jnp.einsum(
        "nkh,kgh->nkg", rows[:, :, 0], weights[:, 1], preferred_element_type=jnp.float32
    ) + jnp.einsum("nkh,kgh->nkg", rows[:, :, 1], weights[:, 0], preferred_element_type=jnp.float32)
    return jnp.stack([first, second], axis=2)


def on_any_device(
    val_density, con_density, screened, coulomb, trans_here, trans_there, shift_map, ordering
):
    con_count = con_density.shape[0]
    points = con_density.shape[1]
    slab_cols = con_density.shape[3]
    blocks = slab_cols // GBLK
    within = (shift_map % GBLK).reshape(points, blocks, GBLK)
    onehot = (
        within[:, :, :, None] == jnp.arange(GBLK, dtype=jnp.int32)[None, None, None, :]
    ).astype(jnp.bfloat16)
    con_blocks = con_density.reshape(con_count, points, 2, blocks, GBLK)
    shifted = (
        jnp.einsum("bkpnh,kngh->bkpng", con_blocks, onehot, preferred_element_type=jnp.float32)
        .astype(jnp.bfloat16)
        .reshape(con_density.shape)
    )
    whole_here = lax.all_gather(trans_here, "pair", axis=0, tiled=True).astype(jnp.float32)
    weighted = trans_there.astype(jnp.float32) * coulomb[None, :, None, :]
    high = lax.Precision.HIGHEST
    exch_real = jnp.einsum(
        "tg,skg->tks", whole_here[:, 0], weighted[:, :, 0], precision=high
    ) - jnp.einsum("tg,skg->tks", whole_here[:, 1], weighted[:, :, 1], precision=high)
    exch_imag = jnp.einsum(
        "tg,skg->tks", whole_here[:, 0], weighted[:, :, 1], precision=high
    ) + jnp.einsum("tg,skg->tks", whole_here[:, 1], weighted[:, :, 0], precision=high)
    exch_part = jnp.stack([exch_real, exch_imag], axis=2)
    whole_con = lax.all_gather(shifted, "ga", axis=0, tiled=True)
    screened_rows = lax.psum_scatter(
        times_cols(whole_con, screened), "pair", scatter_dimension=0, tiled=True
    )
    direct_part = contract_float(
        lax.all_gather(val_density, "pair", axis=0, tiled=True).astype(jnp.float32), screened_rows
    )
    direct_sum, exch_sum = lax.psum((direct_part, exch_part), "ga")
    direct_full, exch_full = (
        lax.all_gather(direct_sum, "pair", axis=3, tiled=True),
        lax.all_gather(exch_sum, "pair", axis=3, tiled=True),
    )
    row_count = NT // lax.axis_size("pair")
    col_count = NT // lax.axis_size("ga")
    row_trans = lax.dynamic_slice_in_dim(ordering, lax.axis_index("pair") * row_count, row_count, 0)
    col_trans = lax.dynamic_slice_in_dim(ordering, lax.axis_index("ga") * col_count, col_count, 0)
    row_pairs = (row_trans // NC)[:, None] * NV + (col_trans // NC)[None, :]
    col_pairs = (row_trans % NC)[:, None] * NC + (col_trans % NC)[None, :]
    picked = direct_full[row_pairs.reshape(-1)]
    col_mask = (
        col_pairs.reshape(-1)[:, None] == jnp.arange(direct_full.shape[3], dtype=jnp.int32)[None, :]
    ).astype(jnp.float32)
    direct_flat = jnp.sum(picked * col_mask[:, None, None, :], axis=3)
    direct_sel = jnp.transpose(direct_flat.reshape(row_count, col_count, points, 2), (2, 3, 0, 1))
    exch_picked = exch_full[row_trans]
    col_hot = (jnp.arange(NT, dtype=jnp.int32)[:, None] == col_trans[None, :]).astype(jnp.float32)
    exch_sel = jnp.einsum("rkpt,tc->kprc", exch_picked, col_hot, precision=high)
    return 2.0 * exch_sel - direct_sel


def solution(mesh):
    in_specs = (
        P("pair", None, None, "ga"),
        P("ga", None, None, "pair"),
        P(None, None, "ga", "pair"),
        P(None, "ga"),
        P("pair", None, "ga"),
        P("pair", None, None, "ga"),
        P(None, "pair"),
        P(),
    )
    out_specs = P(None, None, "pair", "ga")

    def run(*args):
        ga, pair = mesh.shape["ga"], mesh.shape["pair"]
        inner = 1 << (int(math.log2(ga)) // 2)
        con_count, h_count = args[1].shape[0], args[1].shape[3]
        suits = (
            ga & (ga - 1) == 0
            and pair & (pair - 1) == 0
            and inner == 2
            and h_count % (ga * pair * GBLK) == 0
            and con_count % (8 * ga) == 0
            and args[0].shape[0] % (16 * pair) == 0
            and NT % (16 * pair) == 0
            and NT // ga <= 64
        )
        body = (lambda *a: on_device(ga // inner, inner, *a)) if suits else on_any_device
        return jax.shard_map(
            body, mesh=mesh, in_specs=in_specs, out_specs=out_specs, check_vma=False
        )(*args)

    return run
```

```python
import jax
import jax.numpy as jnp
from jax import lax
from jax.experimental import pallas as pl
from jax.experimental.pallas import tpu as pltpu
from jax.sharding import PartitionSpec as P

NV = 16
NC = 24
GBLK = 128
NT = 384

GROUP = 64
EXP_ROWS = 16
STEPS = 128.0
TOP = 32700.0
MAGIC = 1.5 * 2.0**23
NT_DIMS = (((1,), (1,)), ((), ()))
VMEM = 56 * 1024 * 1024


def params():
    return pltpu.CompilerParams(vmem_limit_bytes=VMEM)


def cost(flops, moved):
    return pl.CostEstimate(flops=int(flops), bytes_accessed=int(moved), transcendentals=0)


def mm(left, right):
    return jnp.dot(left, right, preferred_element_type=jnp.float32)


def mm_nt(left, right):
    return lax.dot_general(left, right, NT_DIMS, preferred_element_type=jnp.float32)


def halves(value):
    high = value.astype(jnp.bfloat16)
    low = (value - high.astype(jnp.float32)).astype(jnp.bfloat16)
    return high, low


def encode(value, out_ref):
    rows, width = value.shape
    groups = rows // GROUP
    parts = value.reshape(groups, GROUP, width)
    largest = jnp.maximum(jnp.max(jnp.abs(parts), axis=1), 1e-30)
    level = jnp.ceil(jnp.log2(largest) * STEPS) + 1.0
    factor = TOP * jnp.exp2(level * (-1.0 / STEPS))
    coded = ((parts * factor[:, None, :] + MAGIC) - MAGIC).astype(jnp.int32)
    out_ref[0:rows, :] = coded.reshape(rows, width).astype(jnp.int16)
    pad = jnp.zeros((EXP_ROWS - groups, width), jnp.int32)
    out_ref[rows : rows + EXP_ROWS, :] = jnp.concatenate(
        [level.astype(jnp.int32), pad], axis=0
    ).astype(jnp.int16)


def decode(ref):
    rows = ref.shape[0] - EXP_ROWS
    width = ref.shape[1]
    groups = rows // GROUP
    level = ref[rows : rows + EXP_ROWS, :].astype(jnp.int32).astype(jnp.float32)[0:groups]
    factor = jnp.exp2(level * (1.0 / STEPS)) * (1.0 / TOP)
    parts = ref[0:rows, :].astype(jnp.int32).astype(jnp.float32).reshape(groups, GROUP, width)
    return (parts * factor[:, None, :]).reshape(rows, width)


def shift_kernel(dest_ref, con_ref, map_ref, stay_ref, go_ref):
    slots, _, _, rows, width = stay_ref.shape
    for which, out_ref in enumerate((stay_ref, go_ref)):
        for slot in range(slots):
            first = dest_ref[which * slots + slot] * width
            for block in range(width // GBLK):
                cols = pl.ds(pl.multiple_of(first + block * GBLK, GBLK), GBLK)
                within = jnp.bitwise_and(map_ref[0, 0:1, cols], GBLK - 1)
                within = jnp.broadcast_to(within, (rows, GBLK))
                for part in range(2):
                    values = con_ref[0, part, :, cols].astype(jnp.float32)
                    moved = jnp.take_along_axis(values, within, axis=1)
                    out_ref[slot, 0, part, :, block * GBLK : (block + 1) * GBLK] = moved.astype(
                        jnp.bfloat16
                    )


def shift_call(con, shift_map, dests, width):
    points, _, rows, slab = con.shape
    slots = dests.shape[0] // 2
    grid_spec = pltpu.PrefetchScalarGridSpec(
        num_scalar_prefetch=1,
        grid=(points,),
        in_specs=[
            pl.BlockSpec((1, 2, rows, slab), lambda q, dest: (q, 0, 0, 0)),
            pl.BlockSpec((1, 1, slab), lambda q, dest: (q, 0, 0)),
        ],
        out_specs=[pl.BlockSpec((slots, 1, 2, rows, width), lambda q, dest: (0, q, 0, 0, 0))] * 2,
    )
    return pl.pallas_call(
        shift_kernel,
        grid_spec=grid_spec,
        out_shape=[jax.ShapeDtypeStruct((slots, points, 2, rows, width), jnp.bfloat16)] * 2,
        compiler_params=params(),
        cost_estimate=cost(8 * con.size, 4 * con.size),
    )(dests, con, shift_map.reshape(points, 1, slab))


def x_kernel(slots, at_once, table_ref, *refs):
    val_refs, weight_refs = refs[:slots], refs[slots : slots + at_once]
    go_ref, keep_ref, left_ref = refs[slots + at_once :]
    rows, depth = val_refs[0].shape[2], val_refs[0].shape[3]
    half = slots * rows
    step = pl.program_id(0)
    halfway = pl.num_programs(0) // 2

    @pl.when(step == 0)
    def _():
        for slot in range(slots):
            real, imag = val_refs[slot][0, 0], val_refs[slot][0, 1]
            top = slice(slot * rows, (slot + 1) * rows)
            low = slice(half + slot * rows, half + (slot + 1) * rows)
            left_ref[top, 0:depth] = real
            left_ref[top, depth : 2 * depth] = -imag
            left_ref[low, 0:depth] = imag
            left_ref[low, depth : 2 * depth] = real

    width = weight_refs[0].shape[3]
    for place, weight_ref in enumerate(weight_refs):
        product = mm(left_ref[...], weight_ref[0].reshape(2 * depth, width))
        cols = slice(place * width, (place + 1) * width)

        @pl.when(step < halfway)
        def _():
            encode(product, go_ref.at[:, cols])

        @pl.when(step >= halfway)
        def _():
            keep_ref[:, cols] = product


def x_call(vals, screened, point, table, width, at_once):
    slots = len(vals)
    _, _, rows, depth = vals[0].shape
    height = 2 * slots * rows
    steps = table.shape[0] // at_once
    half = steps // 2
    columns = width * at_once * half
    weights = [
        pl.BlockSpec(
            (1, 2, depth, width), lambda j, t, place=place: (point, 0, 0, t[j * at_once + place])
        )
        for place in range(at_once)
    ]
    grid_spec = pltpu.PrefetchScalarGridSpec(
        num_scalar_prefetch=1,
        grid=(steps,),
        in_specs=[
            pl.BlockSpec((1, 2, rows, depth), lambda j, t: (point, 0, 0, 0)) for _ in vals
        ]
        + weights,
        out_specs=[
            pl.BlockSpec(
                (height + EXP_ROWS, width * at_once), lambda j, t: (0, jnp.minimum(j, half - 1))
            ),
            pl.BlockSpec((height, width * at_once), lambda j, t: (0, jnp.maximum(j - half, 0))),
        ],
        scratch_shapes=[pltpu.VMEM((height, 2 * depth), jnp.bfloat16)],
    )
    return pl.pallas_call(
        lambda *refs: x_kernel(slots, at_once, *refs),
        grid_spec=grid_spec,
        out_shape=[
            jax.ShapeDtypeStruct((height + EXP_ROWS, columns), jnp.int16),
            jax.ShapeDtypeStruct((height, columns), jnp.float32),
        ],
        compiler_params=params(),
        cost_estimate=cost(
            2 * height * 2 * depth * 2 * columns, 8 * depth * columns + 6 * height * columns
        ),
    )(table, *vals, *([screened] * at_once))


def hop_kernel(keep_ref, *refs):
    total = keep_ref[...]
    for ref in refs[:-1]:
        total = total + decode(ref)
    encode(total, refs[-1])


def hop_call(keep, others, block, width):
    height, tall = keep.shape[0], others[0].shape[0]
    return pl.pallas_call(
        hop_kernel,
        grid=(1,),
        in_specs=[pl.BlockSpec((height, width), lambda i: (0, block))]
        + [pl.BlockSpec((tall, width), lambda i: (0, block)) for _ in others],
        out_specs=pl.BlockSpec((tall, width), lambda i: (0, 0)),
        out_shape=jax.ShapeDtypeStruct((tall, width), jnp.int16),
        compiler_params=params(),
        cost_estimate=cost(20 * height * width, 8 * height * width),
    )(keep, *others)


def exchange_kernel(slots, *refs):
    here_refs, (there_ref, coulomb_ref, out_ref, left_ref) = refs[:slots], refs[slots:]
    rows, depth = here_refs[0].shape[1], here_refs[0].shape[2]

    @pl.when(pl.program_id(0) == 0)
    def _():
        for slot in range(slots):
            for part in range(2):
                left_ref[
                    slot * rows : (slot + 1) * rows, part * depth : (part + 1) * depth
                ] = here_refs[slot][part]

    factor = coulomb_ref[0]
    real = there_ref[0, 0].astype(jnp.float32) * factor
    imag = there_ref[0, 1].astype(jnp.float32) * factor
    right = jnp.concatenate(
        [jnp.concatenate([real, -imag], axis=1), jnp.concatenate([imag, real], axis=1)], axis=0
    )
    high, low = halves(right)
    left = left_ref[...]
    both = mm_nt(left, high) + mm_nt(left, low)
    cols = both.shape[1] // 2
    for part in range(2):
        out_ref[0, part] = both[:, part * cols : (part + 1) * cols]


def exchange_call(heres, there, coulomb):
    slots = len(heres)
    points, _, cols, depth = there.shape
    rows = heres[0].shape[1]
    height = slots * rows
    return pl.pallas_call(
        lambda *refs: exchange_kernel(slots, *refs),
        grid=(points,),
        in_specs=[pl.BlockSpec(h.shape, lambda q: (0, 0, 0)) for h in heres]
        + [
            pl.BlockSpec((1, 2, cols, depth), lambda q: (q, 0, 0, 0)),
            pl.BlockSpec((1, 1, depth), lambda q: (q, 0, 0)),
        ],
        out_specs=pl.BlockSpec((1, 2, height, cols), lambda q: (q, 0, 0, 0)),
        out_shape=jax.ShapeDtypeStruct((points, 2, height, cols), jnp.float32),
        scratch_shapes=[pltpu.VMEM((height, 2 * depth), jnp.bfloat16)],
        compiler_params=params(),
        cost_estimate=cost(2 * points * height * 2 * cols * 2 * depth * 2, 8 * points * cols * depth),
    )(*heres, there, coulomb.reshape(points, 1, depth))


def tile_kernel(slots, heard, chunks, index_ref, *refs):
    con_refs, keep_ref = refs[:slots], refs[slots]
    heard_refs = refs[slots + 1 : slots + 1 + heard]
    exch_ref, row_ref, col_direct_ref, col_exch_ref = refs[slots + 1 + heard : slots + 5 + heard]
    out_ref, con_all, direct_ref, natural_ref = refs[slots + 5 + heard :]
    total = keep_ref[...]
    for ref in heard_refs:
        total = total + decode(ref)
    pairs, width = total.shape[0] // 2, total.shape[1]
    rows = con_refs[0].shape[3]
    pitch = con_all.shape[0] // slots
    for slot in range(slots):
        for part in range(2):
            con_all[
                slot * pitch : slot * pitch + rows, part * width : (part + 1) * width
            ] = con_refs[slot][0, 0, part]
    real, imag = total[:pairs], total[pairs:]
    right = jnp.concatenate(
        [jnp.concatenate([real, -imag], axis=1), jnp.concatenate([imag, real], axis=1)], axis=0
    )
    high, low = halves(right)
    left = con_all[...]
    direct = mm_nt(left, high) + mm_nt(left, low)
    lanes = direct_ref.shape[0]
    for slot in range(slots):
        start = pl.multiple_of(index_ref[slot] * rows, 8)
        for lane in range(lanes):
            direct_ref[lane, pl.ds(start, rows), :] = direct[
                slot * pitch : slot * pitch + rows, lane * 128 : (lane + 1) * 128
            ]
    group = 128 // NV
    place = lax.broadcasted_iota(jnp.int32, (NC, 128), 1) // NV
    per_part = lanes // 2
    for part in range(2):
        for chunk in range(NC // group):
            for band in range(NV):
                block = jnp.zeros((NC, 128), jnp.float32)
                for step in range(group):
                    e = chunk * group + step
                    piece = direct_ref[part * per_part + band // group, pl.ds(e, NC, stride=NC), :]
                    turn = (NV * (step - band)) % 128
                    if turn:
                        piece = pltpu.roll(piece, turn, 1)
                    block = jnp.where(place == step, piece, block)
                natural_ref[
                    part, band * NC : (band + 1) * NC, chunk * 128 : (chunk + 1) * 128
                ] = block
    pick_rows = row_ref[...]
    count = NT // chunks
    for part in range(2):
        result = None
        for source, pick_cols in (
            (natural_ref[part], col_direct_ref),
            (exch_ref[0, part], col_exch_ref),
        ):
            for piece in halves(source):
                moved = mm(pick_rows, piece).astype(jnp.bfloat16)
                term = mm(moved, pick_cols[...])
                result = term if result is None else result + term
        for chunk in range(chunks):
            at = (2 * chunk + part) * count
            out_ref[at : at + count, :] = result[chunk * count : (chunk + 1) * count]


def tile_call(cons, point, keep, heard, exch, index, pick_rows, col_direct, col_exch, chunks):
    slots = len(cons)
    _, _, _, rows, width = cons[0][0].shape
    height, tall = keep.shape[0], heard[0].shape[0]
    pitch = -(-rows // 16) * 16
    out_cols = col_direct.shape[1]
    whole = lambda a: pl.BlockSpec(a.shape, lambda i, at: (0,) * a.ndim)
    grid_spec = pltpu.PrefetchScalarGridSpec(
        num_scalar_prefetch=1,
        grid=(1,),
        in_specs=[
            pl.BlockSpec((1, 1, 2, rows, width), lambda i, at, place=place: (place, point, 0, 0, 0))
            for _, place in cons
        ]
        + [pl.BlockSpec((height, width), lambda i, at: (0, 0))]
        + [pl.BlockSpec((tall, width), lambda i, at: (0, 0)) for _ in heard]
        + [
            pl.BlockSpec((1,) + exch.shape[1:], lambda i, at: (point, 0, 0, 0)),
            whole(pick_rows),
            whole(col_direct),
            whole(col_exch),
        ],
        out_specs=pl.BlockSpec((2 * NT, out_cols), lambda i, at: (0, 0)),
        scratch_shapes=[
            pltpu.VMEM((slots * pitch, 2 * width), jnp.bfloat16),
            pltpu.VMEM((height // 128, NC * NC, 128), jnp.float32),
            pltpu.VMEM((2, NT, NT), jnp.float32),
        ],
    )
    return pl.pallas_call(
        lambda *refs: tile_kernel(slots, len(heard), chunks, *refs),
        grid_spec=grid_spec,
        out_shape=jax.ShapeDtypeStruct((2 * NT, out_cols), jnp.float32),
        compiler_params=params(),
        cost_estimate=cost(2.8e9, 8e6),
    )(index, *[c for c, _ in cons], keep, *heard, exch, pick_rows, col_direct, col_exch)


def swap(value, axis, size, bit):
    return lax.ppermute(value, axis, [(i, i ^ bit) for i in range(size)])


def gather_slots(value, axis, size):
    found = {0: value}
    bit = size // 2
    while bit:
        for known in sorted(found):
            found[known ^ bit] = swap(found[known], axis, size, bit)
        bit //= 2
    return [found[r] for r in range(size)]


def halving_order(bits):
    order = [0]
    for bit in reversed(bits):
        order = order + [o ^ bit for o in order]
    return order


def on_device(*args):
    (val_density, con_density, screened, coulomb, trans_here, trans_there, shift_map, ordering) = args
    ga, pair = lax.axis_size("ga"), lax.axis_size("pair")
    points = con_density.shape[1]
    slab = con_density.shape[3]
    width = slab // ga
    me_ga, me_pair = lax.axis_index("ga"), lax.axis_index("pair")
    ga_bits = [1 << b for b in range(ga.bit_length() - 1)]
    pair_bits = [1 << b for b in range(pair.bit_length() - 1)]
    ga_order = halving_order(ga_bits)
    half = ga // 2
    dests = me_ga ^ jnp.asarray(ga_order, jnp.int32)

    vals = gather_slots(jnp.transpose(val_density, (1, 2, 0, 3)), "pair", pair)

    con = jnp.transpose(con_density, (1, 2, 0, 3))
    stay, go = shift_call(con, shift_map, dests, width)
    cons = {}
    for p, slot in enumerate(ga_order):
        cons[slot] = (stay, p) if p < half else (go, p - half)
    for bit in ga_bits:
        moving = [slot for slot in ga_order if slot & bit]
        if bit == ga_bits[0]:
            sent = go
        else:
            sent = jnp.stack([cons[slot][0][cons[slot][1]] for slot in moving])
        got = swap(sent, "ga", ga, bit)
        for place, slot in enumerate(moving):
            cons[slot] = (got, place)
    cons = [cons[slot] for slot in ga_order]

    table = jnp.concatenate([dests[half:], dests[:half]])
    gone, keep = [], []
    for q in range(points):
        coded, own = x_call(vals, screened, q, table, width, 2)
        gone.append(coded)
        keep.append(own)

    heres = gather_slots(jnp.transpose(trans_here, (1, 0, 2)), "pair", pair)
    exch = exchange_call(heres, jnp.transpose(trans_there, (1, 2, 0, 3)), coulomb)

    row_count, col_count = NT // pair, NT // ga
    row_slots = jnp.asarray(halving_order(pair_bits), jnp.int32)
    row_trans = ordering.reshape(pair, row_count)[me_pair ^ row_slots].reshape(-1)
    at_row = ((row_trans // row_count) ^ me_pair) * row_count + row_trans % row_count
    pick_rows = (at_row[:, None] == jnp.arange(NT, dtype=jnp.int32)[None, :]).astype(jnp.bfloat16)
    col_trans = ordering.reshape(ga, col_count)[dests]
    col_trans = jnp.pad(col_trans, ((0, 0), (0, 64 - col_count)), constant_values=-1).reshape(1, -1)
    real_col = col_trans >= 0
    at_direct = jnp.where(real_col, (col_trans % NC) * NV + col_trans // NC, -1)
    own_col = real_col & (col_trans // row_count == me_pair)
    at_exch = jnp.where(own_col, col_trans % row_count, -1)

    def pick_cols(at, size, scale):
        hot = at == jnp.arange(size, dtype=jnp.int32)[:, None]
        return jnp.where(hot, scale, 0.0).astype(jnp.bfloat16)

    col_direct, col_exch = pick_cols(at_direct, NT, -1.0), pick_cols(at_exch, row_count, 2.0)

    heard = [[swap(gone[q], "ga", ga, ga_bits[0])] for q in range(points)]
    part = half
    for bit in ga_bits[1:]:
        part //= 2
        for q in range(points):
            heard[q].append(swap(hop_call(keep[q], heard[q], 1, part * width), "ga", ga, bit))
    outs = []
    for q in range(points):
        tile = tile_call(
            cons, q, keep[q], heard[q], exch, dests, pick_rows, col_direct, col_exch, pair
        )
        for bit in pair_bits:
            rows = tile.shape[0] // 2
            tile = tile[:rows] + swap(tile[rows:], "pair", pair, bit)
        for bit in ga_bits:
            cols = tile.shape[1] // 2
            tile = tile[:, :cols] + swap(tile[:, cols:], "ga", ga, bit)
        outs.append(tile[:, :col_count].reshape(2, row_count, col_count))
    return jnp.stack(outs)


def contract_float(left, right):
    high = lax.Precision.HIGHEST
    real_part = jnp.einsum(
        "nkg,mkg->nkm", left[:, :, 0], right[:, :, 0], precision=high
    ) - jnp.einsum("nkg,mkg->nkm", left[:, :, 1], right[:, :, 1], precision=high)
    imag_part = jnp.einsum(
        "nkg,mkg->nkm", left[:, :, 0], right[:, :, 1], precision=high
    ) + jnp.einsum("nkg,mkg->nkm", left[:, :, 1], right[:, :, 0], precision=high)
    return jnp.stack([real_part, imag_part], axis=2)


def times_cols(rows, weights):
    first = jnp.einsum(
        "nkh,kgh->nkg", rows[:, :, 0], weights[:, 0], preferred_element_type=jnp.float32
    ) - jnp.einsum("nkh,kgh->nkg", rows[:, :, 1], weights[:, 1], preferred_element_type=jnp.float32)
    second = jnp.einsum(
        "nkh,kgh->nkg", rows[:, :, 0], weights[:, 1], preferred_element_type=jnp.float32
    ) + jnp.einsum("nkh,kgh->nkg", rows[:, :, 1], weights[:, 0], preferred_element_type=jnp.float32)
    return jnp.stack([first, second], axis=2)


def on_any_device(
    val_density, con_density, screened, coulomb, trans_here, trans_there, shift_map, ordering
):
    con_count = con_density.shape[0]
    points = con_density.shape[1]
    slab_cols = con_density.shape[3]
    blocks = slab_cols // GBLK
    within = (shift_map % GBLK).reshape(points, blocks, GBLK)
    onehot = (
        within[:, :, :, None] == jnp.arange(GBLK, dtype=jnp.int32)[None, None, None, :]
    ).astype(jnp.bfloat16)
    con_blocks = con_density.reshape(con_count, points, 2, blocks, GBLK)
    shifted = (
        jnp.einsum("bkpnh,kngh->bkpng", con_blocks, onehot, preferred_element_type=jnp.float32)
        .astype(jnp.bfloat16)
        .reshape(con_density.shape)
    )
    whole_here = lax.all_gather(trans_here, "pair", axis=0, tiled=True).astype(jnp.float32)
    weighted = trans_there.astype(jnp.float32) * coulomb[None, :, None, :]
    high = lax.Precision.HIGHEST
    exch_real = jnp.einsum(
        "tg,skg->tks", whole_here[:, 0], weighted[:, :, 0], precision=high
    ) - jnp.einsum("tg,skg->tks", whole_here[:, 1], weighted[:, :, 1], precision=high)
    exch_imag = jnp.einsum(
        "tg,skg->tks", whole_here[:, 0], weighted[:, :, 1], precision=high
    ) + jnp.einsum("tg,skg->tks", whole_here[:, 1], weighted[:, :, 0], precision=high)
    exch_part = jnp.stack([exch_real, exch_imag], axis=2)
    whole_con = lax.all_gather(shifted, "ga", axis=0, tiled=True)
    screened_rows = lax.psum_scatter(
        times_cols(whole_con, screened), "pair", scatter_dimension=0, tiled=True
    )
    direct_part = contract_float(
        lax.all_gather(val_density, "pair", axis=0, tiled=True).astype(jnp.float32), screened_rows
    )
    direct_sum, exch_sum = lax.psum((direct_part, exch_part), "ga")
    direct_full, exch_full = (
        lax.all_gather(direct_sum, "pair", axis=3, tiled=True),
        lax.all_gather(exch_sum, "pair", axis=3, tiled=True),
    )
    row_count = NT // lax.axis_size("pair")
    col_count = NT // lax.axis_size("ga")
    row_trans = lax.dynamic_slice_in_dim(ordering, lax.axis_index("pair") * row_count, row_count, 0)
    col_trans = lax.dynamic_slice_in_dim(ordering, lax.axis_index("ga") * col_count, col_count, 0)
    row_pairs = (row_trans // NC)[:, None] * NV + (col_trans // NC)[None, :]
    col_pairs = (row_trans % NC)[:, None] * NC + (col_trans % NC)[None, :]
    picked = direct_full[row_pairs.reshape(-1)]
    col_mask = (
        col_pairs.reshape(-1)[:, None] == jnp.arange(direct_full.shape[3], dtype=jnp.int32)[None, :]
    ).astype(jnp.float32)
    direct_flat = jnp.sum(picked * col_mask[:, None, None, :], axis=3)
    direct_sel = jnp.transpose(direct_flat.reshape(row_count, col_count, points, 2), (2, 3, 0, 1))
    exch_picked = exch_full[row_trans]
    col_hot = (jnp.arange(NT, dtype=jnp.int32)[:, None] == col_trans[None, :]).astype(jnp.float32)
    exch_sel = jnp.einsum("rkpt,tc->kprc", exch_picked, col_hot, precision=high)
    return 2.0 * exch_sel - direct_sel


def solution(mesh):
    in_specs = (
        P("pair", None, None, "ga"),
        P("ga", None, None, "pair"),
        P(None, None, "ga", "pair"),
        P(None, "ga"),
        P("pair", None, "ga"),
        P("pair", None, None, "ga"),
        P(None, "pair"),
        P(),
    )
    out_specs = P(None, None, "pair", "ga")

    def run(*args):
        ga, pair = mesh.shape["ga"], mesh.shape["pair"]
        con_count, h_count = args[1].shape[0], args[1].shape[3]
        suits = (
            ga & (ga - 1) == 0
            and pair & (pair - 1) == 0
            and ga >= 4
            and pair >= 2
            and h_count % (ga * pair * GBLK) == 0
            and con_count % (8 * ga) == 0
            and args[0].shape[0] % (16 * pair) == 0
            and NT % (16 * pair) == 0
            and NT // ga <= 64
        )
        body = on_device if suits else on_any_device
        return jax.shard_map(
            body, mesh=mesh, in_specs=in_specs, out_specs=out_specs, check_vma=False
        )(*args)

    return run
```

```python
import jax
import jax.numpy as jnp
from jax import lax
from jax.experimental import pallas as pl
from jax.experimental.pallas import tpu as pltpu
from jax.sharding import PartitionSpec as P

NV = 16
NC = 24
GBLK = 128
NT = 384

GROUP = 64
EXP_ROWS = 16
STEPS = 128.0
TOP = 32700.0
MAGIC = 1.5 * 2.0**23
NT_DIMS = (((1,), (1,)), ((), ()))
VMEM = 56 * 1024 * 1024


def params():
    return pltpu.CompilerParams(vmem_limit_bytes=VMEM)


def cost(flops, moved):
    return pl.CostEstimate(flops=int(flops), bytes_accessed=int(moved), transcendentals=0)


def mm(left, right):
    return jnp.dot(left, right, preferred_element_type=jnp.float32)


def mm_nt(left, right):
    return lax.dot_general(left, right, NT_DIMS, preferred_element_type=jnp.float32)


def halves(value):
    high = value.astype(jnp.bfloat16)
    low = (value - high.astype(jnp.float32)).astype(jnp.bfloat16)
    return high, low


def encode(value, out_ref):
    rows, width = value.shape
    groups = rows // GROUP
    parts = value.reshape(groups, GROUP, width)
    largest = jnp.maximum(jnp.max(jnp.abs(parts), axis=1), 1e-30)
    level = jnp.ceil(jnp.log2(largest) * STEPS) + 1.0
    factor = TOP * jnp.exp2(level * (-1.0 / STEPS))
    coded = ((parts * factor[:, None, :] + MAGIC) - MAGIC).astype(jnp.int32)
    out_ref[0:rows, :] = coded.reshape(rows, width).astype(jnp.int16)
    pad = jnp.zeros((EXP_ROWS - groups, width), jnp.int32)
    out_ref[rows : rows + EXP_ROWS, :] = jnp.concatenate(
        [level.astype(jnp.int32), pad], axis=0
    ).astype(jnp.int16)


def decode(ref):
    rows = ref.shape[0] - EXP_ROWS
    width = ref.shape[1]
    groups = rows // GROUP
    level = ref[rows : rows + EXP_ROWS, :].astype(jnp.int32).astype(jnp.float32)[0:groups]
    factor = jnp.exp2(level * (1.0 / STEPS)) * (1.0 / TOP)
    parts = ref[0:rows, :].astype(jnp.int32).astype(jnp.float32).reshape(groups, GROUP, width)
    return (parts * factor[:, None, :]).reshape(rows, width)


def shift_kernel(dest_ref, con_ref, map_ref, stay_ref, go_ref):
    slots, _, _, rows, width = stay_ref.shape
    for which, out_ref in enumerate((stay_ref, go_ref)):
        for slot in range(slots):
            first = dest_ref[which * slots + slot] * width
            for block in range(width // GBLK):
                cols = pl.ds(pl.multiple_of(first + block * GBLK, GBLK), GBLK)
                within = jnp.bitwise_and(map_ref[0, 0:1, cols], GBLK - 1)
                within = jnp.broadcast_to(within, (rows, GBLK))
                for part in range(2):
                    values = con_ref[0, part, :, cols].astype(jnp.float32)
                    moved = jnp.take_along_axis(values, within, axis=1)
                    out_ref[slot, 0, part, :, block * GBLK : (block + 1) * GBLK] = moved.astype(
                        jnp.bfloat16
                    )


def shift_call(con, shift_map, dests, width):
    points, _, rows, slab = con.shape
    slots = dests.shape[0] // 2
    grid_spec = pltpu.PrefetchScalarGridSpec(
        num_scalar_prefetch=1,
        grid=(points,),
        in_specs=[
            pl.BlockSpec((1, 2, rows, slab), lambda q, dest: (q, 0, 0, 0)),
            pl.BlockSpec((1, 1, slab), lambda q, dest: (q, 0, 0)),
        ],
        out_specs=[pl.BlockSpec((slots, 1, 2, rows, width), lambda q, dest: (0, q, 0, 0, 0))] * 2,
    )
    return pl.pallas_call(
        shift_kernel,
        grid_spec=grid_spec,
        out_shape=[jax.ShapeDtypeStruct((slots, points, 2, rows, width), jnp.bfloat16)] * 2,
        compiler_params=params(),
        cost_estimate=cost(8 * con.size, 4 * con.size),
    )(dests, con, shift_map.reshape(points, 1, slab))


def x_kernel(slots, base_ref, *refs):
    val_refs, (weight_ref, go_ref, keep_ref, left_ref) = refs[:slots], refs[slots:]
    rows, depth = val_refs[0].shape[2], val_refs[0].shape[3]
    half = slots * rows
    step = pl.program_id(0)
    halfway = pl.num_programs(0) // 2

    @pl.when(step == 0)
    def _():
        for slot in range(slots):
            real, imag = val_refs[slot][0, 0], val_refs[slot][0, 1]
            top = slice(slot * rows, (slot + 1) * rows)
            low = slice(half + slot * rows, half + (slot + 1) * rows)
            left_ref[top, 0:depth] = real
            left_ref[top, depth : 2 * depth] = -imag
            left_ref[low, 0:depth] = imag
            left_ref[low, depth : 2 * depth] = real

    weight = weight_ref[0].reshape(2 * depth, weight_ref.shape[3])

    @pl.when(step < halfway)
    def _():
        encode(mm(left_ref[...], weight), go_ref)

    @pl.when(step >= halfway)
    def _():
        keep_ref[...] = mm(left_ref[...], weight)


def x_call(vals, screened, place, point, side, steps):
    slots = len(vals)
    _, _, rows, depth = vals[0].shape
    height = 2 * slots * rows
    columns = screened.shape[3] // 2
    half = steps // 2
    width = columns // half
    grid_spec = pltpu.PrefetchScalarGridSpec(
        num_scalar_prefetch=1,
        grid=(steps,),
        in_specs=[
            pl.BlockSpec((1, 2, rows, depth), lambda j, t: (place, 0, 0, 0)) for _ in vals
        ]
        + [
            pl.BlockSpec(
                (1, 2, depth, width), lambda j, t: (point, 0, 0, t[j // half] * half + j % half)
            )
        ],
        out_specs=[
            pl.BlockSpec((height + EXP_ROWS, width), lambda j, t: (0, jnp.minimum(j, half - 1))),
            pl.BlockSpec((height, width), lambda j, t: (0, jnp.maximum(j - half, 0))),
        ],
        scratch_shapes=[pltpu.VMEM((height, 2 * depth), jnp.bfloat16)],
    )
    return pl.pallas_call(
        lambda *refs: x_kernel(slots, *refs),
        grid_spec=grid_spec,
        out_shape=[
            jax.ShapeDtypeStruct((height + EXP_ROWS, columns), jnp.int16),
            jax.ShapeDtypeStruct((height, columns), jnp.float32),
        ],
        compiler_params=params(),
        cost_estimate=cost(
            2 * height * 2 * depth * 2 * columns, 8 * depth * columns + 6 * height * columns
        ),
    )(side, *vals, screened)


def hop_kernel(heard, at_ref, keep_ref, *refs):
    total = keep_ref[...]
    for ref in refs[:heard]:
        total = total + decode(ref)
    encode(total, refs[-1])


def hop_call(keep, others, at, width, after):
    height, tall = keep.shape[0], others[0].shape[0]
    grid_spec = pltpu.PrefetchScalarGridSpec(
        num_scalar_prefetch=1,
        grid=(1,),
        in_specs=[pl.BlockSpec((height, width), lambda i, at: (0, at[0]))]
        + [
            pl.BlockSpec((tall, width), lambda i, at, n=n: (0, at[n + 1]))
            for n in range(len(others))
        ]
        + [pl.BlockSpec(memory_space=pl.ANY) for _ in after],
        out_specs=pl.BlockSpec((tall, width), lambda i, at: (0, 0)),
    )
    return pl.pallas_call(
        lambda *refs: hop_kernel(len(others), *refs),
        grid_spec=grid_spec,
        out_shape=jax.ShapeDtypeStruct((tall, width), jnp.int16),
        compiler_params=params(),
        cost_estimate=cost(20 * height * width, 8 * height * width),
    )(at, keep, *others, *after)


def exchange_kernel(slots, *refs):
    here_refs, (there_ref, coulomb_ref, out_ref, left_ref) = refs[:slots], refs[slots:]
    rows, depth = here_refs[0].shape[1], here_refs[0].shape[2]

    @pl.when(pl.program_id(0) == 0)
    def _():
        for slot in range(slots):
            for part in range(2):
                left_ref[
                    slot * rows : (slot + 1) * rows, part * depth : (part + 1) * depth
                ] = here_refs[slot][part]

    factor = coulomb_ref[0]
    real = there_ref[0, 0].astype(jnp.float32) * factor
    imag = there_ref[0, 1].astype(jnp.float32) * factor
    right = jnp.concatenate(
        [jnp.concatenate([real, -imag], axis=1), jnp.concatenate([imag, real], axis=1)], axis=0
    )
    high, low = halves(right)
    left = left_ref[...]
    both = mm_nt(left, high) + mm_nt(left, low)
    cols = both.shape[1] // 2
    for part in range(2):
        out_ref[0, part] = both[:, part * cols : (part + 1) * cols]


def exchange_call(heres, there, coulomb):
    slots = len(heres)
    points, _, cols, depth = there.shape
    rows = heres[0].shape[1]
    height = slots * rows
    return pl.pallas_call(
        lambda *refs: exchange_kernel(slots, *refs),
        grid=(points,),
        in_specs=[pl.BlockSpec(h.shape, lambda q: (0, 0, 0)) for h in heres]
        + [
            pl.BlockSpec((1, 2, cols, depth), lambda q: (q, 0, 0, 0)),
            pl.BlockSpec((1, 1, depth), lambda q: (q, 0, 0)),
        ],
        out_specs=pl.BlockSpec((1, 2, height, cols), lambda q: (q, 0, 0, 0)),
        out_shape=jax.ShapeDtypeStruct((points, 2, height, cols), jnp.float32),
        scratch_shapes=[pltpu.VMEM((height, 2 * depth), jnp.bfloat16)],
        compiler_params=params(),
        cost_estimate=cost(2 * points * height * 2 * cols * 2 * depth * 2, 8 * points * cols * depth),
    )(*heres, there, coulomb.reshape(points, 1, depth))


def tile_kernel(slots, heard, chunks, waits, index_ref, at_ref, *refs):
    con_refs, keep_ref = refs[:slots], refs[slots]
    heard_refs = refs[slots + 1 : slots + 1 + heard]
    exch_ref, row_ref, col_direct_ref, col_exch_ref = refs[slots + 1 + heard : slots + 5 + heard]
    keep_out, go_out, con_all, direct_ref, natural_ref = refs[slots + 5 + heard + waits :]
    total = keep_ref[...]
    for ref in heard_refs:
        total = total + decode(ref)
    pairs, width = total.shape[0] // 2, total.shape[1]
    rows = con_refs[0].shape[3]
    pitch = con_all.shape[0] // slots
    for slot in range(slots):
        for part in range(2):
            con_all[
                slot * pitch : slot * pitch + rows, part * width : (part + 1) * width
            ] = con_refs[slot][0, 0, part]
    real, imag = total[:pairs], total[pairs:]
    right = jnp.concatenate(
        [jnp.concatenate([real, -imag], axis=1), jnp.concatenate([imag, real], axis=1)], axis=0
    )
    high, low = halves(right)
    left = con_all[...]
    direct = mm_nt(left, high) + mm_nt(left, low)
    lanes = direct_ref.shape[0]
    for slot in range(slots):
        start = pl.multiple_of(index_ref[slot] * rows, 8)
        for lane in range(lanes):
            direct_ref[lane, pl.ds(start, rows), :] = direct[
                slot * pitch : slot * pitch + rows, lane * 128 : (lane + 1) * 128
            ]
    group = 128 // NV
    place = lax.broadcasted_iota(jnp.int32, (NC, 128), 1) // NV
    per_part = lanes // 2
    for part in range(2):
        for chunk in range(NC // group):
            for band in range(NV):
                block = jnp.zeros((NC, 128), jnp.float32)
                for step in range(group):
                    e = chunk * group + step
                    piece = direct_ref[part * per_part + band // group, pl.ds(e, NC, stride=NC), :]
                    turn = (NV * (step - band)) % 128
                    if turn:
                        piece = pltpu.roll(piece, turn, 1)
                    block = jnp.where(place == step, piece, block)
                natural_ref[
                    part, band * NC : (band + 1) * NC, chunk * 128 : (chunk + 1) * 128
                ] = block
    pick_rows = row_ref[...]
    count = NT // chunks
    for part in range(2):
        result = None
        for source, pick_cols in (
            (natural_ref[part], col_direct_ref),
            (exch_ref[0, part], col_exch_ref),
        ):
            for piece in halves(source):
                moved = mm(pick_rows, piece).astype(jnp.bfloat16)
                term = mm(moved, pick_cols[...])
                result = term if result is None else result + term
        for chunk in range(chunks):
            out_ref = keep_out if chunk < chunks // 2 else go_out
            at = (2 * (chunk % (chunks // 2)) + part) * count
            out_ref[at : at + count, :] = result[chunk * count : (chunk + 1) * count]


def tile_call(
    cons, point, keep, heard, exch, index, at, pick_rows, col_direct, col_exch, chunks, after
):
    slots = len(cons)
    _, _, _, rows, width = cons[0][0].shape
    height, tall = keep.shape[0], heard[0].shape[0]
    pitch = -(-rows // 16) * 16
    out_cols = col_direct.shape[1]
    whole = lambda a: pl.BlockSpec(a.shape, lambda i, index, at: (0,) * a.ndim)
    grid_spec = pltpu.PrefetchScalarGridSpec(
        num_scalar_prefetch=2,
        grid=(1,),
        in_specs=[
            pl.BlockSpec(
                (1, 1, 2, rows, width), lambda i, index, at, place=place: (place, point, 0, 0, 0)
            )
            for _, place in cons
        ]
        + [pl.BlockSpec((height, width), lambda i, index, at: (0, at[0]))]
        + [
            pl.BlockSpec((tall, width), lambda i, index, at, n=n: (0, at[n + 1]))
            for n in range(len(heard))
        ]
        + [
            pl.BlockSpec((1,) + exch.shape[1:], lambda i, index, at: (point, 0, 0, 0)),
            whole(pick_rows),
            whole(col_direct),
            whole(col_exch),
        ]
        + [pl.BlockSpec(memory_space=pl.ANY) for _ in after],
        out_specs=[pl.BlockSpec((NT, out_cols), lambda i, index, at: (0, 0))] * 2,
        scratch_shapes=[
            pltpu.VMEM((slots * pitch, 2 * width), jnp.bfloat16),
            pltpu.VMEM((height // 128, NC * NC, 128), jnp.float32),
            pltpu.VMEM((2, NT, NT), jnp.float32),
        ],
    )
    return pl.pallas_call(
        lambda *refs: tile_kernel(slots, len(heard), chunks, len(after), *refs),
        grid_spec=grid_spec,
        out_shape=[jax.ShapeDtypeStruct((NT, out_cols), jnp.float32)] * 2,
        compiler_params=params(),
        cost_estimate=cost(2.8e9, 8e6),
    )(
        index, at, *[c for c, _ in cons], keep, *heard, exch, pick_rows, col_direct, col_exch, *after
    )


def swap(value, axis, size, bit):
    return lax.ppermute(value, axis, [(i, i ^ bit) for i in range(size)])


def gather_slots(value, axis, size):
    found = {0: value}
    bit = size // 2
    while bit:
        for known in sorted(found):
            found[known ^ bit] = swap(found[known], axis, size, bit)
        bit //= 2
    return [found[r] for r in range(size)]


def halving_order(bits):
    order = [0]
    for bit in reversed(bits):
        order = order + [o ^ bit for o in order]
    return order


def on_device(*args):
    (val_density, con_density, screened, coulomb, trans_here, trans_there, shift_map, ordering) = args
    ga, pair = lax.axis_size("ga"), lax.axis_size("pair")
    points = con_density.shape[1]
    slab = con_density.shape[3]
    width = slab // ga
    me_ga, me_pair = lax.axis_index("ga"), lax.axis_index("pair")
    ga_bits = [1 << b for b in range(ga.bit_length() - 1)]
    pair_bits = [1 << b for b in range(pair.bit_length() - 1)]
    ga_order = halving_order(ga_bits)
    half = ga // 2
    dests = me_ga ^ jnp.asarray(ga_order, jnp.int32)
    flags = [(me_ga // bit) % 2 for bit in ga_bits]
    blocks = sum(((dests // bit) % 2) * (half // bit) for bit in ga_bits)
    as_index = lambda items: jnp.stack([jnp.asarray(i, jnp.int32) for i in items])

    def block_at(known, chosen):
        number = jnp.int32(0)
        for flag in flags[known : len(flags) if chosen is None else chosen]:
            number = 2 * number + flag
        return number if chosen is None else 2 * number + 1 - flags[chosen]

    val = jnp.transpose(val_density, (1, 2, 0, 3))
    first, others = gather_slots(val[:1], "pair", pair), gather_slots(val[1:], "pair", pair)

    con = jnp.transpose(con_density, (1, 2, 0, 3))
    stay, go = shift_call(con, shift_map, blocks, width)
    cons = {}
    for p, slot in enumerate(ga_order):
        cons[slot] = (stay, p) if p < half else (go, p - half)
    for bit in ga_bits:
        moving = [slot for slot in ga_order if slot & bit]
        if bit == ga_bits[0]:
            sent = go
        else:
            sent = jnp.stack([cons[slot][0][cons[slot][1]] for slot in moving])
        got = swap(sent, "ga", ga, bit)
        for place, slot in enumerate(moving):
            cons[slot] = (got, place)
    cons = [cons[slot] for slot in ga_order]

    side = as_index([1 - flags[0], flags[0]])
    gone, keep = [], []
    for q in range(points):
        vals, place = (first, 0) if q == 0 else (others, q - 1)
        coded, own = x_call(vals, screened, place, q, side, 4)
        gone.append(coded)
        keep.append(own)

    heres = gather_slots(jnp.transpose(trans_here, (1, 0, 2)), "pair", pair)
    exch = exchange_call(heres, jnp.transpose(trans_there, (1, 2, 0, 3)), coulomb)

    row_count, col_count = NT // pair, NT // ga
    row_slots = jnp.asarray(halving_order(pair_bits), jnp.int32)
    row_trans = ordering.reshape(pair, row_count)[me_pair ^ row_slots].reshape(-1)
    at_row = ((row_trans // row_count) ^ me_pair) * row_count + row_trans % row_count
    pick_rows = (at_row[:, None] == jnp.arange(NT, dtype=jnp.int32)[None, :]).astype(jnp.bfloat16)
    col_trans = ordering.reshape(ga, col_count)[dests]
    col_trans = jnp.pad(col_trans, ((0, 0), (0, 64 - col_count)), constant_values=-1).reshape(1, -1)
    real_col = col_trans >= 0
    at_direct = jnp.where(real_col, (col_trans % NC) * NV + col_trans // NC, -1)
    own_col = real_col & (col_trans // row_count == me_pair)
    at_exch = jnp.where(own_col, col_trans % row_count, -1)

    def pick_cols(at, size, scale):
        hot = at == jnp.arange(size, dtype=jnp.int32)[:, None]
        return jnp.where(hot, scale, 0.0).astype(jnp.bfloat16)

    col_direct, col_exch = pick_cols(at_direct, NT, -1.0), pick_cols(at_exch, row_count, 2.0)

    heard = [[swap(gone[q], "ga", ga, ga_bits[0])] for q in range(points)]
    outs = [None] * points
    stages = len(ga_bits)
    after = []
    for wave in range(2 * points + stages):
        for q in reversed(range(points)):
            stage = wave - 2 * q
            if 1 <= stage < stages:
                columns = ga >> (stage + 1)
                at = as_index([block_at(k, stage) for k in [1] + list(range(1, stage + 1))])
                coded = hop_call(keep[q], heard[q], at, columns * width, after)
                after = [coded]
                heard[q].append(swap(coded, "ga", ga, ga_bits[stage]))
            elif stage == stages:
                at = as_index([block_at(k, None) for k in [1] + list(range(1, stages + 1))])
                tile, sent = tile_call(
                    cons, q, keep[q], heard[q], exch, dests, at, pick_rows, col_direct, col_exch,
                    pair, after,
                )
                after = [sent]
                tile = tile + swap(sent, "pair", pair, pair_bits[0])
                for bit in pair_bits[1:]:
                    rows = tile.shape[0] // 2
                    tile = tile[:rows] + swap(tile[rows:], "pair", pair, bit)
                for bit in ga_bits:
                    cols = tile.shape[1] // 2
                    tile = tile[:, :cols] + swap(tile[:, cols:], "ga", ga, bit)
                outs[q] = tile[:, :col_count].reshape(2, row_count, col_count)
    return jnp.stack(outs)


def contract_float(left, right):
    high = lax.Precision.HIGHEST
    real_part = jnp.einsum(
        "nkg,mkg->nkm", left[:, :, 0], right[:, :, 0], precision=high
    ) - jnp.einsum("nkg,mkg->nkm", left[:, :, 1], right[:, :, 1], precision=high)
    imag_part = jnp.einsum(
        "nkg,mkg->nkm", left[:, :, 0], right[:, :, 1], precision=high
    ) + jnp.einsum("nkg,mkg->nkm", left[:, :, 1], right[:, :, 0], precision=high)
    return jnp.stack([real_part, imag_part], axis=2)


def times_cols(rows, weights):
    first = jnp.einsum(
        "nkh,kgh->nkg", rows[:, :, 0], weights[:, 0], preferred_element_type=jnp.float32
    ) - jnp.einsum("nkh,kgh->nkg", rows[:, :, 1], weights[:, 1], preferred_element_type=jnp.float32)
    second = jnp.einsum(
        "nkh,kgh->nkg", rows[:, :, 0], weights[:, 1], preferred_element_type=jnp.float32
    ) + jnp.einsum("nkh,kgh->nkg", rows[:, :, 1], weights[:, 0], preferred_element_type=jnp.float32)
    return jnp.stack([first, second], axis=2)


def on_any_device(
    val_density, con_density, screened, coulomb, trans_here, trans_there, shift_map, ordering
):
    con_count = con_density.shape[0]
    points = con_density.shape[1]
    slab_cols = con_density.shape[3]
    blocks = slab_cols // GBLK
    within = (shift_map % GBLK).reshape(points, blocks, GBLK)
    onehot = (
        within[:, :, :, None] == jnp.arange(GBLK, dtype=jnp.int32)[None, None, None, :]
    ).astype(jnp.bfloat16)
    con_blocks = con_density.reshape(con_count, points, 2, blocks, GBLK)
    shifted = (
        jnp.einsum("bkpnh,kngh->bkpng", con_blocks, onehot, preferred_element_type=jnp.float32)
        .astype(jnp.bfloat16)
        .reshape(con_density.shape)
    )
    whole_here = lax.all_gather(trans_here, "pair", axis=0, tiled=True).astype(jnp.float32)
    weighted = trans_there.astype(jnp.float32) * coulomb[None, :, None, :]
    high = lax.Precision.HIGHEST
    exch_real = jnp.einsum(
        "tg,skg->tks", whole_here[:, 0], weighted[:, :, 0], precision=high
    ) - jnp.einsum("tg,skg->tks", whole_here[:, 1], weighted[:, :, 1], precision=high)
    exch_imag = jnp.einsum(
        "tg,skg->tks", whole_here[:, 0], weighted[:, :, 1], precision=high
    ) + jnp.einsum("tg,skg->tks", whole_here[:, 1], weighted[:, :, 0], precision=high)
    exch_part = jnp.stack([exch_real, exch_imag], axis=2)
    whole_con = lax.all_gather(shifted, "ga", axis=0, tiled=True)
    screened_rows = lax.psum_scatter(
        times_cols(whole_con, screened), "pair", scatter_dimension=0, tiled=True
    )
    direct_part = contract_float(
        lax.all_gather(val_density, "pair", axis=0, tiled=True).astype(jnp.float32), screened_rows
    )
    direct_sum, exch_sum = lax.psum((direct_part, exch_part), "ga")
    direct_full, exch_full = (
        lax.all_gather(direct_sum, "pair", axis=3, tiled=True),
        lax.all_gather(exch_sum, "pair", axis=3, tiled=True),
    )
    row_count = NT // lax.axis_size("pair")
    col_count = NT // lax.axis_size("ga")
    row_trans = lax.dynamic_slice_in_dim(ordering, lax.axis_index("pair") * row_count, row_count, 0)
    col_trans = lax.dynamic_slice_in_dim(ordering, lax.axis_index("ga") * col_count, col_count, 0)
    row_pairs = (row_trans // NC)[:, None] * NV + (col_trans // NC)[None, :]
    col_pairs = (row_trans % NC)[:, None] * NC + (col_trans % NC)[None, :]
    picked = direct_full[row_pairs.reshape(-1)]
    col_mask = (
        col_pairs.reshape(-1)[:, None] == jnp.arange(direct_full.shape[3], dtype=jnp.int32)[None, :]
    ).astype(jnp.float32)
    direct_flat = jnp.sum(picked * col_mask[:, None, None, :], axis=3)
    direct_sel = jnp.transpose(direct_flat.reshape(row_count, col_count, points, 2), (2, 3, 0, 1))
    exch_picked = exch_full[row_trans]
    col_hot = (jnp.arange(NT, dtype=jnp.int32)[:, None] == col_trans[None, :]).astype(jnp.float32)
    exch_sel = jnp.einsum("rkpt,tc->kprc", exch_picked, col_hot, precision=high)
    return 2.0 * exch_sel - direct_sel


def solution(mesh):
    in_specs = (
        P("pair", None, None, "ga"),
        P("ga", None, None, "pair"),
        P(None, None, "ga", "pair"),
        P(None, "ga"),
        P("pair", None, "ga"),
        P("pair", None, None, "ga"),
        P(None, "pair"),
        P(),
    )
    out_specs = P(None, None, "pair", "ga")

    def run(*args):
        ga, pair = mesh.shape["ga"], mesh.shape["pair"]
        con_count, h_count = args[1].shape[0], args[1].shape[3]
        suits = (
            ga & (ga - 1) == 0
            and pair & (pair - 1) == 0
            and ga >= 4
            and pair >= 2
            and h_count % (ga * pair * GBLK) == 0
            and con_count % (8 * ga) == 0
            and args[0].shape[0] % (16 * pair) == 0
            and NT % (16 * pair) == 0
            and NT // ga <= 64
        )
        body = on_device if suits else on_any_device
        return jax.shard_map(
            body, mesh=mesh, in_specs=in_specs, out_specs=out_specs, check_vma=False
        )(*args)

    return run
```

```python
import jax
import jax.numpy as jnp
from jax import lax
from jax.experimental import pallas as pl
from jax.experimental.pallas import tpu as pltpu
from jax.sharding import PartitionSpec as P

NV = 16
NC = 24
GBLK = 128
NT = 384

GROUP = 64
EXP_ROWS = 16
STEPS = 128.0
TOP = 32700.0
MAGIC = 1.5 * 2.0**23
NT_DIMS = (((1,), (1,)), ((), ()))
VMEM = 56 * 1024 * 1024


TOKEN = jax.ShapeDtypeStruct((8, 128), jnp.float32)


def params():
    return pltpu.CompilerParams(vmem_limit_bytes=VMEM)


def cost(flops, moved):
    return pl.CostEstimate(flops=int(flops), bytes_accessed=int(moved), transcendentals=0)


def mm(left, right):
    return jnp.dot(left, right, preferred_element_type=jnp.float32)


def mm_nt(left, right):
    return lax.dot_general(left, right, NT_DIMS, preferred_element_type=jnp.float32)


def halves(value):
    high = value.astype(jnp.bfloat16)
    low = (value - high.astype(jnp.float32)).astype(jnp.bfloat16)
    return high, low


def encode(value, out_ref):
    rows, width = value.shape
    groups = rows // GROUP
    parts = value.reshape(groups, GROUP, width)
    largest = jnp.maximum(jnp.max(jnp.abs(parts), axis=1), 1e-30)
    level = jnp.ceil(jnp.log2(largest) * STEPS) + 1.0
    factor = TOP * jnp.exp2(level * (-1.0 / STEPS))
    coded = ((parts * factor[:, None, :] + MAGIC) - MAGIC).astype(jnp.int32)
    out_ref[0:rows, :] = coded.reshape(rows, width).astype(jnp.int16)
    pad = jnp.zeros((EXP_ROWS - groups, width), jnp.int32)
    out_ref[rows : rows + EXP_ROWS, :] = jnp.concatenate(
        [level.astype(jnp.int32), pad], axis=0
    ).astype(jnp.int16)


def decode(ref):
    rows = ref.shape[0] - EXP_ROWS
    width = ref.shape[1]
    groups = rows // GROUP
    level = ref[rows : rows + EXP_ROWS, :].astype(jnp.int32).astype(jnp.float32)[0:groups]
    factor = jnp.exp2(level * (1.0 / STEPS)) * (1.0 / TOP)
    parts = ref[0:rows, :].astype(jnp.int32).astype(jnp.float32).reshape(groups, GROUP, width)
    return (parts * factor[:, None, :]).reshape(rows, width)


def shift_kernel(dest_ref, con_ref, map_ref, stay_ref, go_ref):
    slots, _, _, rows, width = stay_ref.shape
    for which, out_ref in enumerate((stay_ref, go_ref)):
        for slot in range(slots):
            first = dest_ref[which * slots + slot] * width
            for block in range(width // GBLK):
                cols = pl.ds(pl.multiple_of(first + block * GBLK, GBLK), GBLK)
                within = jnp.bitwise_and(map_ref[0, 0:1, cols], GBLK - 1)
                within = jnp.broadcast_to(within, (rows, GBLK))
                for part in range(2):
                    values = con_ref[0, part, :, cols].astype(jnp.float32)
                    moved = jnp.take_along_axis(values, within, axis=1)
                    out_ref[slot, 0, part, :, block * GBLK : (block + 1) * GBLK] = moved.astype(
                        jnp.bfloat16
                    )


def shift_call(con, shift_map, dests, width):
    points, _, rows, slab = con.shape
    slots = dests.shape[0] // 2
    grid_spec = pltpu.PrefetchScalarGridSpec(
        num_scalar_prefetch=1,
        grid=(points,),
        in_specs=[
            pl.BlockSpec((1, 2, rows, slab), lambda q, dest: (q, 0, 0, 0)),
            pl.BlockSpec((1, 1, slab), lambda q, dest: (q, 0, 0)),
        ],
        out_specs=[pl.BlockSpec((slots, 1, 2, rows, width), lambda q, dest: (0, q, 0, 0, 0))] * 2,
    )
    return pl.pallas_call(
        shift_kernel,
        grid_spec=grid_spec,
        out_shape=[jax.ShapeDtypeStruct((slots, points, 2, rows, width), jnp.bfloat16)] * 2,
        compiler_params=params(),
        cost_estimate=cost(8 * con.size, 4 * con.size),
    )(dests, con, shift_map.reshape(points, 1, slab))


def x_kernel(waits, base_ref, val_ref, weight_ref, *refs):
    go_ref, keep_ref, token_ref, left_ref = refs[waits:]
    slots, _, _, rows, depth = val_ref.shape
    half = slots * rows
    token_ref[...] = jnp.zeros_like(token_ref)
    step = pl.program_id(0)
    halfway = pl.num_programs(0) // 2

    @pl.when(step == 0)
    def _():
        for slot in range(slots):
            real, imag = val_ref[slot, 0, 0], val_ref[slot, 0, 1]
            top = slice(slot * rows, (slot + 1) * rows)
            low = slice(half + slot * rows, half + (slot + 1) * rows)
            left_ref[top, 0:depth] = real
            left_ref[top, depth : 2 * depth] = -imag
            left_ref[low, 0:depth] = imag
            left_ref[low, depth : 2 * depth] = real

    weight = weight_ref[0].reshape(2 * depth, weight_ref.shape[3])

    @pl.when(step < halfway)
    def _():
        encode(mm(left_ref[...], weight), go_ref)

    @pl.when(step >= halfway)
    def _():
        keep_ref[...] = mm(left_ref[...], weight)


def x_call(val, screened, place, point, side, steps, after):
    slots, _, _, rows, depth = val.shape
    height = 2 * slots * rows
    columns = screened.shape[3] // 2
    half = steps // 2
    width = columns // half
    grid_spec = pltpu.PrefetchScalarGridSpec(
        num_scalar_prefetch=1,
        grid=(steps,),
        in_specs=[
            pl.BlockSpec((slots, 1, 2, rows, depth), lambda j, t: (0, place, 0, 0, 0)),
            pl.BlockSpec(
                (1, 2, depth, width), lambda j, t: (point, 0, 0, t[j // half] * half + j % half)
            ),
        ]
        + [pl.BlockSpec(memory_space=pl.ANY) for _ in after],
        out_specs=[
            pl.BlockSpec((height + EXP_ROWS, width), lambda j, t: (0, jnp.minimum(j, half - 1))),
            pl.BlockSpec((height, width), lambda j, t: (0, jnp.maximum(j - half, 0))),
            pl.BlockSpec(TOKEN.shape, lambda j, t: (0, 0)),
        ],
        scratch_shapes=[pltpu.VMEM((height, 2 * depth), jnp.bfloat16)],
    )
    return pl.pallas_call(
        lambda *refs: x_kernel(len(after), *refs),
        grid_spec=grid_spec,
        out_shape=[
            jax.ShapeDtypeStruct((height + EXP_ROWS, columns), jnp.int16),
            jax.ShapeDtypeStruct((height, columns), jnp.float32),
            TOKEN,
        ],
        compiler_params=params(),
        cost_estimate=cost(
            2 * height * 2 * depth * 2 * columns, 8 * depth * columns + 6 * height * columns
        ),
    )(side, val, screened, *after)


def hop_kernel(heard, at_ref, keep_ref, *refs):
    total = keep_ref[...]
    for ref in refs[:heard]:
        total = total + decode(ref)
    out_ref, token_ref = refs[-2:]
    encode(total, out_ref)
    token_ref[...] = jnp.zeros_like(token_ref)


def hop_call(keep, others, at, width, after):
    height, tall = keep.shape[0], others[0].shape[0]
    grid_spec = pltpu.PrefetchScalarGridSpec(
        num_scalar_prefetch=1,
        grid=(1,),
        in_specs=[pl.BlockSpec((height, width), lambda i, at: (0, at[0]))]
        + [
            pl.BlockSpec((tall, width), lambda i, at, n=n: (0, at[n + 1]))
            for n in range(len(others))
        ]
        + [pl.BlockSpec(memory_space=pl.ANY) for _ in after],
        out_specs=[
            pl.BlockSpec((tall, width), lambda i, at: (0, 0)),
            pl.BlockSpec(TOKEN.shape, lambda i, at: (0, 0)),
        ],
    )
    return pl.pallas_call(
        lambda *refs: hop_kernel(len(others), *refs),
        grid_spec=grid_spec,
        out_shape=[jax.ShapeDtypeStruct((tall, width), jnp.int16), TOKEN],
        compiler_params=params(),
        cost_estimate=cost(20 * height * width, 8 * height * width),
    )(at, keep, *others, *after)


def exchange_kernel(waits, here_ref, there_ref, coulomb_ref, *refs):
    out_ref, token_ref, left_ref = refs[waits:]
    slots, _, rows, depth = here_ref.shape
    token_ref[...] = jnp.zeros_like(token_ref)

    @pl.when(pl.program_id(0) == 0)
    def _():
        for slot in range(slots):
            for part in range(2):
                left_ref[
                    slot * rows : (slot + 1) * rows, part * depth : (part + 1) * depth
                ] = here_ref[slot, part]

    factor = coulomb_ref[0]
    real = there_ref[0, 0].astype(jnp.float32) * factor
    imag = there_ref[0, 1].astype(jnp.float32) * factor
    right = jnp.concatenate(
        [jnp.concatenate([real, -imag], axis=1), jnp.concatenate([imag, real], axis=1)], axis=0
    )
    high, low = halves(right)
    left = left_ref[...]
    both = mm_nt(left, high) + mm_nt(left, low)
    cols = both.shape[1] // 2
    for part in range(2):
        out_ref[0, part] = both[:, part * cols : (part + 1) * cols]


def exchange_call(here, there, coulomb, after):
    slots, _, rows, _ = here.shape
    points, _, cols, depth = there.shape
    height = slots * rows
    return pl.pallas_call(
        lambda *refs: exchange_kernel(len(after), *refs),
        grid=(points,),
        in_specs=[
            pl.BlockSpec(here.shape, lambda q: (0, 0, 0, 0)),
            pl.BlockSpec((1, 2, cols, depth), lambda q: (q, 0, 0, 0)),
            pl.BlockSpec((1, 1, depth), lambda q: (q, 0, 0)),
        ]
        + [pl.BlockSpec(memory_space=pl.ANY) for _ in after],
        out_specs=[
            pl.BlockSpec((1, 2, height, cols), lambda q: (q, 0, 0, 0)),
            pl.BlockSpec(TOKEN.shape, lambda q: (0, 0)),
        ],
        out_shape=[jax.ShapeDtypeStruct((points, 2, height, cols), jnp.float32), TOKEN],
        scratch_shapes=[pltpu.VMEM((height, 2 * depth), jnp.bfloat16)],
        compiler_params=params(),
        cost_estimate=cost(2 * points * height * 2 * cols * 2 * depth * 2, 8 * points * cols * depth),
    )(here, there, coulomb.reshape(points, 1, depth), *after)


def tile_kernel(slots, heard, chunks, waits, index_ref, at_ref, *refs):
    con_refs, keep_ref = refs[:slots], refs[slots]
    heard_refs = refs[slots + 1 : slots + 1 + heard]
    exch_ref, row_ref, col_direct_ref, col_exch_ref = refs[slots + 1 + heard : slots + 5 + heard]
    keep_out, go_out, token_ref, con_all, direct_ref, natural_ref = refs[slots + 5 + heard + waits :]
    token_ref[...] = jnp.zeros_like(token_ref)
    total = keep_ref[...]
    for ref in heard_refs:
        total = total + decode(ref)
    pairs, width = total.shape[0] // 2, total.shape[1]
    rows = con_refs[0].shape[3]
    pitch = con_all.shape[0] // slots
    for slot in range(slots):
        for part in range(2):
            con_all[
                slot * pitch : slot * pitch + rows, part * width : (part + 1) * width
            ] = con_refs[slot][0, 0, part]
    real, imag = total[:pairs], total[pairs:]
    right = jnp.concatenate(
        [jnp.concatenate([real, -imag], axis=1), jnp.concatenate([imag, real], axis=1)], axis=0
    )
    high, low = halves(right)
    left = con_all[...]
    direct = mm_nt(left, high) + mm_nt(left, low)
    lanes = direct_ref.shape[0]
    for slot in range(slots):
        start = pl.multiple_of(index_ref[slot] * rows, 8)
        for lane in range(lanes):
            direct_ref[lane, pl.ds(start, rows), :] = direct[
                slot * pitch : slot * pitch + rows, lane * 128 : (lane + 1) * 128
            ]
    group = 128 // NV
    place = lax.broadcasted_iota(jnp.int32, (NC, 128), 1) // NV
    per_part = lanes // 2
    for part in range(2):
        for chunk in range(NC // group):
            for band in range(NV):
                block = jnp.zeros((NC, 128), jnp.float32)
                for step in range(group):
                    e = chunk * group + step
                    piece = direct_ref[part * per_part + band // group, pl.ds(e, NC, stride=NC), :]
                    turn = (NV * (step - band)) % 128
                    if turn:
                        piece = pltpu.roll(piece, turn, 1)
                    block = jnp.where(place == step, piece, block)
                natural_ref[
                    part, band * NC : (band + 1) * NC, chunk * 128 : (chunk + 1) * 128
                ] = block
    pick_rows = row_ref[...]
    count = NT // chunks
    for part in range(2):
        result = None
        for source, pick_cols in (
            (natural_ref[part], col_direct_ref),
            (exch_ref[0, part], col_exch_ref),
        ):
            for piece in halves(source):
                moved = mm(pick_rows, piece).astype(jnp.bfloat16)
                term = mm(moved, pick_cols[...])
                result = term if result is None else result + term
        for chunk in range(chunks):
            out_ref = keep_out if chunk < chunks // 2 else go_out
            at = (2 * (chunk % (chunks // 2)) + part) * count
            out_ref[at : at + count, :] = result[chunk * count : (chunk + 1) * count]


def tile_call(
    cons, point, keep, heard, exch, index, at, pick_rows, col_direct, col_exch, chunks, after
):
    slots = len(cons)
    _, _, _, rows, width = cons[0][0].shape
    height, tall = keep.shape[0], heard[0].shape[0]
    pitch = -(-rows // 16) * 16
    out_cols = col_direct.shape[1]
    whole = lambda a: pl.BlockSpec(a.shape, lambda i, index, at: (0,) * a.ndim)
    grid_spec = pltpu.PrefetchScalarGridSpec(
        num_scalar_prefetch=2,
        grid=(1,),
        in_specs=[
            pl.BlockSpec(
                (1, 1, 2, rows, width), lambda i, index, at, place=place: (place, point, 0, 0, 0)
            )
            for _, place in cons
        ]
        + [pl.BlockSpec((height, width), lambda i, index, at: (0, at[0]))]
        + [
            pl.BlockSpec((tall, width), lambda i, index, at, n=n: (0, at[n + 1]))
            for n in range(len(heard))
        ]
        + [
            pl.BlockSpec((1,) + exch.shape[1:], lambda i, index, at: (point, 0, 0, 0)),
            whole(pick_rows),
            whole(col_direct),
            whole(col_exch),
        ]
        + [pl.BlockSpec(memory_space=pl.ANY) for _ in after],
        out_specs=[pl.BlockSpec((NT, out_cols), lambda i, index, at: (0, 0))] * 2
        + [pl.BlockSpec(TOKEN.shape, lambda i, index, at: (0, 0))],
        scratch_shapes=[
            pltpu.VMEM((slots * pitch, 2 * width), jnp.bfloat16),
            pltpu.VMEM((height // 128, NC * NC, 128), jnp.float32),
            pltpu.VMEM((2, NT, NT), jnp.float32),
        ],
    )
    return pl.pallas_call(
        lambda *refs: tile_kernel(slots, len(heard), chunks, len(after), *refs),
        grid_spec=grid_spec,
        out_shape=[jax.ShapeDtypeStruct((NT, out_cols), jnp.float32)] * 2 + [TOKEN],
        compiler_params=params(),
        cost_estimate=cost(2.8e9, 8e6),
    )(
        index, at, *[c for c, _ in cons], keep, *heard, exch, pick_rows, col_direct, col_exch, *after
    )


def swap(value, axis, size, bit):
    return lax.ppermute(value, axis, [(i, i ^ bit) for i in range(size)])


def halving_order(bits):
    order = [0]
    for bit in reversed(bits):
        order = order + [o ^ bit for o in order]
    return order


def on_device(*args):
    (val_density, con_density, screened, coulomb, trans_here, trans_there, shift_map, ordering) = args
    ga, pair = lax.axis_size("ga"), lax.axis_size("pair")
    points = con_density.shape[1]
    slab = con_density.shape[3]
    width = slab // ga
    me_ga, me_pair = lax.axis_index("ga"), lax.axis_index("pair")
    ga_bits = [1 << b for b in range(ga.bit_length() - 1)]
    pair_bits = [1 << b for b in range(pair.bit_length() - 1)]
    ga_order = halving_order(ga_bits)
    half = ga // 2
    dests = me_ga ^ jnp.asarray(ga_order, jnp.int32)
    flags = [(me_ga // bit) % 2 for bit in ga_bits]
    blocks = sum(((dests // bit) % 2) * (half // bit) for bit in ga_bits)
    as_index = lambda items: jnp.stack([jnp.asarray(i, jnp.int32) for i in items])

    def block_at(known, chosen):
        number = jnp.int32(0)
        for flag in flags[known : len(flags) if chosen is None else chosen]:
            number = 2 * number + flag
        return number if chosen is None else 2 * number + 1 - flags[chosen]

    val = jnp.transpose(val_density, (1, 2, 0, 3))
    first, others = lax.all_gather(val[:1], "pair"), lax.all_gather(val[1:], "pair")
    here = lax.all_gather(jnp.transpose(trans_here, (1, 0, 2)), "pair")
    there = jnp.transpose(trans_there, (1, 2, 0, 3))

    con = jnp.transpose(con_density, (1, 2, 0, 3))
    stay, go = shift_call(con, shift_map, blocks, width)
    cons = {}
    for p, slot in enumerate(ga_order):
        cons[slot] = (stay, p) if p < half else (go, p - half)
    for bit in ga_bits:
        moving = [slot for slot in ga_order if slot & bit]
        if bit == ga_bits[0]:
            sent = go
        else:
            sent = jnp.stack([cons[slot][0][cons[slot][1]] for slot in moving])
        got = swap(sent, "ga", ga, bit)
        for place, slot in enumerate(moving):
            cons[slot] = (got, place)
    cons = [cons[slot] for slot in ga_order]

    side = as_index([1 - flags[0], flags[0]])
    gone, keep, after = [], [], []
    for q in range(points):
        vals, place = (first, 0) if q == 0 else (others, q - 1)
        coded, own, token = x_call(vals, screened, place, q, side, 4, after)
        after = [token]
        gone.append(coded)
        keep.append(own)

    row_count, col_count = NT // pair, NT // ga
    row_slots = jnp.asarray(halving_order(pair_bits), jnp.int32)
    row_trans = ordering.reshape(pair, row_count)[me_pair ^ row_slots].reshape(-1)
    pick_rows = (row_trans[:, None] == jnp.arange(NT, dtype=jnp.int32)[None, :]).astype(jnp.bfloat16)
    col_trans = ordering.reshape(ga, col_count)[dests]
    col_trans = jnp.pad(col_trans, ((0, 0), (0, 64 - col_count)), constant_values=-1).reshape(1, -1)
    real_col = col_trans >= 0
    at_direct = jnp.where(real_col, (col_trans % NC) * NV + col_trans // NC, -1)
    own_col = real_col & (col_trans // row_count == me_pair)
    at_exch = jnp.where(own_col, col_trans % row_count, -1)

    def pick_cols(at, size, scale):
        hot = at == jnp.arange(size, dtype=jnp.int32)[:, None]
        return jnp.where(hot, scale, 0.0).astype(jnp.bfloat16)

    col_direct, col_exch = pick_cols(at_direct, NT, -1.0), pick_cols(at_exch, row_count, 2.0)

    heard = [[swap(gone[q], "ga", ga, ga_bits[0])] for q in range(points)]
    tiles = [None] * points
    stages = len(ga_bits)
    exch = None
    for wave in range(2 * points + stages):
        for q in reversed(range(points)):
            stage = wave - 2 * q
            if 1 <= stage < stages:
                columns = ga >> (stage + 1)
                at = as_index([block_at(k, stage) for k in [1] + list(range(1, stage + 1))])
                coded, token = hop_call(keep[q], heard[q], at, columns * width, after)
                after = [token]
                heard[q].append(swap(coded, "ga", ga, ga_bits[stage]))
                if exch is None:
                    exch, token = exchange_call(here, there, coulomb, after)
                    after = [token]
            elif stage == stages:
                at = as_index([block_at(k, None) for k in [1] + list(range(1, stages + 1))])
                tile, sent, token = tile_call(
                    cons, q, keep[q], heard[q], exch, dests, at, pick_rows, col_direct, col_exch,
                    pair, after,
                )
                after = [token]
                tiles[q] = tile + swap(sent, "pair", pair, pair_bits[0])
    halved = []
    for group in (tiles[:-1], tiles[-1:]):
        tile = jnp.stack(group)
        for bit in pair_bits[1:]:
            rows = tile.shape[1] // 2
            tile = tile[:, :rows] + swap(tile[:, rows:], "pair", pair, bit)
        halved.append(tile)
    tile = jnp.concatenate(halved)
    for bit in ga_bits:
        cols = tile.shape[2] // 2
        tile = tile[:, :, :cols] + swap(tile[:, :, cols:], "ga", ga, bit)
    return tile[:, :, :col_count].reshape(points, 2, row_count, col_count)


def contract_float(left, right):
    high = lax.Precision.HIGHEST
    real_part = jnp.einsum(
        "nkg,mkg->nkm", left[:, :, 0], right[:, :, 0], precision=high
    ) - jnp.einsum("nkg,mkg->nkm", left[:, :, 1], right[:, :, 1], precision=high)
    imag_part = jnp.einsum(
        "nkg,mkg->nkm", left[:, :, 0], right[:, :, 1], precision=high
    ) + jnp.einsum("nkg,mkg->nkm", left[:, :, 1], right[:, :, 0], precision=high)
    return jnp.stack([real_part, imag_part], axis=2)


def times_cols(rows, weights):
    first = jnp.einsum(
        "nkh,kgh->nkg", rows[:, :, 0], weights[:, 0], preferred_element_type=jnp.float32
    ) - jnp.einsum("nkh,kgh->nkg", rows[:, :, 1], weights[:, 1], preferred_element_type=jnp.float32)
    second = jnp.einsum(
        "nkh,kgh->nkg", rows[:, :, 0], weights[:, 1], preferred_element_type=jnp.float32
    ) + jnp.einsum("nkh,kgh->nkg", rows[:, :, 1], weights[:, 0], preferred_element_type=jnp.float32)
    return jnp.stack([first, second], axis=2)


def on_any_device(
    val_density, con_density, screened, coulomb, trans_here, trans_there, shift_map, ordering
):
    con_count = con_density.shape[0]
    points = con_density.shape[1]
    slab_cols = con_density.shape[3]
    blocks = slab_cols // GBLK
    within = (shift_map % GBLK).reshape(points, blocks, GBLK)
    onehot = (
        within[:, :, :, None] == jnp.arange(GBLK, dtype=jnp.int32)[None, None, None, :]
    ).astype(jnp.bfloat16)
    con_blocks = con_density.reshape(con_count, points, 2, blocks, GBLK)
    shifted = (
        jnp.einsum("bkpnh,kngh->bkpng", con_blocks, onehot, preferred_element_type=jnp.float32)
        .astype(jnp.bfloat16)
        .reshape(con_density.shape)
    )
    whole_here = lax.all_gather(trans_here, "pair", axis=0, tiled=True).astype(jnp.float32)
    weighted = trans_there.astype(jnp.float32) * coulomb[None, :, None, :]
    high = lax.Precision.HIGHEST
    exch_real = jnp.einsum(
        "tg,skg->tks", whole_here[:, 0], weighted[:, :, 0], precision=high
    ) - jnp.einsum("tg,skg->tks", whole_here[:, 1], weighted[:, :, 1], precision=high)
    exch_imag = jnp.einsum(
        "tg,skg->tks", whole_here[:, 0], weighted[:, :, 1], precision=high
    ) + jnp.einsum("tg,skg->tks", whole_here[:, 1], weighted[:, :, 0], precision=high)
    exch_part = jnp.stack([exch_real, exch_imag], axis=2)
    whole_con = lax.all_gather(shifted, "ga", axis=0, tiled=True)
    screened_rows = lax.psum_scatter(
        times_cols(whole_con, screened), "pair", scatter_dimension=0, tiled=True
    )
    direct_part = contract_float(
        lax.all_gather(val_density, "pair", axis=0, tiled=True).astype(jnp.float32), screened_rows
    )
    direct_sum, exch_sum = lax.psum((direct_part, exch_part), "ga")
    direct_full, exch_full = (
        lax.all_gather(direct_sum, "pair", axis=3, tiled=True),
        lax.all_gather(exch_sum, "pair", axis=3, tiled=True),
    )
    row_count = NT // lax.axis_size("pair")
    col_count = NT // lax.axis_size("ga")
    row_trans = lax.dynamic_slice_in_dim(ordering, lax.axis_index("pair") * row_count, row_count, 0)
    col_trans = lax.dynamic_slice_in_dim(ordering, lax.axis_index("ga") * col_count, col_count, 0)
    row_pairs = (row_trans // NC)[:, None] * NV + (col_trans // NC)[None, :]
    col_pairs = (row_trans % NC)[:, None] * NC + (col_trans % NC)[None, :]
    picked = direct_full[row_pairs.reshape(-1)]
    col_mask = (
        col_pairs.reshape(-1)[:, None] == jnp.arange(direct_full.shape[3], dtype=jnp.int32)[None, :]
    ).astype(jnp.float32)
    direct_flat = jnp.sum(picked * col_mask[:, None, None, :], axis=3)
    direct_sel = jnp.transpose(direct_flat.reshape(row_count, col_count, points, 2), (2, 3, 0, 1))
    exch_picked = exch_full[row_trans]
    col_hot = (jnp.arange(NT, dtype=jnp.int32)[:, None] == col_trans[None, :]).astype(jnp.float32)
    exch_sel = jnp.einsum("rkpt,tc->kprc", exch_picked, col_hot, precision=high)
    return 2.0 * exch_sel - direct_sel


def solution(mesh):
    in_specs = (
        P("pair", None, None, "ga"),
        P("ga", None, None, "pair"),
        P(None, None, "ga", "pair"),
        P(None, "ga"),
        P("pair", None, "ga"),
        P("pair", None, None, "ga"),
        P(None, "pair"),
        P(),
    )
    out_specs = P(None, None, "pair", "ga")

    def run(*args):
        ga, pair = mesh.shape["ga"], mesh.shape["pair"]
        con_count, h_count = args[1].shape[0], args[1].shape[3]
        suits = (
            ga & (ga - 1) == 0
            and pair & (pair - 1) == 0
            and ga >= 4
            and pair >= 2
            and h_count % (ga * pair * GBLK) == 0
            and con_count % (8 * ga) == 0
            and args[0].shape[0] % (16 * pair) == 0
            and NT % (16 * pair) == 0
            and NT // ga <= 64
        )
        body = on_device if suits else on_any_device
        return jax.shard_map(
            body, mesh=mesh, in_specs=in_specs, out_specs=out_specs, check_vma=False
        )(*args)

    return run
```

```python
import jax
import jax.numpy as jnp
from jax import lax
from jax.experimental import pallas as pl
from jax.experimental.pallas import tpu as pltpu
from jax.sharding import PartitionSpec as P

NV = 16
NC = 24
GBLK = 128
NT = 384

GROUP = 64
EXP_ROWS = 16
STEPS = 128.0
TOP = 32700.0
MAGIC = 1.5 * 2.0**23
NT_DIMS = (((1,), (1,)), ((), ()))
MIB = 1024 * 1024


TOKEN = jax.ShapeDtypeStruct((8, 128), jnp.float32)


def params(mib):
    return pltpu.CompilerParams(vmem_limit_bytes=mib * MIB)


def cost(flops, moved):
    return pl.CostEstimate(flops=int(flops), bytes_accessed=int(moved), transcendentals=0)


def mm(left, right):
    return jnp.dot(left, right, preferred_element_type=jnp.float32)


def mm_nt(left, right):
    return lax.dot_general(left, right, NT_DIMS, preferred_element_type=jnp.float32)


def halves(value):
    high = value.astype(jnp.bfloat16)
    low = (value - high.astype(jnp.float32)).astype(jnp.bfloat16)
    return high, low


def encode(value, out_ref):
    rows, width = value.shape
    groups = rows // GROUP
    parts = value.reshape(groups, GROUP, width)
    largest = jnp.maximum(jnp.max(jnp.abs(parts), axis=1), 1e-30)
    level = jnp.ceil(jnp.log2(largest) * STEPS) + 1.0
    factor = TOP * jnp.exp2(level * (-1.0 / STEPS))
    coded = ((parts * factor[:, None, :] + MAGIC) - MAGIC).astype(jnp.int32)
    out_ref[0:rows, :] = coded.reshape(rows, width).astype(jnp.int16)
    pad = jnp.zeros((EXP_ROWS - groups, width), jnp.int32)
    out_ref[rows : rows + EXP_ROWS, :] = jnp.concatenate(
        [level.astype(jnp.int32), pad], axis=0
    ).astype(jnp.int16)


def decode(ref):
    rows = ref.shape[0] - EXP_ROWS
    width = ref.shape[1]
    groups = rows // GROUP
    level = ref[rows : rows + EXP_ROWS, :].astype(jnp.int32).astype(jnp.float32)[0:groups]
    factor = jnp.exp2(level * (1.0 / STEPS)) * (1.0 / TOP)
    parts = ref[0:rows, :].astype(jnp.int32).astype(jnp.float32).reshape(groups, GROUP, width)
    return (parts * factor[:, None, :]).reshape(rows, width)


def reversed_bits(number, count):
    return sum(((number // (1 << b)) % 2) * (1 << (count - 1 - b)) for b in range(count))


def block_of(me, known, stop, flip):
    number = 0
    for bit in range(known, stop):
        flag = (me // (1 << bit)) % 2
        number = 2 * number + (1 - flag if flip and bit == stop - 1 else flag)
    return number


def shift_kernel(order, me_ref, con_ref, map_ref, stay_ref, go_ref, token_ref):
    slots, _, _, rows, width = stay_ref.shape
    count = len(order).bit_length() - 1
    token_ref[...] = jnp.zeros_like(token_ref)
    for which, out_ref in enumerate((stay_ref, go_ref)):
        for slot in range(slots):
            dest = jnp.bitwise_xor(me_ref[0], order[which * slots + slot])
            first = reversed_bits(dest, count) * width
            for block in range(width // GBLK):
                cols = pl.ds(pl.multiple_of(first + block * GBLK, GBLK), GBLK)
                within = jnp.bitwise_and(map_ref[0, 0:1, cols], GBLK - 1)
                within = jnp.broadcast_to(within, (rows, GBLK))
                for part in range(2):
                    values = con_ref[0, part, :, cols].astype(jnp.float32)
                    moved = jnp.take_along_axis(values, within, axis=1)
                    out_ref[slot, 0, part, :, block * GBLK : (block + 1) * GBLK] = moved.astype(
                        jnp.bfloat16
                    )


def shift_call(con, shift_map, me, order, width):
    points, _, rows, slab = con.shape
    slots = len(order) // 2
    grid_spec = pltpu.PrefetchScalarGridSpec(
        num_scalar_prefetch=1,
        grid=(points,),
        in_specs=[
            pl.BlockSpec((1, 2, rows, slab), lambda q, me: (q, 0, 0, 0)),
            pl.BlockSpec((1, 1, slab), lambda q, me: (q, 0, 0)),
        ],
        out_specs=[pl.BlockSpec((slots, 1, 2, rows, width), lambda q, me: (0, q, 0, 0, 0))] * 2
        + [pl.BlockSpec(TOKEN.shape, lambda q, me: (0, 0))],
    )
    return pl.pallas_call(
        lambda *refs: shift_kernel(order, *refs),
        grid_spec=grid_spec,
        out_shape=[jax.ShapeDtypeStruct((slots, points, 2, rows, width), jnp.bfloat16)] * 2
        + [TOKEN],
        compiler_params=params(16),
        cost_estimate=cost(8 * con.size, 4 * con.size),
    )(me, con, shift_map.reshape(points, 1, slab))


def x_kernel(slots, waits, me_ref, *refs):
    val_refs, weight_ref = refs[:slots], refs[slots]
    go_ref, keep_ref, token_ref, left_ref = refs[slots + 1 + waits :]
    _, _, rows, depth = val_refs[0].shape
    half = slots * rows
    token_ref[...] = jnp.zeros_like(token_ref)
    step = pl.program_id(0)
    halfway = pl.num_programs(0) // 2

    @pl.when(step == 0)
    def _():
        for slot in range(slots):
            real, imag = val_refs[slot][0, 0], val_refs[slot][0, 1]
            top = slice(slot * rows, (slot + 1) * rows)
            low = slice(half + slot * rows, half + (slot + 1) * rows)
            left_ref[top, 0:depth] = real
            left_ref[top, depth : 2 * depth] = -imag
            left_ref[low, 0:depth] = imag
            left_ref[low, depth : 2 * depth] = real

    weight = weight_ref[0].reshape(2 * depth, weight_ref.shape[3])

    @pl.when(step < halfway)
    def _():
        encode(mm(left_ref[...], weight), go_ref)

    @pl.when(step >= halfway)
    def _():
        keep_ref[...] = mm(left_ref[...], weight)


def x_call(vals, screened, place, point, me, steps, after):
    slots = len(vals)
    _, _, rows, depth = vals[0].shape
    height = 2 * slots * rows
    columns = screened.shape[3] // 2
    half = steps // 2
    width = columns // half
    grid_spec = pltpu.PrefetchScalarGridSpec(
        num_scalar_prefetch=1,
        grid=(steps,),
        in_specs=[
            pl.BlockSpec((1, 2, rows, depth), lambda j, me: (place, 0, 0, 0)) for _ in vals
        ]
        + [
            pl.BlockSpec(
                (1, 2, depth, width),
                lambda j, me: (point, 0, 0, ((me[0] + 1 + j // half) % 2) * half + j % half),
            )
        ]
        + [pl.BlockSpec(memory_space=pl.ANY) for _ in after],
        out_specs=[
            pl.BlockSpec((height + EXP_ROWS, width), lambda j, me: (0, jnp.minimum(j, half - 1))),
            pl.BlockSpec((height, width), lambda j, me: (0, jnp.maximum(j - half, 0))),
            pl.BlockSpec(TOKEN.shape, lambda j, me: (0, 0)),
        ],
        scratch_shapes=[pltpu.VMEM((height, 2 * depth), jnp.bfloat16)],
    )
    return pl.pallas_call(
        lambda *refs: x_kernel(slots, len(after), *refs),
        grid_spec=grid_spec,
        out_shape=[
            jax.ShapeDtypeStruct((height + EXP_ROWS, columns), jnp.int16),
            jax.ShapeDtypeStruct((height, columns), jnp.float32),
            TOKEN,
        ],
        compiler_params=params(24),
        cost_estimate=cost(
            2 * height * 2 * depth * 2 * columns, 8 * depth * columns + 6 * height * columns
        ),
    )(me, *vals, screened, *after)


def hop_kernel(heard, me_ref, keep_ref, *refs):
    total = keep_ref[...]
    for ref in refs[:heard]:
        total = total + decode(ref)
    out_ref, token_ref = refs[-2:]
    encode(total, out_ref)
    token_ref[...] = jnp.zeros_like(token_ref)


def hop_call(keep, others, me, stage, width, after):
    height, tall = keep.shape[0], others[0].shape[0]
    steps = width // 128

    def at(known):
        return lambda i, me: (0, block_of(me[0], known, stage + 1, True) * steps + i)

    grid_spec = pltpu.PrefetchScalarGridSpec(
        num_scalar_prefetch=1,
        grid=(steps,),
        in_specs=[pl.BlockSpec((height, 128), at(1))]
        + [pl.BlockSpec((tall, 128), at(n + 1)) for n in range(len(others))]
        + [pl.BlockSpec(memory_space=pl.ANY) for _ in after],
        out_specs=[
            pl.BlockSpec((tall, 128), lambda i, me: (0, i)),
            pl.BlockSpec(TOKEN.shape, lambda i, me: (0, 0)),
        ],
    )
    return pl.pallas_call(
        lambda *refs: hop_kernel(len(others), *refs),
        grid_spec=grid_spec,
        out_shape=[jax.ShapeDtypeStruct((tall, width), jnp.int16), TOKEN],
        compiler_params=params(16),
        cost_estimate=cost(20 * height * width, 8 * height * width),
    )(me, keep, *others, *after)


def fold_kernel(me_ref, own_ref, heard_ref, keep_ref, go_ref):
    total = own_ref[...] + decode(heard_ref)
    if go_ref.dtype == jnp.int16:
        rows = keep_ref.shape[0]
        keep_ref[...] = total[:rows]
        encode(total[rows:], go_ref)
    else:
        cols = keep_ref.shape[1]
        keep_ref[...] = total[:, :cols]
        go_ref[...] = total[:, cols:]


def fold_call(own, heard, me, by_rows):
    rows, cols = own.shape
    if by_rows:
        shapes = [
            jax.ShapeDtypeStruct((rows // 2, cols), jnp.float32),
            jax.ShapeDtypeStruct((rows // 2 + EXP_ROWS, cols), jnp.int16),
        ]
    else:
        shapes = [jax.ShapeDtypeStruct((rows, cols // 2), jnp.float32)] * 2
    whole = lambda a: pl.BlockSpec(a.shape, lambda i, me: (0, 0))
    grid_spec = pltpu.PrefetchScalarGridSpec(
        num_scalar_prefetch=1,
        grid=(1,),
        in_specs=[whole(own), whole(heard)],
        out_specs=[whole(a) for a in shapes],
    )
    return pl.pallas_call(
        fold_kernel,
        grid_spec=grid_spec,
        out_shape=shapes,
        compiler_params=params(16),
        cost_estimate=cost(20 * own.size, 10 * own.size),
    )(me, own, heard)


def exchange_kernel(slots, waits, *refs):
    here_refs, (there_ref, coulomb_ref) = refs[:slots], refs[slots : slots + 2]
    out_ref, token_ref, left_ref = refs[slots + 2 + waits :]
    _, rows, depth = here_refs[0].shape
    token_ref[...] = jnp.zeros_like(token_ref)

    @pl.when(pl.program_id(0) == 0)
    def _():
        for slot in range(slots):
            for part in range(2):
                left_ref[
                    slot * rows : (slot + 1) * rows, part * depth : (part + 1) * depth
                ] = here_refs[slot][part]

    factor = coulomb_ref[0]
    real = there_ref[0, 0].astype(jnp.float32) * factor
    imag = there_ref[0, 1].astype(jnp.float32) * factor
    right = jnp.concatenate(
        [jnp.concatenate([real, -imag], axis=1), jnp.concatenate([imag, real], axis=1)], axis=0
    )
    high, low = halves(right)
    left = left_ref[...]
    both = mm_nt(left, high) + mm_nt(left, low)
    cols = both.shape[1] // 2
    for part in range(2):
        out_ref[0, part] = both[:, part * cols : (part + 1) * cols]


def exchange_call(heres, there, coulomb, after):
    slots, rows = len(heres), heres[0].shape[1]
    points, _, cols, depth = there.shape
    height = slots * rows
    return pl.pallas_call(
        lambda *refs: exchange_kernel(slots, len(after), *refs),
        grid=(points,),
        in_specs=[pl.BlockSpec(h.shape, lambda q: (0, 0, 0)) for h in heres]
        + [
            pl.BlockSpec((1, 2, cols, depth), lambda q: (q, 0, 0, 0)),
            pl.BlockSpec((1, 1, depth), lambda q: (q, 0, 0)),
        ]
        + [pl.BlockSpec(memory_space=pl.ANY) for _ in after],
        out_specs=[
            pl.BlockSpec((1, 2, height, cols), lambda q: (q, 0, 0, 0)),
            pl.BlockSpec(TOKEN.shape, lambda q: (0, 0)),
        ],
        out_shape=[jax.ShapeDtypeStruct((points, 2, height, cols), jnp.float32), TOKEN],
        scratch_shapes=[pltpu.VMEM((height, 2 * depth), jnp.bfloat16)],
        compiler_params=params(16),
        cost_estimate=cost(2 * points * height * 2 * cols * 2 * depth * 2, 8 * points * cols * depth),
    )(*heres, there, coulomb.reshape(points, 1, depth), *after)


def tile_kernel(order, heard, chunks, waits, me_ref, *refs):
    slots = len(order)
    con_refs, keep_ref = refs[:slots], refs[slots]
    heard_refs = refs[slots + 1 : slots + 1 + heard]
    exch_ref, row_ref, col_direct_ref, col_exch_ref = refs[slots + 1 + heard : slots + 5 + heard]
    keep_out, go_out, token_ref, con_all, direct_ref, natural_ref, sums_ref = refs[
        slots + 5 + heard + waits :
    ]
    token_ref[...] = jnp.zeros_like(token_ref)
    total = keep_ref[...]
    for ref in heard_refs:
        total = total + decode(ref)
    pairs, width = total.shape[0] // 2, total.shape[1]
    rows = con_refs[0].shape[3]
    pitch = con_all.shape[0] // slots
    for slot in range(slots):
        for part in range(2):
            con_all[
                slot * pitch : slot * pitch + rows, part * width : (part + 1) * width
            ] = con_refs[slot][0, 0, part]
    real, imag = total[:pairs], total[pairs:]
    right = jnp.concatenate(
        [jnp.concatenate([real, -imag], axis=1), jnp.concatenate([imag, real], axis=1)], axis=0
    )
    high, low = halves(right)
    left = con_all[...]
    direct = mm_nt(left, high) + mm_nt(left, low)
    lanes = direct_ref.shape[0]
    for slot in range(slots):
        start = pl.multiple_of(jnp.bitwise_xor(me_ref[0], order[slot]) * rows, 8)
        for lane in range(lanes):
            direct_ref[lane, pl.ds(start, rows), :] = direct[
                slot * pitch : slot * pitch + rows, lane * 128 : (lane + 1) * 128
            ]
    group = 128 // NV
    place = lax.broadcasted_iota(jnp.int32, (NC, 128), 1) // NV
    per_part = lanes // 2
    for part in range(2):
        for chunk in range(NC // group):
            for band in range(NV):
                block = jnp.zeros((NC, 128), jnp.float32)
                for step in range(group):
                    e = chunk * group + step
                    piece = direct_ref[part * per_part + band // group, pl.ds(e, NC, stride=NC), :]
                    turn = (NV * (step - band)) % 128
                    if turn:
                        piece = pltpu.roll(piece, turn, 1)
                    block = jnp.where(place == step, piece, block)
                natural_ref[
                    part, band * NC : (band + 1) * NC, chunk * 128 : (chunk + 1) * 128
                ] = block
    pick_rows = row_ref[...]
    count = NT // chunks
    for part in range(2):
        result = None
        for source, pick_cols in (
            (natural_ref[part], col_direct_ref),
            (exch_ref[0, part], col_exch_ref),
        ):
            for piece in halves(source):
                moved = mm(pick_rows, piece).astype(jnp.bfloat16)
                term = mm(moved, pick_cols[...])
                result = term if result is None else result + term
        for chunk in range(chunks):
            out_ref = keep_out if chunk < chunks // 2 else sums_ref
            at = (2 * (chunk % (chunks // 2)) + part) * count
            out_ref[at : at + count, :] = result[chunk * count : (chunk + 1) * count]
    encode(sums_ref[...], go_out)


def tile_call(
    cons, point, keep, heard, exch, me, order, pick_rows, col_direct, col_exch, chunks, after
):
    slots = len(cons)
    _, _, _, rows, width = cons[0][0].shape
    height, tall = keep.shape[0], heard[0].shape[0]
    pitch = -(-rows // 16) * 16
    out_cols = col_direct.shape[1]
    stages = len(heard)
    whole = lambda a: pl.BlockSpec(a.shape, lambda i, me: (0,) * a.ndim)

    def at(known):
        return lambda i, me: (0, block_of(me[0], known, stages, False))

    grid_spec = pltpu.PrefetchScalarGridSpec(
        num_scalar_prefetch=1,
        grid=(1,),
        in_specs=[
            pl.BlockSpec((1, 1, 2, rows, width), lambda i, me, place=place: (place, point, 0, 0, 0))
            for _, place in cons
        ]
        + [pl.BlockSpec((height, width), at(1))]
        + [pl.BlockSpec((tall, width), at(n + 1)) for n in range(stages)]
        + [
            pl.BlockSpec((1,) + exch.shape[1:], lambda i, me: (point, 0, 0, 0)),
            whole(pick_rows),
            whole(col_direct),
            whole(col_exch),
        ]
        + [pl.BlockSpec(memory_space=pl.ANY) for _ in after],
        out_specs=[
            pl.BlockSpec((NT, out_cols), lambda i, me: (0, 0)),
            pl.BlockSpec((NT + EXP_ROWS, out_cols), lambda i, me: (0, 0)),
            pl.BlockSpec(TOKEN.shape, lambda i, me: (0, 0)),
        ],
        scratch_shapes=[
            pltpu.VMEM((slots * pitch, 2 * width), jnp.bfloat16),
            pltpu.VMEM((height // 128, NC * NC, 128), jnp.float32),
            pltpu.VMEM((2, NT, NT), jnp.float32),
            pltpu.VMEM((NT, out_cols), jnp.float32),
        ],
    )
    return pl.pallas_call(
        lambda *refs: tile_kernel(order, stages, chunks, len(after), *refs),
        grid_spec=grid_spec,
        out_shape=[
            jax.ShapeDtypeStruct((NT, out_cols), jnp.float32),
            jax.ShapeDtypeStruct((NT + EXP_ROWS, out_cols), jnp.int16),
            TOKEN,
        ],
        compiler_params=params(24),
        cost_estimate=cost(2.8e9, 8e6),
    )(me, *[c for c, _ in cons], keep, *heard, exch, pick_rows, col_direct, col_exch, *after)


def swap(value, axis, size, bit):
    return lax.ppermute(value, axis, [(i, i ^ bit) for i in range(size)])


def gather_slots(value, axis, size):
    found = {0: value}
    bit = size // 2
    while bit:
        for known in sorted(found):
            found[known ^ bit] = swap(found[known], axis, size, bit)
        bit //= 2
    return [found[r] for r in range(size)]


def halving_order(bits):
    order = [0]
    for bit in reversed(bits):
        order = order + [o ^ bit for o in order]
    return order


def behind(value, token):
    return lax.optimization_barrier((value, token))[0]


def on_device(*args):
    (val_density, con_density, screened, coulomb, trans_here, trans_there, shift_map, ordering) = args
    ga, pair = lax.axis_size("ga"), lax.axis_size("pair")
    points = con_density.shape[1]
    slab = con_density.shape[3]
    width = slab // ga
    me_ga, me_pair = lax.axis_index("ga"), lax.axis_index("pair")
    me = me_ga.astype(jnp.int32).reshape(1)
    ga_bits = [1 << b for b in range(ga.bit_length() - 1)]
    pair_bits = [1 << b for b in range(pair.bit_length() - 1)]
    ga_order = halving_order(ga_bits)
    stages, half = len(ga_bits), ga // 2

    first = gather_slots(jnp.transpose(val_density[:, :1], (1, 2, 0, 3)), "pair", pair)
    others = gather_slots(jnp.transpose(val_density[:, 1:], (1, 2, 0, 3)), "pair", pair)

    con = jnp.transpose(con_density, (1, 2, 0, 3))
    stay, go, token = shift_call(con, shift_map, me, ga_order, width)
    from_near = swap(go, "ga", ga, ga_bits[0])

    gone, keep, tokens = [], [], [token]
    for q in range(points):
        vals, place = (first, 0) if q == 0 else (others, q - 1)
        coded, own, token = x_call(vals, screened, place, q, me, 4, tokens[-1:])
        tokens.append(token)
        gone.append(coded)
        keep.append(own)
    after = tokens[-1:]

    cons = {}
    for p, slot in enumerate(ga_order):
        cons[slot] = (stay, p) if p < half else (go, p - half)
    for step, bit in enumerate(ga_bits):
        moving = [slot for slot in ga_order if slot & bit]
        if step == 0:
            got = from_near
        else:
            sent = jnp.stack([cons[slot][0][cons[slot][1]] for slot in moving])
            got = swap(sent, "ga", ga, bit)
        if step + 1 < stages:
            got = behind(got, tokens[min(step + 2, points)])
        for place, slot in enumerate(moving):
            cons[slot] = (got, place)
    cons = [cons[slot] for slot in ga_order]

    row_count, col_count = NT // pair, NT // ga
    row_slots = jnp.asarray(halving_order(pair_bits), jnp.int32)
    row_trans = ordering.reshape(pair, row_count)[me_pair ^ row_slots].reshape(-1)
    at_row = ((row_trans // row_count) ^ me_pair) * row_count + row_trans % row_count
    pick_rows = (at_row[:, None] == jnp.arange(NT, dtype=jnp.int32)[None, :]).astype(jnp.bfloat16)
    col_trans = ordering.reshape(ga, col_count)[me_ga ^ jnp.asarray(ga_order, jnp.int32)]
    col_trans = jnp.pad(col_trans, ((0, 0), (0, 64 - col_count)), constant_values=-1).reshape(1, -1)
    real_col = col_trans >= 0
    at_direct = jnp.where(real_col, (col_trans % NC) * NV + col_trans // NC, -1)
    own_col = real_col & (col_trans // row_count == me_pair)
    at_exch = jnp.where(own_col, col_trans % row_count, -1)

    def pick_cols(at, size, scale):
        hot = at == jnp.arange(size, dtype=jnp.int32)[:, None]
        return jnp.where(hot, scale, 0.0).astype(jnp.bfloat16)

    col_direct, col_exch = pick_cols(at_direct, NT, -1.0), pick_cols(at_exch, row_count, 2.0)

    heard = [[swap(gone[q], "ga", ga, ga_bits[0])] for q in range(points)]
    outs = [None] * points
    exch = None
    for wave in range(2 * points + stages):
        for q in reversed(range(points)):
            stage = wave - 2 * q
            if 1 <= stage < stages:
                columns = (ga >> (stage + 1)) * width
                coded, token = hop_call(keep[q], heard[q], me, stage, columns, after)
                after = [token]
                heard[q].append(swap(coded, "ga", ga, ga_bits[stage]))
                if exch is None:
                    heres = gather_slots(
                        jnp.transpose(behind(trans_here, tokens[1]), (1, 0, 2)), "pair", pair
                    )
                    there = jnp.transpose(behind(trans_there, tokens[1]), (1, 2, 0, 3))
                    exch, token = exchange_call(heres, there, coulomb, after)
                    after = [token]
            elif stage == stages:
                tile, sent, token = tile_call(
                    cons, q, keep[q], heard[q], exch, me, ga_order, pick_rows, col_direct,
                    col_exch, pair, after,
                )
                after = [token]
                for step, bit in enumerate(pair_bits):
                    got = swap(sent, "pair", pair, bit)
                    tile, sent = fold_call(tile, got, me, step + 1 < len(pair_bits))
                tile = tile + swap(sent, "ga", ga, ga_bits[0])
                for bit in ga_bits[1:]:
                    cols = tile.shape[1] // 2
                    tile = tile[:, :cols] + swap(tile[:, cols:], "ga", ga, bit)
                outs[q] = tile[:, :col_count].reshape(2, row_count, col_count)
    return jnp.stack(outs)


def contract_float(left, right):
    high = lax.Precision.HIGHEST
    real_part = jnp.einsum(
        "nkg,mkg->nkm", left[:, :, 0], right[:, :, 0], precision=high
    ) - jnp.einsum("nkg,mkg->nkm", left[:, :, 1], right[:, :, 1], precision=high)
    imag_part = jnp.einsum(
        "nkg,mkg->nkm", left[:, :, 0], right[:, :, 1], precision=high
    ) + jnp.einsum("nkg,mkg->nkm", left[:, :, 1], right[:, :, 0], precision=high)
    return jnp.stack([real_part, imag_part], axis=2)


def times_cols(rows, weights):
    first = jnp.einsum(
        "nkh,kgh->nkg", rows[:, :, 0], weights[:, 0], preferred_element_type=jnp.float32
    ) - jnp.einsum("nkh,kgh->nkg", rows[:, :, 1], weights[:, 1], preferred_element_type=jnp.float32)
    second = jnp.einsum(
        "nkh,kgh->nkg", rows[:, :, 0], weights[:, 1], preferred_element_type=jnp.float32
    ) + jnp.einsum("nkh,kgh->nkg", rows[:, :, 1], weights[:, 0], preferred_element_type=jnp.float32)
    return jnp.stack([first, second], axis=2)


def on_any_device(
    val_density, con_density, screened, coulomb, trans_here, trans_there, shift_map, ordering
):
    con_count = con_density.shape[0]
    points = con_density.shape[1]
    slab_cols = con_density.shape[3]
    blocks = slab_cols // GBLK
    within = (shift_map % GBLK).reshape(points, blocks, GBLK)
    onehot = (
        within[:, :, :, None] == jnp.arange(GBLK, dtype=jnp.int32)[None, None, None, :]
    ).astype(jnp.bfloat16)
    con_blocks = con_density.reshape(con_count, points, 2, blocks, GBLK)
    shifted = (
        jnp.einsum("bkpnh,kngh->bkpng", con_blocks, onehot, preferred_element_type=jnp.float32)
        .astype(jnp.bfloat16)
        .reshape(con_density.shape)
    )
    whole_here = lax.all_gather(trans_here, "pair", axis=0, tiled=True).astype(jnp.float32)
    weighted = trans_there.astype(jnp.float32) * coulomb[None, :, None, :]
    high = lax.Precision.HIGHEST
    exch_real = jnp.einsum(
        "tg,skg->tks", whole_here[:, 0], weighted[:, :, 0], precision=high
    ) - jnp.einsum("tg,skg->tks", whole_here[:, 1], weighted[:, :, 1], precision=high)
    exch_imag = jnp.einsum(
        "tg,skg->tks", whole_here[:, 0], weighted[:, :, 1], precision=high
    ) + jnp.einsum("tg,skg->tks", whole_here[:, 1], weighted[:, :, 0], precision=high)
    exch_part = jnp.stack([exch_real, exch_imag], axis=2)
    whole_con = lax.all_gather(shifted, "ga", axis=0, tiled=True)
    screened_rows = lax.psum_scatter(
        times_cols(whole_con, screened), "pair", scatter_dimension=0, tiled=True
    )
    direct_part = contract_float(
        lax.all_gather(val_density, "pair", axis=0, tiled=True).astype(jnp.float32), screened_rows
    )
    direct_sum, exch_sum = lax.psum((direct_part, exch_part), "ga")
    direct_full, exch_full = (
        lax.all_gather(direct_sum, "pair", axis=3, tiled=True),
        lax.all_gather(exch_sum, "pair", axis=3, tiled=True),
    )
    row_count = NT // lax.axis_size("pair")
    col_count = NT // lax.axis_size("ga")
    row_trans = lax.dynamic_slice_in_dim(ordering, lax.axis_index("pair") * row_count, row_count, 0)
    col_trans = lax.dynamic_slice_in_dim(ordering, lax.axis_index("ga") * col_count, col_count, 0)
    row_pairs = (row_trans // NC)[:, None] * NV + (col_trans // NC)[None, :]
    col_pairs = (row_trans % NC)[:, None] * NC + (col_trans % NC)[None, :]
    picked = direct_full[row_pairs.reshape(-1)]
    col_mask = (
        col_pairs.reshape(-1)[:, None] == jnp.arange(direct_full.shape[3], dtype=jnp.int32)[None, :]
    ).astype(jnp.float32)
    direct_flat = jnp.sum(picked * col_mask[:, None, None, :], axis=3)
    direct_sel = jnp.transpose(direct_flat.reshape(row_count, col_count, points, 2), (2, 3, 0, 1))
    exch_picked = exch_full[row_trans]
    col_hot = (jnp.arange(NT, dtype=jnp.int32)[:, None] == col_trans[None, :]).astype(jnp.float32)
    exch_sel = jnp.einsum("rkpt,tc->kprc", exch_picked, col_hot, precision=high)
    return 2.0 * exch_sel - direct_sel


def solution(mesh):
    in_specs = (
        P("pair", None, None, "ga"),
        P("ga", None, None, "pair"),
        P(None, None, "ga", "pair"),
        P(None, "ga"),
        P("pair", None, "ga"),
        P("pair", None, None, "ga"),
        P(None, "pair"),
        P(),
    )
    out_specs = P(None, None, "pair", "ga")

    def run(*args):
        ga, pair = mesh.shape["ga"], mesh.shape["pair"]
        con_count, h_count = args[1].shape[0], args[1].shape[3]
        suits = (
            ga & (ga - 1) == 0
            and pair & (pair - 1) == 0
            and ga >= 4
            and pair >= 2
            and NT % (pair * GROUP // 2) == 0
            and h_count % (ga * pair * GBLK) == 0
            and con_count % (8 * ga) == 0
            and args[0].shape[0] % (16 * pair) == 0
            and NT % (16 * pair) == 0
            and NT // ga <= 64
        )
        body = on_device if suits else on_any_device
        return jax.shard_map(
            body, mesh=mesh, in_specs=in_specs, out_specs=out_specs, check_vma=False
        )(*args)

    return run
```

```python
import jax
import jax.numpy as jnp
from jax import lax
from jax.experimental import pallas as pl
from jax.experimental.pallas import tpu as pltpu
from jax.sharding import PartitionSpec as P

NV = 16
NC = 24
GBLK = 128
NT = 384

GROUP = 64
EXP_ROWS = 16
STEPS = 128.0
TOP = 32700.0
MAGIC = 1.5 * 2.0**23
NT_DIMS = (((1,), (1,)), ((), ()))
MIB = 1024 * 1024


TOKEN = jax.ShapeDtypeStruct((8, 128), jnp.float32)


def params(mib):
    return pltpu.CompilerParams(vmem_limit_bytes=mib * MIB)


def cost(flops, moved):
    return pl.CostEstimate(flops=int(flops), bytes_accessed=int(moved), transcendentals=0)


def mm(left, right):
    return jnp.dot(left, right, preferred_element_type=jnp.float32)


def mm_nt(left, right):
    return lax.dot_general(left, right, NT_DIMS, preferred_element_type=jnp.float32)


def halves(value):
    high = value.astype(jnp.bfloat16)
    low = (value - high.astype(jnp.float32)).astype(jnp.bfloat16)
    return high, low


def encode(value, out_ref):
    rows, width = value.shape
    groups = rows // GROUP
    parts = value.reshape(groups, GROUP, width)
    largest = jnp.maximum(jnp.max(jnp.abs(parts), axis=1), 1e-30)
    level = jnp.ceil(jnp.log2(largest) * STEPS) + 1.0
    factor = TOP * jnp.exp2(level * (-1.0 / STEPS))
    coded = ((parts * factor[:, None, :] + MAGIC) - MAGIC).astype(jnp.int32)
    out_ref[0:rows, :] = coded.reshape(rows, width).astype(jnp.int16)
    pad = jnp.zeros((EXP_ROWS - groups, width), jnp.int32)
    out_ref[rows : rows + EXP_ROWS, :] = jnp.concatenate(
        [level.astype(jnp.int32), pad], axis=0
    ).astype(jnp.int16)


def decode(ref):
    rows = ref.shape[0] - EXP_ROWS
    width = ref.shape[1]
    groups = rows // GROUP
    level = ref[rows : rows + EXP_ROWS, :].astype(jnp.int32).astype(jnp.float32)[0:groups]
    factor = jnp.exp2(level * (1.0 / STEPS)) * (1.0 / TOP)
    parts = ref[0:rows, :].astype(jnp.int32).astype(jnp.float32).reshape(groups, GROUP, width)
    return (parts * factor[:, None, :]).reshape(rows, width)


def reversed_bits(number, count):
    return sum(((number // (1 << b)) % 2) * (1 << (count - 1 - b)) for b in range(count))


def block_of(me, known, stop, flip):
    number = 0
    for bit in range(known, stop):
        flag = (me // (1 << bit)) % 2
        number = 2 * number + (1 - flag if flip and bit == stop - 1 else flag)
    return number


def shift_kernel(order, me_ref, con_ref, map_ref, stay_ref, go_ref, token_ref):
    slots, _, _, rows, width = stay_ref.shape
    count = len(order).bit_length() - 1
    token_ref[...] = jnp.zeros_like(token_ref)
    for which, out_ref in enumerate((stay_ref, go_ref)):
        for slot in range(slots):
            dest = jnp.bitwise_xor(me_ref[0], order[which * slots + slot])
            first = reversed_bits(dest, count) * width
            for block in range(width // GBLK):
                cols = pl.ds(pl.multiple_of(first + block * GBLK, GBLK), GBLK)
                within = jnp.bitwise_and(map_ref[0, 0:1, cols], GBLK - 1)
                within = jnp.broadcast_to(within, (rows, GBLK))
                for part in range(2):
                    values = con_ref[0, part, :, cols].astype(jnp.float32)
                    moved = jnp.take_along_axis(values, within, axis=1)
                    out_ref[slot, 0, part, :, block * GBLK : (block + 1) * GBLK] = moved.astype(
                        jnp.bfloat16
                    )


def shift_call(con, shift_map, me, order, width):
    points, _, rows, slab = con.shape
    slots = len(order) // 2
    grid_spec = pltpu.PrefetchScalarGridSpec(
        num_scalar_prefetch=1,
        grid=(points,),
        in_specs=[
            pl.BlockSpec((1, 2, rows, slab), lambda q, me: (q, 0, 0, 0)),
            pl.BlockSpec((1, 1, slab), lambda q, me: (q, 0, 0)),
        ],
        out_specs=[pl.BlockSpec((slots, 1, 2, rows, width), lambda q, me: (0, q, 0, 0, 0))] * 2
        + [pl.BlockSpec(TOKEN.shape, lambda q, me: (0, 0))],
    )
    return pl.pallas_call(
        lambda *refs: shift_kernel(order, *refs),
        grid_spec=grid_spec,
        out_shape=[jax.ShapeDtypeStruct((slots, points, 2, rows, width), jnp.bfloat16)] * 2
        + [TOKEN],
        compiler_params=params(16),
        cost_estimate=cost(8 * con.size, 4 * con.size),
    )(me, con, shift_map.reshape(points, 1, slab))


def x_kernel(slots, waits, me_ref, *refs):
    val_refs, weight_ref = refs[:slots], refs[slots]
    go_ref, keep_ref, token_ref, left_ref = refs[slots + 1 + waits :]
    _, _, rows, depth = val_refs[0].shape
    half = slots * rows
    token_ref[...] = jnp.zeros_like(token_ref)
    step = pl.program_id(0)
    halfway = pl.num_programs(0) // 2

    @pl.when(step == 0)
    def _():
        for slot in range(slots):
            real, imag = val_refs[slot][0, 0], val_refs[slot][0, 1]
            top = slice(slot * rows, (slot + 1) * rows)
            low = slice(half + slot * rows, half + (slot + 1) * rows)
            left_ref[top, 0:depth] = real
            left_ref[top, depth : 2 * depth] = -imag
            left_ref[low, 0:depth] = imag
            left_ref[low, depth : 2 * depth] = real

    weight = weight_ref[0].reshape(2 * depth, weight_ref.shape[3])

    @pl.when(step < halfway)
    def _():
        encode(mm(left_ref[...], weight), go_ref)

    @pl.when(step >= halfway)
    def _():
        keep_ref[...] = mm(left_ref[...], weight)


def x_call(vals, screened, place, point, me, steps, after):
    slots = len(vals)
    _, _, rows, depth = vals[0].shape
    height = 2 * slots * rows
    columns = screened.shape[3] // 2
    half = steps // 2
    width = columns // half
    grid_spec = pltpu.PrefetchScalarGridSpec(
        num_scalar_prefetch=1,
        grid=(steps,),
        in_specs=[
            pl.BlockSpec((1, 2, rows, depth), lambda j, me: (place, 0, 0, 0)) for _ in vals
        ]
        + [
            pl.BlockSpec(
                (1, 2, depth, width),
                lambda j, me: (point, 0, 0, ((me[0] + 1 + j // half) % 2) * half + j % half),
            )
        ]
        + [pl.BlockSpec(memory_space=pl.ANY) for _ in after],
        out_specs=[
            pl.BlockSpec((height + EXP_ROWS, width), lambda j, me: (0, jnp.minimum(j, half - 1))),
            pl.BlockSpec((height, width), lambda j, me: (0, jnp.maximum(j - half, 0))),
            pl.BlockSpec(TOKEN.shape, lambda j, me: (0, 0)),
        ],
        scratch_shapes=[pltpu.VMEM((height, 2 * depth), jnp.bfloat16)],
    )
    return pl.pallas_call(
        lambda *refs: x_kernel(slots, len(after), *refs),
        grid_spec=grid_spec,
        out_shape=[
            jax.ShapeDtypeStruct((height + EXP_ROWS, columns), jnp.int16),
            jax.ShapeDtypeStruct((height, columns), jnp.float32),
            TOKEN,
        ],
        compiler_params=params(42),
        cost_estimate=cost(
            2 * height * 2 * depth * 2 * columns, 8 * depth * columns + 6 * height * columns
        ),
    )(me, *vals, screened, *after)


def hop_kernel(heard, me_ref, keep_ref, *refs):
    total = keep_ref[...]
    for ref in refs[:heard]:
        total = total + decode(ref)
    out_ref, token_ref = refs[-2:]
    encode(total, out_ref)
    token_ref[...] = jnp.zeros_like(token_ref)


def hop_call(keep, others, me, stage, width, after):
    height, tall = keep.shape[0], others[0].shape[0]
    steps = width // 128

    def at(known):
        return lambda i, me: (0, block_of(me[0], known, stage + 1, True) * steps + i)

    grid_spec = pltpu.PrefetchScalarGridSpec(
        num_scalar_prefetch=1,
        grid=(steps,),
        in_specs=[pl.BlockSpec((height, 128), at(1))]
        + [pl.BlockSpec((tall, 128), at(n + 1)) for n in range(len(others))]
        + [pl.BlockSpec(memory_space=pl.ANY) for _ in after],
        out_specs=[
            pl.BlockSpec((tall, 128), lambda i, me: (0, i)),
            pl.BlockSpec(TOKEN.shape, lambda i, me: (0, 0)),
        ],
    )
    return pl.pallas_call(
        lambda *refs: hop_kernel(len(others), *refs),
        grid_spec=grid_spec,
        out_shape=[jax.ShapeDtypeStruct((tall, width), jnp.int16), TOKEN],
        compiler_params=params(16),
        cost_estimate=cost(20 * height * width, 8 * height * width),
    )(me, keep, *others, *after)


def fold_kernel(*refs):
    own_ref, heard_ref, keep_ref, go_ref = refs
    total = own_ref[...] + decode(heard_ref)
    rows = keep_ref.shape[0]
    keep_ref[...] = total[:rows]
    encode(total[rows:], go_ref)


def fold_call(own, heard):
    rows, cols = own.shape
    shapes = [
        jax.ShapeDtypeStruct((rows // 2, cols), jnp.float32),
        jax.ShapeDtypeStruct((rows // 2 + EXP_ROWS, cols), jnp.int16),
    ]
    return pl.pallas_call(
        fold_kernel,
        out_shape=shapes,
        compiler_params=params(16),
        cost_estimate=cost(20 * own.size, 10 * own.size),
    )(own, heard)


def pack_kernel(own_ref, *refs):
    heard_refs, out_ref = refs[:-1], refs[-1]
    total = own_ref[...]
    for ref in heard_refs:
        total = total + decode(ref)
    rows = out_ref.shape[1]
    first = lax.broadcasted_iota(jnp.int32, (rows, 128), 1) < 64
    for block in range(out_ref.shape[0] // 2):
        cols = slice(block * 128, (block + 1) * 128)
        real, imag = total[:rows, cols], total[rows:, cols]
        out_ref[2 * block] = jnp.where(first, real, pltpu.roll(imag, 64, 1))
        out_ref[2 * block + 1] = jnp.where(first, pltpu.roll(real, 64, 1), imag)


def pack_call(own, heard):
    rows, cols = own.shape
    return pl.pallas_call(
        pack_kernel,
        out_shape=jax.ShapeDtypeStruct((cols // 64, rows // 2, 128), jnp.float32),
        compiler_params=params(16),
        cost_estimate=cost(20 * own.size, 10 * own.size),
    )(own, *heard)


def exchange_kernel(slots, waits, *refs):
    here_refs, (there_ref, coulomb_ref) = refs[:slots], refs[slots : slots + 2]
    out_ref, token_ref, left_ref = refs[slots + 2 + waits :]
    _, rows, depth = here_refs[0].shape
    token_ref[...] = jnp.zeros_like(token_ref)

    @pl.when(pl.program_id(0) == 0)
    def _():
        for slot in range(slots):
            for part in range(2):
                left_ref[
                    slot * rows : (slot + 1) * rows, part * depth : (part + 1) * depth
                ] = here_refs[slot][part]

    factor = coulomb_ref[0]
    real = there_ref[0, 0].astype(jnp.float32) * factor
    imag = there_ref[0, 1].astype(jnp.float32) * factor
    right = jnp.concatenate(
        [jnp.concatenate([real, -imag], axis=1), jnp.concatenate([imag, real], axis=1)], axis=0
    )
    high, low = halves(right)
    left = left_ref[...]
    both = mm_nt(left, high) + mm_nt(left, low)
    cols = both.shape[1] // 2
    for part in range(2):
        out_ref[0, part] = both[:, part * cols : (part + 1) * cols]


def exchange_call(heres, there, coulomb, after):
    slots, rows = len(heres), heres[0].shape[1]
    points, _, cols, depth = there.shape
    height = slots * rows
    return pl.pallas_call(
        lambda *refs: exchange_kernel(slots, len(after), *refs),
        grid=(points,),
        in_specs=[pl.BlockSpec(h.shape, lambda q: (0, 0, 0)) for h in heres]
        + [
            pl.BlockSpec((1, 2, cols, depth), lambda q: (q, 0, 0, 0)),
            pl.BlockSpec((1, 1, depth), lambda q: (q, 0, 0)),
        ]
        + [pl.BlockSpec(memory_space=pl.ANY) for _ in after],
        out_specs=[
            pl.BlockSpec((1, 2, height, cols), lambda q: (q, 0, 0, 0)),
            pl.BlockSpec(TOKEN.shape, lambda q: (0, 0)),
        ],
        out_shape=[jax.ShapeDtypeStruct((points, 2, height, cols), jnp.float32), TOKEN],
        scratch_shapes=[pltpu.VMEM((height, 2 * depth), jnp.bfloat16)],
        compiler_params=params(16),
        cost_estimate=cost(2 * points * height * 2 * cols * 2 * depth * 2, 8 * points * cols * depth),
    )(*heres, there, coulomb.reshape(points, 1, depth), *after)


def tile_kernel(order, heard, chunks, waits, me_ref, *refs):
    slots = len(order)
    con_refs, keep_ref = refs[:slots], refs[slots]
    heard_refs = refs[slots + 1 : slots + 1 + heard]
    exch_ref, row_ref, col_direct_ref, col_exch_ref = refs[slots + 1 + heard : slots + 5 + heard]
    keep_out, *go_outs, token_ref, con_all, direct_ref, natural_ref, sums_ref = refs[
        slots + 5 + heard + waits :
    ]
    token_ref[...] = jnp.zeros_like(token_ref)
    total = keep_ref[...]
    for ref in heard_refs:
        total = total + decode(ref)
    pairs, width = total.shape[0] // 2, total.shape[1]
    rows = con_refs[0].shape[3]
    pitch = con_all.shape[0] // slots
    for slot in range(slots):
        for part in range(2):
            con_all[
                slot * pitch : slot * pitch + rows, part * width : (part + 1) * width
            ] = con_refs[slot][0, 0, part]
    real, imag = total[:pairs], total[pairs:]
    right = jnp.concatenate(
        [jnp.concatenate([real, -imag], axis=1), jnp.concatenate([imag, real], axis=1)], axis=0
    )
    high, low = halves(right)
    left = con_all[...]
    direct = mm_nt(left, high) + mm_nt(left, low)
    lanes = direct_ref.shape[0]
    for slot in range(slots):
        start = pl.multiple_of(jnp.bitwise_xor(me_ref[0], order[slot]) * rows, 8)
        for lane in range(lanes):
            direct_ref[lane, pl.ds(start, rows), :] = direct[
                slot * pitch : slot * pitch + rows, lane * 128 : (lane + 1) * 128
            ]
    group = 128 // NV
    place = lax.broadcasted_iota(jnp.int32, (NC, 128), 1) // NV
    per_part = lanes // 2
    for part in range(2):
        for chunk in range(NC // group):
            for band in range(NV):
                block = jnp.zeros((NC, 128), jnp.float32)
                for step in range(group):
                    e = chunk * group + step
                    piece = direct_ref[part * per_part + band // group, pl.ds(e, NC, stride=NC), :]
                    turn = (NV * (step - band)) % 128
                    if turn:
                        piece = pltpu.roll(piece, turn, 1)
                    block = jnp.where(place == step, piece, block)
                natural_ref[
                    part, band * NC : (band + 1) * NC, chunk * 128 : (chunk + 1) * 128
                ] = block
    pick_rows = row_ref[...]
    count = NT // chunks
    for part in range(2):
        result = None
        for source, pick_cols in (
            (natural_ref[part], col_direct_ref),
            (exch_ref[0, part], col_exch_ref),
        ):
            for piece in halves(source):
                moved = mm(pick_rows, piece).astype(jnp.bfloat16)
                term = mm(moved, pick_cols[...])
                result = term if result is None else result + term
        for chunk in range(chunks):
            at = (2 * chunk + part) * count
            sums_ref[at : at + count, :] = result[chunk * count : (chunk + 1) * count]
    stays = keep_out.shape[0]
    keep_out[...] = sums_ref[0:stays, :]
    at = stays
    for out_ref in go_outs:
        rows = out_ref.shape[0] - EXP_ROWS
        encode(sums_ref[at : at + rows, :], out_ref)
        at += rows


def tile_call(
    cons, point, keep, heard, exch, me, order, pick_rows, col_direct, col_exch, chunks, after, direct
):
    slots = len(cons)
    _, _, _, rows, width = cons[0][0].shape
    height, tall = keep.shape[0], heard[0].shape[0]
    pitch = -(-rows // 16) * 16
    out_cols = col_direct.shape[1]
    stages = len(heard)
    whole = lambda a: pl.BlockSpec(a.shape, lambda i, me: (0,) * len(a.shape))
    each, others = (2 * NT // chunks, chunks - 1) if direct else (NT, 1)
    shapes = [jax.ShapeDtypeStruct((each, out_cols), jnp.float32)]
    shapes += [jax.ShapeDtypeStruct((each + EXP_ROWS, out_cols), jnp.int16)] * others + [TOKEN]

    def at(known):
        return lambda i, me: (0, block_of(me[0], known, stages, False))

    grid_spec = pltpu.PrefetchScalarGridSpec(
        num_scalar_prefetch=1,
        grid=(1,),
        in_specs=[
            pl.BlockSpec((1, 1, 2, rows, width), lambda i, me, place=place: (place, point, 0, 0, 0))
            for _, place in cons
        ]
        + [pl.BlockSpec((height, width), at(1))]
        + [pl.BlockSpec((tall, width), at(n + 1)) for n in range(stages)]
        + [
            pl.BlockSpec((1,) + exch.shape[1:], lambda i, me: (point, 0, 0, 0)),
            whole(pick_rows),
            whole(col_direct),
            whole(col_exch),
        ]
        + [pl.BlockSpec(memory_space=pl.ANY) for _ in after],
        out_specs=[whole(a) for a in shapes],
        scratch_shapes=[
            pltpu.VMEM((slots * pitch, 2 * width), jnp.bfloat16),
            pltpu.VMEM((height // 128, NC * NC, 128), jnp.float32),
            pltpu.VMEM((2, NT, NT), jnp.float32),
            pltpu.VMEM((2 * NT, out_cols), jnp.float32),
        ],
    )
    return pl.pallas_call(
        lambda *refs: tile_kernel(order, stages, chunks, len(after), *refs),
        grid_spec=grid_spec,
        out_shape=shapes,
        compiler_params=params(24),
        cost_estimate=cost(2.8e9, 8e6),
    )(me, *[c for c, _ in cons], keep, *heard, exch, pick_rows, col_direct, col_exch, *after)


def swap(value, axis, size, bit):
    return lax.ppermute(value, axis, [(i, i ^ bit) for i in range(size)])


def gather_slots(value, axis, size, token=None):
    found = {0: value}
    bit = size // 2
    while bit:
        for known in sorted(found):
            ready = found[known] if token is None or not known else behind(found[known], token)
            found[known ^ bit] = swap(ready, axis, size, bit)
        bit //= 2
    return [found[r] for r in range(size)]


def halving_order(bits):
    order = [0]
    for bit in reversed(bits):
        order = order + [o ^ bit for o in order]
    return order


def behind(value, token):
    return lax.optimization_barrier((value, token))[0]


def on_device(*args):
    (val_density, con_density, screened, coulomb, trans_here, trans_there, shift_map, ordering) = args
    ga, pair = lax.axis_size("ga"), lax.axis_size("pair")
    points = con_density.shape[1]
    slab = con_density.shape[3]
    width = slab // ga
    me_ga, me_pair = lax.axis_index("ga"), lax.axis_index("pair")
    me = me_ga.astype(jnp.int32).reshape(1)
    ga_bits = [1 << b for b in range(ga.bit_length() - 1)]
    pair_bits = [1 << b for b in range(pair.bit_length() - 1)]
    ga_order = halving_order(ga_bits)
    stages, half = len(ga_bits), ga // 2

    first = gather_slots(jnp.transpose(val_density[:, :1], (1, 2, 0, 3)), "pair", pair)

    con = jnp.transpose(con_density, (1, 2, 0, 3))
    stay, go, token = shift_call(con, shift_map, me, ga_order, width)
    from_near = swap(go, "ga", ga, ga_bits[0])
    others = behind(val_density[:, 1:], first[pair // 2])
    others = gather_slots(jnp.transpose(others, (1, 2, 0, 3)), "pair", pair)

    gone, keep, tokens = [], [], [token]
    for q in range(points):
        vals, place = (first, 0) if q == 0 else (others, q - 1)
        coded, own, token = x_call(vals, screened, place, q, me, 4, tokens[-1:])
        tokens.append(token)
        gone.append(coded)
        keep.append(own)
    after = tokens[-1:]

    cons = {}
    for p, slot in enumerate(ga_order):
        cons[slot] = (stay, p) if p < half else (go, p - half)
    for step, bit in enumerate(ga_bits[:1] + ga_bits[:0:-1]):
        moving = [slot for slot in ga_order if slot & bit]
        if step == 0:
            got = from_near
        else:
            got = swap(jnp.stack([cons[slot][0][cons[slot][1]] for slot in moving]), "ga", ga, bit)
        if step + 1 < stages:
            got = behind(got, tokens[min(2 * step + 1, points)])
        for place, slot in enumerate(moving):
            cons[slot] = (got, place)
    cons = [cons[slot] for slot in ga_order]

    row_count, col_count = NT // pair, NT // ga
    row_slots = jnp.asarray(halving_order(pair_bits), jnp.int32)
    row_trans = ordering.reshape(pair, row_count)[me_pair ^ row_slots].reshape(-1)
    at_row = ((row_trans // row_count) ^ me_pair) * row_count + row_trans % row_count
    pick_rows = (at_row[:, None] == jnp.arange(NT, dtype=jnp.int32)[None, :]).astype(jnp.bfloat16)
    col_trans = ordering.reshape(ga, col_count)[me_ga ^ jnp.asarray(ga_order, jnp.int32)]
    col_trans = jnp.pad(col_trans, ((0, 0), (0, 64 - col_count)), constant_values=-1).reshape(1, -1)
    real_col = col_trans >= 0
    at_direct = jnp.where(real_col, (col_trans % NC) * NV + col_trans // NC, -1)
    own_col = real_col & (col_trans // row_count == me_pair)
    at_exch = jnp.where(own_col, col_trans % row_count, -1)

    def pick_cols(at, size, scale):
        hot = at == jnp.arange(size, dtype=jnp.int32)[:, None]
        return jnp.where(hot, scale, 0.0).astype(jnp.bfloat16)

    col_direct, col_exch = pick_cols(at_direct, NT, -1.0), pick_cols(at_exch, row_count, 2.0)

    heard = [[swap(gone[q], "ga", ga, ga_bits[0])] for q in range(points)]
    packed = [None] * points
    exch = None
    for wave in range(2 * points + stages):
        for q in reversed(range(points)):
            stage = wave - 2 * q
            if 1 <= stage < stages:
                columns = (ga >> (stage + 1)) * width
                coded, token = hop_call(keep[q], heard[q], me, stage, columns, after)
                after = [token]
                heard[q].append(swap(coded, "ga", ga, ga_bits[stage]))
                if exch is None:
                    here = jnp.transpose(behind(trans_here, tokens[1]), (1, 0, 2))
                    heres = gather_slots(here, "pair", pair, tokens[-1])
                    there = jnp.transpose(behind(trans_there, tokens[1]), (1, 2, 0, 3))
                    exch, token = exchange_call(heres, there, coulomb, after)
                    after = [token]
            elif stage == stages:
                last = q == points - 1
                tile, *sent, token = tile_call(
                    cons, q, keep[q], heard[q], exch, me, ga_order, pick_rows, col_direct,
                    col_exch, pair, after, last,
                )
                after = [token]
                if last:
                    slots = halving_order(pair_bits)[1:]
                    got = [swap(part, "pair", pair, slot) for slot, part in zip(slots, sent)]
                    packed[q] = pack_call(tile, got)
                    continue
                got = swap(sent[0], "pair", pair, pair_bits[0])
                for bit in pair_bits[1:]:
                    tile, sent = fold_call(tile, got)
                    got = swap(sent, "pair", pair, bit)
                packed[q] = pack_call(tile, [got])
    early = jnp.stack(packed[:-1], axis=1)
    for bit in ga_bits:
        size = early.shape[0] // 2
        early = early[:size] + swap(early[size:], "ga", ga, bit)
    late = packed[-1]
    total = late[0]
    for place, slot in enumerate(ga_order[1:]):
        total = total + swap(late[place + 1], "ga", ga, slot)
    out = jnp.concatenate([early[0], total[None]])
    out = out.reshape(points, row_count, 2, 64)[..., :col_count]
    return jnp.transpose(out, (0, 2, 1, 3))


def contract_float(left, right):
    high = lax.Precision.HIGHEST
    real_part = jnp.einsum(
        "nkg,mkg->nkm", left[:, :, 0], right[:, :, 0], precision=high
    ) - jnp.einsum("nkg,mkg->nkm", left[:, :, 1], right[:, :, 1], precision=high)
    imag_part = jnp.einsum(
        "nkg,mkg->nkm", left[:, :, 0], right[:, :, 1], precision=high
    ) + jnp.einsum("nkg,mkg->nkm", left[:, :, 1], right[:, :, 0], precision=high)
    return jnp.stack([real_part, imag_part], axis=2)


def times_cols(rows, weights):
    first = jnp.einsum(
        "nkh,kgh->nkg", rows[:, :, 0], weights[:, 0], preferred_element_type=jnp.float32
    ) - jnp.einsum("nkh,kgh->nkg", rows[:, :, 1], weights[:, 1], preferred_element_type=jnp.float32)
    second = jnp.einsum(
        "nkh,kgh->nkg", rows[:, :, 0], weights[:, 1], preferred_element_type=jnp.float32
    ) + jnp.einsum("nkh,kgh->nkg", rows[:, :, 1], weights[:, 0], preferred_element_type=jnp.float32)
    return jnp.stack([first, second], axis=2)


def on_any_device(
    val_density, con_density, screened, coulomb, trans_here, trans_there, shift_map, ordering
):
    con_count = con_density.shape[0]
    points = con_density.shape[1]
    slab_cols = con_density.shape[3]
    blocks = slab_cols // GBLK
    within = (shift_map % GBLK).reshape(points, blocks, GBLK)
    onehot = (
        within[:, :, :, None] == jnp.arange(GBLK, dtype=jnp.int32)[None, None, None, :]
    ).astype(jnp.bfloat16)
    con_blocks = con_density.reshape(con_count, points, 2, blocks, GBLK)
    shifted = (
        jnp.einsum("bkpnh,kngh->bkpng", con_blocks, onehot, preferred_element_type=jnp.float32)
        .astype(jnp.bfloat16)
        .reshape(con_density.shape)
    )
    whole_here = lax.all_gather(trans_here, "pair", axis=0, tiled=True).astype(jnp.float32)
    weighted = trans_there.astype(jnp.float32) * coulomb[None, :, None, :]
    high = lax.Precision.HIGHEST
    exch_real = jnp.einsum(
        "tg,skg->tks", whole_here[:, 0], weighted[:, :, 0], precision=high
    ) - jnp.einsum("tg,skg->tks", whole_here[:, 1], weighted[:, :, 1], precision=high)
    exch_imag = jnp.einsum(
        "tg,skg->tks", whole_here[:, 0], weighted[:, :, 1], precision=high
    ) + jnp.einsum("tg,skg->tks", whole_here[:, 1], weighted[:, :, 0], precision=high)
    exch_part = jnp.stack([exch_real, exch_imag], axis=2)
    whole_con = lax.all_gather(shifted, "ga", axis=0, tiled=True)
    screened_rows = lax.psum_scatter(
        times_cols(whole_con, screened), "pair", scatter_dimension=0, tiled=True
    )
    direct_part = contract_float(
        lax.all_gather(val_density, "pair", axis=0, tiled=True).astype(jnp.float32), screened_rows
    )
    direct_sum, exch_sum = lax.psum((direct_part, exch_part), "ga")
    direct_full, exch_full = (
        lax.all_gather(direct_sum, "pair", axis=3, tiled=True),
        lax.all_gather(exch_sum, "pair", axis=3, tiled=True),
    )
    row_count = NT // lax.axis_size("pair")
    col_count = NT // lax.axis_size("ga")
    row_trans = lax.dynamic_slice_in_dim(ordering, lax.axis_index("pair") * row_count, row_count, 0)
    col_trans = lax.dynamic_slice_in_dim(ordering, lax.axis_index("ga") * col_count, col_count, 0)
    row_pairs = (row_trans // NC)[:, None] * NV + (col_trans // NC)[None, :]
    col_pairs = (row_trans % NC)[:, None] * NC + (col_trans % NC)[None, :]
    picked = direct_full[row_pairs.reshape(-1)]
    col_mask = (
        col_pairs.reshape(-1)[:, None] == jnp.arange(direct_full.shape[3], dtype=jnp.int32)[None, :]
    ).astype(jnp.float32)
    direct_flat = jnp.sum(picked * col_mask[:, None, None, :], axis=3)
    direct_sel = jnp.transpose(direct_flat.reshape(row_count, col_count, points, 2), (2, 3, 0, 1))
    exch_picked = exch_full[row_trans]
    col_hot = (jnp.arange(NT, dtype=jnp.int32)[:, None] == col_trans[None, :]).astype(jnp.float32)
    exch_sel = jnp.einsum("rkpt,tc->kprc", exch_picked, col_hot, precision=high)
    return 2.0 * exch_sel - direct_sel


def solution(mesh):
    in_specs = (
        P("pair", None, None, "ga"),
        P("ga", None, None, "pair"),
        P(None, None, "ga", "pair"),
        P(None, "ga"),
        P("pair", None, "ga"),
        P("pair", None, None, "ga"),
        P(None, "pair"),
        P(),
    )
    out_specs = P(None, None, "pair", "ga")

    def run(*args):
        ga, pair = mesh.shape["ga"], mesh.shape["pair"]
        con_count, h_count = args[1].shape[0], args[1].shape[3]
        suits = (
            ga & (ga - 1) == 0
            and pair & (pair - 1) == 0
            and ga >= 4
            and pair >= 2
            and NT % (pair * GROUP // 2) == 0
            and h_count % (ga * pair * GBLK) == 0
            and con_count % (8 * ga) == 0
            and args[0].shape[0] % (16 * pair) == 0
            and NT % (16 * pair) == 0
            and NT // ga <= 64
        )
        body = on_device if suits else on_any_device
        return jax.shard_map(
            body, mesh=mesh, in_specs=in_specs, out_specs=out_specs, check_vma=False
        )(*args)

    return run
```

```python
import jax
import jax.numpy as jnp
from jax import lax
from jax.experimental import pallas as pl
from jax.experimental.pallas import tpu as pltpu
from jax.sharding import PartitionSpec as P

NV = 16
NC = 24
GBLK = 128
NT = 384

GROUP = 64
EXP_ROWS = 16
STEPS = 128.0
TOP = 32700.0
MAGIC = 1.5 * 2.0**23
NT_DIMS = (((1,), (1,)), ((), ()))
VMEM = 40 * 1024 * 1024


TOKEN = jax.ShapeDtypeStruct((8, 128), jnp.float32)


def params():
    return pltpu.CompilerParams(vmem_limit_bytes=VMEM)


def cost(flops, moved):
    return pl.CostEstimate(flops=int(flops) // 64, bytes_accessed=int(moved) // 64, transcendentals=0)


def mm(left, right):
    return jnp.dot(left, right, preferred_element_type=jnp.float32)


def mm_nt(left, right):
    return lax.dot_general(left, right, NT_DIMS, preferred_element_type=jnp.float32)


def halves(value):
    high = value.astype(jnp.bfloat16)
    low = (value - high.astype(jnp.float32)).astype(jnp.bfloat16)
    return high, low


def encode(value, out_ref):
    rows, width = value.shape
    groups = rows // GROUP
    parts = value.reshape(groups, GROUP, width)
    largest = jnp.maximum(jnp.max(jnp.abs(parts), axis=1), 1e-30)
    level = jnp.ceil(jnp.log2(largest) * STEPS) + 1.0
    factor = TOP * jnp.exp2(level * (-1.0 / STEPS))
    coded = ((parts * factor[:, None, :] + MAGIC) - MAGIC).astype(jnp.int32)
    out_ref[0:rows, :] = coded.reshape(rows, width).astype(jnp.int16)
    pad = jnp.zeros((EXP_ROWS - groups, width), jnp.int32)
    out_ref[rows : rows + EXP_ROWS, :] = jnp.concatenate(
        [level.astype(jnp.int32), pad], axis=0
    ).astype(jnp.int16)


def decode(ref):
    rows = ref.shape[0] - EXP_ROWS
    width = ref.shape[1]
    groups = rows // GROUP
    level = ref[rows : rows + EXP_ROWS, :].astype(jnp.int32).astype(jnp.float32)[0:groups]
    factor = jnp.exp2(level * (1.0 / STEPS)) * (1.0 / TOP)
    parts = ref[0:rows, :].astype(jnp.int32).astype(jnp.float32).reshape(groups, GROUP, width)
    return (parts * factor[:, None, :]).reshape(rows, width)


def reversed_bits(number, count):
    return sum(((number // (1 << b)) % 2) * (1 << (count - 1 - b)) for b in range(count))


def block_of(me, known, stop, flip):
    number = 0
    for bit in range(known, stop):
        flag = (me // (1 << bit)) % 2
        number = 2 * number + (1 - flag if flip and bit == stop - 1 else flag)
    return number


def shift_kernel(order, me_ref, con_ref, map_ref, *refs):
    *stay_refs, go_ref, token_ref = refs
    half, _, _, rows, width = go_ref.shape
    count = len(order).bit_length() - 1
    token_ref[...] = jnp.zeros_like(token_ref)
    for p, slot in enumerate(order):
        out_ref = stay_refs[p].at[0] if p < half else go_ref.at[p - half]
        first = reversed_bits(jnp.bitwise_xor(me_ref[0], slot), count) * width
        for block in range(width // GBLK):
            cols = pl.ds(pl.multiple_of(first + block * GBLK, GBLK), GBLK)
            within = jnp.bitwise_and(map_ref[0, 0:1, cols], GBLK - 1)
            within = jnp.broadcast_to(within, (rows, GBLK))
            for part in range(2):
                values = con_ref[0, part, :, cols].astype(jnp.float32)
                moved = jnp.take_along_axis(values, within, axis=1)
                out_ref[0, part, :, block * GBLK : (block + 1) * GBLK] = moved.astype(jnp.bfloat16)


def shift_call(con, shift_map, me, order, width):
    points, _, rows, slab = con.shape
    half = len(order) // 2
    counts = [1] * half + [half]
    grid_spec = pltpu.PrefetchScalarGridSpec(
        num_scalar_prefetch=1,
        grid=(points,),
        in_specs=[
            pl.BlockSpec((1, 2, rows, slab), lambda q, me: (q, 0, 0, 0)),
            pl.BlockSpec((1, 1, slab), lambda q, me: (q, 0, 0)),
        ],
        out_specs=[
            pl.BlockSpec((n, 1, 2, rows, width), lambda q, me: (0, q, 0, 0, 0)) for n in counts
        ]
        + [pl.BlockSpec(TOKEN.shape, lambda q, me: (0, 0))],
    )
    return pl.pallas_call(
        lambda *refs: shift_kernel(order, *refs),
        grid_spec=grid_spec,
        out_shape=[
            jax.ShapeDtypeStruct((n, points, 2, rows, width), jnp.bfloat16) for n in counts
        ]
        + [TOKEN],
        compiler_params=params(),
        cost_estimate=cost(8 * con.size, 4 * con.size),
    )(me, con, shift_map.reshape(points, 1, slab))


def x_kernel(slots, waits, me_ref, *refs):
    val_refs, weight_ref = refs[:slots], refs[slots]
    go_ref, keep_ref, token_ref, left_ref = refs[slots + 1 + waits :]
    _, _, _, rows, depth = val_refs[0].shape
    half = slots * rows
    token_ref[...] = jnp.zeros_like(token_ref)
    step = pl.program_id(0)
    halfway = pl.num_programs(0) // 2

    @pl.when(step == 0)
    def _():
        for slot in range(slots):
            real, imag = val_refs[slot][0, 0, 0], val_refs[slot][0, 0, 1]
            top = slice(slot * rows, (slot + 1) * rows)
            low = slice(half + slot * rows, half + (slot + 1) * rows)
            left_ref[top, 0:depth] = real
            left_ref[top, depth : 2 * depth] = -imag
            left_ref[low, 0:depth] = imag
            left_ref[low, depth : 2 * depth] = real

    weight = weight_ref[0].reshape(2 * depth, weight_ref.shape[3])

    @pl.when(step < halfway)
    def _():
        encode(mm(left_ref[...], weight), go_ref)

    @pl.when(step >= halfway)
    def _():
        keep_ref[...] = mm(left_ref[...], weight)


def x_call(vals, screened, place, point, me, steps, after):
    slots = len(vals)
    _, _, _, rows, depth = vals[0][0].shape
    height = 2 * slots * rows
    columns = screened.shape[3] // 2
    half = steps // 2
    width = columns // half
    grid_spec = pltpu.PrefetchScalarGridSpec(
        num_scalar_prefetch=1,
        grid=(steps,),
        in_specs=[
            pl.BlockSpec((1, 1, 2, rows, depth), lambda j, me, slot=slot: (slot, place, 0, 0, 0))
            for _, slot in vals
        ]
        + [
            pl.BlockSpec(
                (1, 2, depth, width),
                lambda j, me: (point, 0, 0, ((me[0] + 1 + j // half) % 2) * half + j % half),
            )
        ]
        + [pl.BlockSpec(memory_space=pl.ANY) for _ in after],
        out_specs=[
            pl.BlockSpec((height + EXP_ROWS, width), lambda j, me: (0, jnp.minimum(j, half - 1))),
            pl.BlockSpec((height, width), lambda j, me: (0, jnp.maximum(j - half, 0))),
            pl.BlockSpec(TOKEN.shape, lambda j, me: (0, 0)),
        ],
        scratch_shapes=[pltpu.VMEM((height, 2 * depth), jnp.bfloat16)],
    )
    return pl.pallas_call(
        lambda *refs: x_kernel(slots, len(after), *refs),
        grid_spec=grid_spec,
        out_shape=[
            jax.ShapeDtypeStruct((height + EXP_ROWS, columns), jnp.int16),
            jax.ShapeDtypeStruct((height, columns), jnp.float32),
            TOKEN,
        ],
        compiler_params=params(),
        cost_estimate=cost(
            2 * height * 2 * depth * 2 * columns, 8 * depth * columns + 6 * height * columns
        ),
    )(me, *[v for v, _ in vals], screened, *after)


def hop_kernel(heard, me_ref, keep_ref, *refs):
    total = keep_ref[...]
    for ref in refs[:heard]:
        total = total + decode(ref)
    out_ref, token_ref = refs[-2:]
    encode(total, out_ref)
    token_ref[...] = jnp.zeros_like(token_ref)


def hop_call(keep, others, me, stage, width, after):
    height, tall = keep.shape[0], others[0].shape[0]
    steps = width // 128

    def at(known):
        return lambda i, me: (0, block_of(me[0], known, stage + 1, True) * steps + i)

    grid_spec = pltpu.PrefetchScalarGridSpec(
        num_scalar_prefetch=1,
        grid=(steps,),
        in_specs=[pl.BlockSpec((height, 128), at(1))]
        + [pl.BlockSpec((tall, 128), at(n + 1)) for n in range(len(others))]
        + [pl.BlockSpec(memory_space=pl.ANY) for _ in after],
        out_specs=[
            pl.BlockSpec((tall, 128), lambda i, me: (0, i)),
            pl.BlockSpec(TOKEN.shape, lambda i, me: (0, 0)),
        ],
    )
    return pl.pallas_call(
        lambda *refs: hop_kernel(len(others), *refs),
        grid_spec=grid_spec,
        out_shape=[jax.ShapeDtypeStruct((tall, width), jnp.int16), TOKEN],
        compiler_params=params(),
        cost_estimate=cost(20 * height * width, 8 * height * width),
    )(me, keep, *others, *after)


def fold_kernel(own_ref, heard_ref, keep_ref, go_ref):
    rows = keep_ref.shape[1]
    for n in range(own_ref.shape[0]):
        total = own_ref[n] + decode(heard_ref.at[n])
        keep_ref[n] = total[:rows]
        encode(total[rows:], go_ref.at[n])


def fold_call(own, heard):
    count, rows, cols = own.shape
    shapes = [
        jax.ShapeDtypeStruct((count, rows // 2, cols), jnp.float32),
        jax.ShapeDtypeStruct((count, rows // 2 + EXP_ROWS, cols), jnp.int16),
    ]
    return pl.pallas_call(
        fold_kernel,
        out_shape=shapes,
        compiler_params=params(),
        cost_estimate=cost(20 * own.size, 10 * own.size),
    )(own, heard)


def pack_kernel(own_ref, heard_ref, out_ref):
    rows = out_ref.shape[2]
    first = lax.broadcasted_iota(jnp.int32, (rows, 128), 1) < 64
    for n in range(own_ref.shape[0]):
        total = own_ref[n] + decode(heard_ref.at[n])
        for block in range(out_ref.shape[0] // 2):
            cols = slice(block * 128, (block + 1) * 128)
            real, imag = total[:rows, cols], total[rows:, cols]
            out_ref[2 * block, n] = jnp.where(first, real, pltpu.roll(imag, 64, 1))
            out_ref[2 * block + 1, n] = jnp.where(first, pltpu.roll(real, 64, 1), imag)


def pack_call(own, heard):
    count, rows, cols = own.shape
    return pl.pallas_call(
        pack_kernel,
        out_shape=jax.ShapeDtypeStruct((cols // 64, count, rows // 2, 128), jnp.float32),
        compiler_params=params(),
        cost_estimate=cost(20 * own.size, 10 * own.size),
    )(own, heard)


def exchange_kernel(slots, waits, *refs):
    here_refs, (there_ref, coulomb_ref) = refs[:slots], refs[slots : slots + 2]
    out_ref, token_ref, left_ref = refs[slots + 2 + waits :]
    _, _, rows, depth = here_refs[0].shape
    token_ref[...] = jnp.zeros_like(token_ref)

    @pl.when(pl.program_id(0) == 0)
    def _():
        for slot in range(slots):
            for part in range(2):
                left_ref[
                    slot * rows : (slot + 1) * rows, part * depth : (part + 1) * depth
                ] = here_refs[slot][0, part]

    factor = coulomb_ref[0]
    real = there_ref[0, 0].astype(jnp.float32) * factor
    imag = there_ref[0, 1].astype(jnp.float32) * factor
    right = jnp.concatenate(
        [jnp.concatenate([real, -imag], axis=1), jnp.concatenate([imag, real], axis=1)], axis=0
    )
    high, low = halves(right)
    left = left_ref[...]
    both = mm_nt(left, high) + mm_nt(left, low)
    cols = both.shape[1] // 2
    for part in range(2):
        out_ref[0, part] = both[:, part * cols : (part + 1) * cols]


def exchange_call(heres, there, coulomb, after):
    slots, rows = len(heres), heres[0][0].shape[2]
    points, _, cols, depth = there.shape
    height = slots * rows
    return pl.pallas_call(
        lambda *refs: exchange_kernel(slots, len(after), *refs),
        grid=(points,),
        in_specs=[
            pl.BlockSpec((1,) + h.shape[1:], lambda q, slot=slot: (slot, 0, 0, 0))
            for h, slot in heres
        ]
        + [
            pl.BlockSpec((1, 2, cols, depth), lambda q: (q, 0, 0, 0)),
            pl.BlockSpec((1, 1, depth), lambda q: (q, 0, 0)),
        ]
        + [pl.BlockSpec(memory_space=pl.ANY) for _ in after],
        out_specs=[
            pl.BlockSpec((1, 2, height, cols), lambda q: (q, 0, 0, 0)),
            pl.BlockSpec(TOKEN.shape, lambda q: (0, 0)),
        ],
        out_shape=[jax.ShapeDtypeStruct((points, 2, height, cols), jnp.float32), TOKEN],
        scratch_shapes=[pltpu.VMEM((height, 2 * depth), jnp.bfloat16)],
        compiler_params=params(),
        cost_estimate=cost(2 * points * height * 2 * cols * 2 * depth * 2, 8 * points * cols * depth),
    )(*[h for h, _ in heres], there, coulomb.reshape(points, 1, depth), *after)


def tile_kernel(order, heard, chunks, waits, me_ref, *refs):
    slots = len(order)
    con_refs, keep_ref = refs[:slots], refs[slots]
    heard_refs = refs[slots + 1 : slots + 1 + heard]
    exch_ref, row_ref, col_direct_ref, col_exch_ref = refs[slots + 1 + heard : slots + 5 + heard]
    keep_out, go_out, token_ref, con_all, direct_ref, natural_ref, sums_ref = refs[
        slots + 5 + heard + waits :
    ]
    token_ref[...] = jnp.zeros_like(token_ref)
    total = keep_ref[...]
    for ref in heard_refs:
        total = total + decode(ref)
    pairs, width = total.shape[0] // 2, total.shape[1]
    rows = con_refs[0].shape[3]
    pitch = con_all.shape[0] // slots
    for slot in range(slots):
        for part in range(2):
            con_all[
                slot * pitch : slot * pitch + rows, part * width : (part + 1) * width
            ] = con_refs[slot][0, 0, part]
    real, imag = total[:pairs], total[pairs:]
    right = jnp.concatenate(
        [jnp.concatenate([real, -imag], axis=1), jnp.concatenate([imag, real], axis=1)], axis=0
    )
    high, low = halves(right)
    left = con_all[...]
    direct = mm_nt(left, high) + mm_nt(left, low)
    lanes = direct_ref.shape[0]
    for slot in range(slots):
        start = pl.multiple_of(jnp.bitwise_xor(me_ref[0], order[slot]) * rows, 8)
        for lane in range(lanes):
            direct_ref[lane, pl.ds(start, rows), :] = direct[
                slot * pitch : slot * pitch + rows, lane * 128 : (lane + 1) * 128
            ]
    group = 128 // NV
    place = lax.broadcasted_iota(jnp.int32, (NC, 128), 1) // NV
    per_part = lanes // 2
    for part in range(2):
        for chunk in range(NC // group):
            for band in range(NV):
                block = jnp.zeros((NC, 128), jnp.float32)
                for step in range(group):
                    e = chunk * group + step
                    piece = direct_ref[part * per_part + band // group, pl.ds(e, NC, stride=NC), :]
                    turn = (NV * (step - band)) % 128
                    if turn:
                        piece = pltpu.roll(piece, turn, 1)
                    block = jnp.where(place == step, piece, block)
                natural_ref[
                    part, band * NC : (band + 1) * NC, chunk * 128 : (chunk + 1) * 128
                ] = block
    pick_rows = row_ref[...]
    count = NT // chunks
    for part in range(2):
        result = None
        for source, pick_cols in (
            (natural_ref[part], col_direct_ref),
            (exch_ref[0, part], col_exch_ref),
        ):
            for piece in halves(source):
                moved = mm(pick_rows, piece).astype(jnp.bfloat16)
                term = mm(moved, pick_cols[...])
                result = term if result is None else result + term
        for chunk in range(chunks):
            at = (2 * chunk + part) * count
            sums_ref[at : at + count, :] = result[chunk * count : (chunk + 1) * count]
    stays = keep_out.shape[0]
    keep_out[...] = sums_ref[0:stays, :]
    encode(sums_ref[stays:, :], go_out)


def tile_call(
    cons, point, keep, heard, exch, me, order, pick_rows, col_direct, col_exch, chunks, after
):
    slots = len(cons)
    _, _, _, rows, width = cons[0][0].shape
    height, tall = keep.shape[0], heard[0].shape[0]
    pitch = -(-rows // 16) * 16
    out_cols = col_direct.shape[1]
    stages = len(heard)
    whole = lambda a: pl.BlockSpec(a.shape, lambda i, me: (0,) * len(a.shape))
    shapes = [
        jax.ShapeDtypeStruct((NT, out_cols), jnp.float32),
        jax.ShapeDtypeStruct((NT + EXP_ROWS, out_cols), jnp.int16),
        TOKEN,
    ]

    def at(known):
        return lambda i, me: (0, block_of(me[0], known, stages, False))

    grid_spec = pltpu.PrefetchScalarGridSpec(
        num_scalar_prefetch=1,
        grid=(1,),
        in_specs=[
            pl.BlockSpec((1, 1, 2, rows, width), lambda i, me, place=place: (place, point, 0, 0, 0))
            for _, place in cons
        ]
        + [pl.BlockSpec((height, width), at(1))]
        + [pl.BlockSpec((tall, width), at(n + 1)) for n in range(stages)]
        + [
            pl.BlockSpec((1,) + exch.shape[1:], lambda i, me: (point, 0, 0, 0)),
            whole(pick_rows),
            whole(col_direct),
            whole(col_exch),
        ]
        + [pl.BlockSpec(memory_space=pl.ANY) for _ in after],
        out_specs=[whole(a) for a in shapes],
        scratch_shapes=[
            pltpu.VMEM((slots * pitch, 2 * width), jnp.bfloat16),
            pltpu.VMEM((height // 128, NC * NC, 128), jnp.float32),
            pltpu.VMEM((2, NT, NT), jnp.float32),
            pltpu.VMEM((2 * NT, out_cols), jnp.float32),
        ],
    )
    return pl.pallas_call(
        lambda *refs: tile_kernel(order, stages, chunks, len(after), *refs),
        grid_spec=grid_spec,
        out_shape=shapes,
        compiler_params=params(),
        cost_estimate=cost(2.8e9, 8e6),
    )(me, *[c for c, _ in cons], keep, *heard, exch, pick_rows, col_direct, col_exch, *after)


def swap(value, axis, size, bit):
    return lax.ppermute(value, axis, [(i, i ^ bit) for i in range(size)])


def gather_slots(value, axis, size, token=None):
    found = {0: (value[None], 0)}
    bit = size // 2
    while bit:
        known = sorted(found)
        sent = jnp.concatenate([found[r][0][found[r][1] :][:1] for r in known])
        if token is not None and len(known) > 1:
            sent = behind(sent, token)
        got = swap(sent, axis, size, bit)
        for place, r in enumerate(known):
            found[r ^ bit] = (got, place)
        bit //= 2
    return [found[r] for r in range(size)]


def halving_order(bits):
    order = [0]
    for bit in reversed(bits):
        order = order + [o ^ bit for o in order]
    return order


def behind(value, token):
    return lax.optimization_barrier((value, token))[0]


def on_device(*args):
    (val_density, con_density, screened, coulomb, trans_here, trans_there, shift_map, ordering) = args
    ga, pair = lax.axis_size("ga"), lax.axis_size("pair")
    points = con_density.shape[1]
    slab = con_density.shape[3]
    width = slab // ga
    me_ga, me_pair = lax.axis_index("ga"), lax.axis_index("pair")
    me = me_ga.astype(jnp.int32).reshape(1)
    ga_bits = [1 << b for b in range(ga.bit_length() - 1)]
    pair_bits = [1 << b for b in range(pair.bit_length() - 1)]
    ga_order = halving_order(ga_bits)
    stages, half = len(ga_bits), ga // 2

    con = jnp.transpose(con_density, (1, 2, 0, 3))
    *stay, go, token = shift_call(con, shift_map, me, ga_order, width)
    first = gather_slots(jnp.transpose(val_density[:, :1], (1, 2, 0, 3)), "pair", pair, token)
    nearest = ga_bits[0]
    from_near = swap(go, "ga", ga, nearest)
    cons = {0: (stay[0], 0)}
    for slot, block in zip(ga_order[1:half], stay[1:]):
        cons[slot] = (swap(block, "ga", ga, slot), 0)
    later = behind(val_density[:, 1:], first[pair // 2][0])
    later = jnp.transpose(later, (1, 2, 0, 3))

    gone, keep, tokens = [], [], [token]
    for q in range(points):
        vals, place = (first, 0) if q == 0 else (others, q - 1)
        coded, own, token = x_call(vals, screened, place, q, me, 4, tokens[-1:])
        if q == 0:
            first_token = token
            others = gather_slots(later, "pair", pair, first_token)
        if q + 1 < min(points, half):
            token = behind(token, cons[ga_order[q + 1]][0])
        tokens.append(token)
        gone.append(coded)
        keep.append(own)
    after = tokens[-1:]

    from_near = behind(from_near, first_token)
    for place, slot in enumerate(ga_order[half:]):
        cons[slot] = (from_near, 0)
        if slot != nearest:
            cons[slot] = (swap(from_near[place : place + 1], "ga", ga, slot ^ nearest), 0)
    after = [behind(after[0], [cons[slot][0] for slot in ga_order[half:]])]
    cons = [cons[slot] for slot in ga_order]

    row_count, col_count = NT // pair, NT // ga
    row_slots = jnp.asarray(halving_order(pair_bits), jnp.int32)
    row_trans = ordering.reshape(pair, row_count)[me_pair ^ row_slots].reshape(-1)
    at_row = ((row_trans // row_count) ^ me_pair) * row_count + row_trans % row_count
    pick_rows = (at_row[:, None] == jnp.arange(NT, dtype=jnp.int32)[None, :]).astype(jnp.bfloat16)
    col_trans = ordering.reshape(ga, col_count)[me_ga ^ jnp.asarray(ga_order, jnp.int32)]
    col_trans = jnp.pad(col_trans, ((0, 0), (0, 64 - col_count)), constant_values=-1).reshape(1, -1)
    real_col = col_trans >= 0
    at_direct = jnp.where(real_col, (col_trans % NC) * NV + col_trans // NC, -1)
    own_col = real_col & (col_trans // row_count == me_pair)
    at_exch = jnp.where(own_col, col_trans % row_count, -1)

    def pick_cols(at, size, scale):
        hot = at == jnp.arange(size, dtype=jnp.int32)[:, None]
        return jnp.where(hot, scale, 0.0).astype(jnp.bfloat16)

    col_direct, col_exch = pick_cols(at_direct, NT, -1.0), pick_cols(at_exch, row_count, 2.0)

    heard = [[swap(gone[q], "ga", ga, ga_bits[0])] for q in range(points)]
    tiles = [None] * points
    exch = None
    for wave in range(2 * points + stages):
        for q in reversed(range(points)):
            stage = wave - 2 * q
            if 1 <= stage < stages:
                columns = (ga >> (stage + 1)) * width
                coded, token = hop_call(keep[q], heard[q], me, stage, columns, after)
                after = [token]
                heard[q].append(swap(coded, "ga", ga, ga_bits[stage]))
                if exch is None:
                    here = jnp.transpose(behind(trans_here, tokens[1]), (1, 0, 2))
                    heres = gather_slots(here, "pair", pair, tokens[-1])
                    there = jnp.transpose(behind(trans_there, tokens[1]), (1, 2, 0, 3))
                    exch, token = exchange_call(heres, there, coulomb, after)
                    after = [token]
            elif stage == stages:
                *tiles[q], token = tile_call(
                    cons, q, keep[q], heard[q], exch, me, ga_order, pick_rows, col_direct,
                    col_exch, pair, after,
                )
                after = [token]
            if (q, stage) == (points - 1, stages - 1):
                gate = token

    outs = []
    for group in (tiles[:-1], tiles[-1:]):
        own, sent = (jnp.stack(items) for items in zip(*group))
        if len(outs) == 0:
            sent = behind(sent, gate)
        for bit in pair_bits[:-1]:
            own, sent = fold_call(own, swap(sent, "pair", pair, bit))
        total = pack_call(own, swap(sent, "pair", pair, pair_bits[-1]))
        for bit in ga_bits:
            size = total.shape[0] // 2
            total = total[:size] + swap(total[size:], "ga", ga, bit)
        outs.append(total[0])
    out = jnp.concatenate(outs).reshape(points, row_count, 2, 64)[..., :col_count]
    return jnp.transpose(out, (0, 2, 1, 3))


def contract_float(left, right):
    high = lax.Precision.HIGHEST
    real_part = jnp.einsum(
        "nkg,mkg->nkm", left[:, :, 0], right[:, :, 0], precision=high
    ) - jnp.einsum("nkg,mkg->nkm", left[:, :, 1], right[:, :, 1], precision=high)
    imag_part = jnp.einsum(
        "nkg,mkg->nkm", left[:, :, 0], right[:, :, 1], precision=high
    ) + jnp.einsum("nkg,mkg->nkm", left[:, :, 1], right[:, :, 0], precision=high)
    return jnp.stack([real_part, imag_part], axis=2)


def times_cols(rows, weights):
    first = jnp.einsum(
        "nkh,kgh->nkg", rows[:, :, 0], weights[:, 0], preferred_element_type=jnp.float32
    ) - jnp.einsum("nkh,kgh->nkg", rows[:, :, 1], weights[:, 1], preferred_element_type=jnp.float32)
    second = jnp.einsum(
        "nkh,kgh->nkg", rows[:, :, 0], weights[:, 1], preferred_element_type=jnp.float32
    ) + jnp.einsum("nkh,kgh->nkg", rows[:, :, 1], weights[:, 0], preferred_element_type=jnp.float32)
    return jnp.stack([first, second], axis=2)


def on_any_device(
    val_density, con_density, screened, coulomb, trans_here, trans_there, shift_map, ordering
):
    con_count = con_density.shape[0]
    points = con_density.shape[1]
    slab_cols = con_density.shape[3]
    blocks = slab_cols // GBLK
    within = (shift_map % GBLK).reshape(points, blocks, GBLK)
    onehot = (
        within[:, :, :, None] == jnp.arange(GBLK, dtype=jnp.int32)[None, None, None, :]
    ).astype(jnp.bfloat16)
    con_blocks = con_density.reshape(con_count, points, 2, blocks, GBLK)
    shifted = (
        jnp.einsum("bkpnh,kngh->bkpng", con_blocks, onehot, preferred_element_type=jnp.float32)
        .astype(jnp.bfloat16)
        .reshape(con_density.shape)
    )
    whole_here = lax.all_gather(trans_here, "pair", axis=0, tiled=True).astype(jnp.float32)
    weighted = trans_there.astype(jnp.float32) * coulomb[None, :, None, :]
    high = lax.Precision.HIGHEST
    exch_real = jnp.einsum(
        "tg,skg->tks", whole_here[:, 0], weighted[:, :, 0], precision=high
    ) - jnp.einsum("tg,skg->tks", whole_here[:, 1], weighted[:, :, 1], precision=high)
    exch_imag = jnp.einsum(
        "tg,skg->tks", whole_here[:, 0], weighted[:, :, 1], precision=high
    ) + jnp.einsum("tg,skg->tks", whole_here[:, 1], weighted[:, :, 0], precision=high)
    exch_part = jnp.stack([exch_real, exch_imag], axis=2)
    whole_con = lax.all_gather(shifted, "ga", axis=0, tiled=True)
    screened_rows = lax.psum_scatter(
        times_cols(whole_con, screened), "pair", scatter_dimension=0, tiled=True
    )
    direct_part = contract_float(
        lax.all_gather(val_density, "pair", axis=0, tiled=True).astype(jnp.float32), screened_rows
    )
    direct_sum, exch_sum = lax.psum((direct_part, exch_part), "ga")
    direct_full, exch_full = (
        lax.all_gather(direct_sum, "pair", axis=3, tiled=True),
        lax.all_gather(exch_sum, "pair", axis=3, tiled=True),
    )
    row_count = NT // lax.axis_size("pair")
    col_count = NT // lax.axis_size("ga")
    row_trans = lax.dynamic_slice_in_dim(ordering, lax.axis_index("pair") * row_count, row_count, 0)
    col_trans = lax.dynamic_slice_in_dim(ordering, lax.axis_index("ga") * col_count, col_count, 0)
    row_pairs = (row_trans // NC)[:, None] * NV + (col_trans // NC)[None, :]
    col_pairs = (row_trans % NC)[:, None] * NC + (col_trans % NC)[None, :]
    picked = direct_full[row_pairs.reshape(-1)]
    col_mask = (
        col_pairs.reshape(-1)[:, None] == jnp.arange(direct_full.shape[3], dtype=jnp.int32)[None, :]
    ).astype(jnp.float32)
    direct_flat = jnp.sum(picked * col_mask[:, None, None, :], axis=3)
    direct_sel = jnp.transpose(direct_flat.reshape(row_count, col_count, points, 2), (2, 3, 0, 1))
    exch_picked = exch_full[row_trans]
    col_hot = (jnp.arange(NT, dtype=jnp.int32)[:, None] == col_trans[None, :]).astype(jnp.float32)
    exch_sel = jnp.einsum("rkpt,tc->kprc", exch_picked, col_hot, precision=high)
    return 2.0 * exch_sel - direct_sel


def solution(mesh):
    in_specs = (
        P("pair", None, None, "ga"),
        P("ga", None, None, "pair"),
        P(None, None, "ga", "pair"),
        P(None, "ga"),
        P("pair", None, "ga"),
        P("pair", None, None, "ga"),
        P(None, "pair"),
        P(),
    )
    out_specs = P(None, None, "pair", "ga")

    def run(*args):
        ga, pair = mesh.shape["ga"], mesh.shape["pair"]
        con_count, h_count = args[1].shape[0], args[1].shape[3]
        suits = (
            ga & (ga - 1) == 0
            and pair & (pair - 1) == 0
            and ga >= 4
            and pair >= 2
            and NT % (pair * GROUP // 2) == 0
            and h_count % (ga * pair * GBLK) == 0
            and con_count % (8 * ga) == 0
            and args[0].shape[0] % (16 * pair) == 0
            and NT % (16 * pair) == 0
            and NT // ga <= 64
        )
        body = on_device if suits else on_any_device
        return jax.shard_map(
            body, mesh=mesh, in_specs=in_specs, out_specs=out_specs, check_vma=False
        )(*args)

    return run
```

```python
import jax
import jax.numpy as jnp
from jax import lax
from jax.experimental import pallas as pl
from jax.experimental.pallas import tpu as pltpu
from jax.sharding import PartitionSpec as P

NV = 16
NC = 24
GBLK = 128
NT = 384

GROUP = 64
EXP_ROWS = 16
STEPS = 128.0
TOP = 32700.0
MAGIC = 1.5 * 2.0**23
NT_DIMS = (((1,), (1,)), ((), ()))
VMEM = 40 * 1024 * 1024


TOKEN = jax.ShapeDtypeStruct((8, 128), jnp.float32)


def params():
    return pltpu.CompilerParams(vmem_limit_bytes=VMEM)


def cost(flops, moved):
    return pl.CostEstimate(flops=int(flops) // 64, bytes_accessed=int(moved) // 64, transcendentals=0)


def mm(left, right):
    return jnp.dot(left, right, preferred_element_type=jnp.float32)


def mm_nt(left, right):
    return lax.dot_general(left, right, NT_DIMS, preferred_element_type=jnp.float32)


def halves(value):
    high = value.astype(jnp.bfloat16)
    low = (value - high.astype(jnp.float32)).astype(jnp.bfloat16)
    return high, low


def encode(value, out_ref):
    rows, width = value.shape
    groups = rows // GROUP
    parts = value.reshape(groups, GROUP, width)
    largest = jnp.maximum(jnp.max(jnp.abs(parts), axis=1), 1e-30)
    level = jnp.ceil(jnp.log2(largest) * STEPS) + 1.0
    factor = TOP * jnp.exp2(level * (-1.0 / STEPS))
    coded = ((parts * factor[:, None, :] + MAGIC) - MAGIC).astype(jnp.int32)
    out_ref[0:rows, :] = coded.reshape(rows, width).astype(jnp.int16)
    pad = jnp.zeros((EXP_ROWS - groups, width), jnp.int32)
    out_ref[rows : rows + EXP_ROWS, :] = jnp.concatenate(
        [level.astype(jnp.int32), pad], axis=0
    ).astype(jnp.int16)


def decode(ref):
    rows = ref.shape[0] - EXP_ROWS
    width = ref.shape[1]
    groups = rows // GROUP
    level = ref[rows : rows + EXP_ROWS, :].astype(jnp.int32).astype(jnp.float32)[0:groups]
    factor = jnp.exp2(level * (1.0 / STEPS)) * (1.0 / TOP)
    parts = ref[0:rows, :].astype(jnp.int32).astype(jnp.float32).reshape(groups, GROUP, width)
    return (parts * factor[:, None, :]).reshape(rows, width)


def reversed_bits(number, count):
    return sum(((number // (1 << b)) % 2) * (1 << (count - 1 - b)) for b in range(count))


def block_of(me, known, stop, flip):
    number = 0
    for bit in range(known, stop):
        flag = (me // (1 << bit)) % 2
        number = 2 * number + (1 - flag if flip and bit == stop - 1 else flag)
    return number


def shift_kernel(order, me_ref, con_ref, map_ref, stay_ref, go_ref, token_ref):
    slots, _, _, rows, width = stay_ref.shape
    count = len(order).bit_length() - 1
    token_ref[...] = jnp.zeros_like(token_ref)
    for which, out_ref in enumerate((stay_ref, go_ref)):
        for slot in range(slots):
            dest = jnp.bitwise_xor(me_ref[0], order[which * slots + slot])
            first = reversed_bits(dest, count) * width
            for block in range(width // GBLK):
                cols = pl.ds(pl.multiple_of(first + block * GBLK, GBLK), GBLK)
                within = jnp.bitwise_and(map_ref[0, 0:1, cols], GBLK - 1)
                within = jnp.broadcast_to(within, (rows, GBLK))
                for part in range(2):
                    values = con_ref[0, part, :, cols].astype(jnp.float32)
                    moved = jnp.take_along_axis(values, within, axis=1)
                    out_ref[slot, 0, part, :, block * GBLK : (block + 1) * GBLK] = moved.astype(
                        jnp.bfloat16
                    )


def shift_call(con, shift_map, me, order, width):
    points, _, rows, slab = con.shape
    slots = len(order) // 2
    grid_spec = pltpu.PrefetchScalarGridSpec(
        num_scalar_prefetch=1,
        grid=(points,),
        in_specs=[
            pl.BlockSpec((1, 2, rows, slab), lambda q, me: (q, 0, 0, 0)),
            pl.BlockSpec((1, 1, slab), lambda q, me: (q, 0, 0)),
        ],
        out_specs=[pl.BlockSpec((slots, 1, 2, rows, width), lambda q, me: (0, q, 0, 0, 0))] * 2
        + [pl.BlockSpec(TOKEN.shape, lambda q, me: (0, 0))],
    )
    return pl.pallas_call(
        lambda *refs: shift_kernel(order, *refs),
        grid_spec=grid_spec,
        out_shape=[jax.ShapeDtypeStruct((slots, points, 2, rows, width), jnp.bfloat16)] * 2
        + [TOKEN],
        compiler_params=params(),
        cost_estimate=cost(8 * con.size, 4 * con.size),
    )(me, con, shift_map.reshape(points, 1, slab))


def x_kernel(slots, waits, me_ref, *refs):
    val_refs, weight_ref = refs[:slots], refs[slots]
    go_ref, keep_ref, token_ref, left_ref = refs[slots + 1 + waits :]
    _, _, _, rows, depth = val_refs[0].shape
    half = slots * rows
    token_ref[...] = jnp.zeros_like(token_ref)
    step = pl.program_id(0)
    halfway = pl.num_programs(0) // 2

    @pl.when(step == 0)
    def _():
        for slot in range(slots):
            real, imag = val_refs[slot][0, 0, 0], val_refs[slot][0, 0, 1]
            top = slice(slot * rows, (slot + 1) * rows)
            low = slice(half + slot * rows, half + (slot + 1) * rows)
            left_ref[top, 0:depth] = real
            left_ref[top, depth : 2 * depth] = -imag
            left_ref[low, 0:depth] = imag
            left_ref[low, depth : 2 * depth] = real

    weight = weight_ref[0].reshape(2 * depth, weight_ref.shape[3])

    @pl.when(step < halfway)
    def _():
        encode(mm(left_ref[...], weight), go_ref)

    @pl.when(step >= halfway)
    def _():
        keep_ref[...] = mm(left_ref[...], weight)


def x_call(vals, screened, place, point, me, steps, after):
    slots = len(vals)
    _, _, _, rows, depth = vals[0][0].shape
    height = 2 * slots * rows
    columns = screened.shape[3] // 2
    half = steps // 2
    width = columns // half
    grid_spec = pltpu.PrefetchScalarGridSpec(
        num_scalar_prefetch=1,
        grid=(steps,),
        in_specs=[
            pl.BlockSpec((1, 1, 2, rows, depth), lambda j, me, slot=slot: (slot, place, 0, 0, 0))
            for _, slot in vals
        ]
        + [
            pl.BlockSpec(
                (1, 2, depth, width),
                lambda j, me: (point, 0, 0, ((me[0] + 1 + j // half) % 2) * half + j % half),
            )
        ]
        + [pl.BlockSpec(memory_space=pl.ANY) for _ in after],
        out_specs=[
            pl.BlockSpec((height + EXP_ROWS, width), lambda j, me: (0, jnp.minimum(j, half - 1))),
            pl.BlockSpec((height, width), lambda j, me: (0, jnp.maximum(j - half, 0))),
            pl.BlockSpec(TOKEN.shape, lambda j, me: (0, 0)),
        ],
        scratch_shapes=[pltpu.VMEM((height, 2 * depth), jnp.bfloat16)],
    )
    return pl.pallas_call(
        lambda *refs: x_kernel(slots, len(after), *refs),
        grid_spec=grid_spec,
        out_shape=[
            jax.ShapeDtypeStruct((height + EXP_ROWS, columns), jnp.int16),
            jax.ShapeDtypeStruct((height, columns), jnp.float32),
            TOKEN,
        ],
        compiler_params=params(),
        cost_estimate=cost(
            2 * height * 2 * depth * 2 * columns, 8 * depth * columns + 6 * height * columns
        ),
    )(me, *[v for v, _ in vals], screened, *after)


def hop_kernel(heard, me_ref, keep_ref, *refs):
    total = keep_ref[...]
    for ref in refs[:heard]:
        total = total + decode(ref)
    out_ref, token_ref = refs[-2:]
    encode(total, out_ref)
    token_ref[...] = jnp.zeros_like(token_ref)


def hop_call(keep, others, me, stage, width, after):
    height, tall = keep.shape[0], others[0].shape[0]
    steps = width // 128

    def at(known):
        return lambda i, me: (0, block_of(me[0], known, stage + 1, True) * steps + i)

    grid_spec = pltpu.PrefetchScalarGridSpec(
        num_scalar_prefetch=1,
        grid=(steps,),
        in_specs=[pl.BlockSpec((height, 128), at(1))]
        + [pl.BlockSpec((tall, 128), at(n + 1)) for n in range(len(others))]
        + [pl.BlockSpec(memory_space=pl.ANY) for _ in after],
        out_specs=[
            pl.BlockSpec((tall, 128), lambda i, me: (0, i)),
            pl.BlockSpec(TOKEN.shape, lambda i, me: (0, 0)),
        ],
    )
    return pl.pallas_call(
        lambda *refs: hop_kernel(len(others), *refs),
        grid_spec=grid_spec,
        out_shape=[jax.ShapeDtypeStruct((tall, width), jnp.int16), TOKEN],
        compiler_params=params(),
        cost_estimate=cost(20 * height * width, 8 * height * width),
    )(me, keep, *others, *after)


def fold_kernel(own_ref, heard_ref, keep_ref, go_ref):
    rows = keep_ref.shape[1]
    for n in range(own_ref.shape[0]):
        total = own_ref[n] + decode(heard_ref.at[n])
        keep_ref[n] = total[:rows]
        encode(total[rows:], go_ref.at[n])


def fold_call(own, heard):
    count, rows, cols = own.shape
    shapes = [
        jax.ShapeDtypeStruct((count, rows // 2, cols), jnp.float32),
        jax.ShapeDtypeStruct((count, rows // 2 + EXP_ROWS, cols), jnp.int16),
    ]
    return pl.pallas_call(
        fold_kernel,
        out_shape=shapes,
        compiler_params=params(),
        cost_estimate=cost(20 * own.size, 10 * own.size),
    )(own, heard)


def pack_kernel(own_ref, heard_ref, out_ref):
    rows = out_ref.shape[2]
    first = lax.broadcasted_iota(jnp.int32, (rows, 128), 1) < 64
    for n in range(own_ref.shape[0]):
        total = own_ref[n] + decode(heard_ref.at[n])
        for block in range(out_ref.shape[0] // 2):
            cols = slice(block * 128, (block + 1) * 128)
            real, imag = total[:rows, cols], total[rows:, cols]
            out_ref[2 * block, n] = jnp.where(first, real, pltpu.roll(imag, 64, 1))
            out_ref[2 * block + 1, n] = jnp.where(first, pltpu.roll(real, 64, 1), imag)


def pack_call(own, heard):
    count, rows, cols = own.shape
    return pl.pallas_call(
        pack_kernel,
        out_shape=jax.ShapeDtypeStruct((cols // 64, count, rows // 2, 128), jnp.float32),
        compiler_params=params(),
        cost_estimate=cost(20 * own.size, 10 * own.size),
    )(own, heard)


def exchange_kernel(slots, waits, *refs):
    here_refs, (there_ref, coulomb_ref) = refs[:slots], refs[slots : slots + 2]
    out_ref, token_ref, left_ref = refs[slots + 2 + waits :]
    _, _, rows, depth = here_refs[0].shape
    token_ref[...] = jnp.zeros_like(token_ref)

    @pl.when(pl.program_id(0) == 0)
    def _():
        for slot in range(slots):
            for part in range(2):
                left_ref[
                    slot * rows : (slot + 1) * rows, part * depth : (part + 1) * depth
                ] = here_refs[slot][0, part]

    factor = coulomb_ref[0]
    real = there_ref[0, 0].astype(jnp.float32) * factor
    imag = there_ref[0, 1].astype(jnp.float32) * factor
    right = jnp.concatenate(
        [jnp.concatenate([real, -imag], axis=1), jnp.concatenate([imag, real], axis=1)], axis=0
    )
    high, low = halves(right)
    left = left_ref[...]
    both = mm_nt(left, high) + mm_nt(left, low)
    cols = both.shape[1] // 2
    for part in range(2):
        out_ref[0, part] = both[:, part * cols : (part + 1) * cols]


def exchange_call(heres, there, coulomb, after):
    slots, rows = len(heres), heres[0][0].shape[2]
    points, _, cols, depth = there.shape
    height = slots * rows
    return pl.pallas_call(
        lambda *refs: exchange_kernel(slots, len(after), *refs),
        grid=(points,),
        in_specs=[
            pl.BlockSpec((1,) + h.shape[1:], lambda q, slot=slot: (slot, 0, 0, 0))
            for h, slot in heres
        ]
        + [
            pl.BlockSpec((1, 2, cols, depth), lambda q: (q, 0, 0, 0)),
            pl.BlockSpec((1, 1, depth), lambda q: (q, 0, 0)),
        ]
        + [pl.BlockSpec(memory_space=pl.ANY) for _ in after],
        out_specs=[
            pl.BlockSpec((1, 2, height, cols), lambda q: (q, 0, 0, 0)),
            pl.BlockSpec(TOKEN.shape, lambda q: (0, 0)),
        ],
        out_shape=[jax.ShapeDtypeStruct((points, 2, height, cols), jnp.float32), TOKEN],
        scratch_shapes=[pltpu.VMEM((height, 2 * depth), jnp.bfloat16)],
        compiler_params=params(),
        cost_estimate=cost(2 * points * height * 2 * cols * 2 * depth * 2, 8 * points * cols * depth),
    )(*[h for h, _ in heres], there, coulomb.reshape(points, 1, depth), *after)


def tile_kernel(order, heard, chunks, waits, me_ref, *refs):
    slots = len(order)
    con_refs, keep_ref = refs[:slots], refs[slots]
    heard_refs = refs[slots + 1 : slots + 1 + heard]
    exch_ref, row_ref, col_direct_ref, col_exch_ref = refs[slots + 1 + heard : slots + 5 + heard]
    keep_out, go_out, token_ref, con_all, direct_ref, natural_ref, sums_ref = refs[
        slots + 5 + heard + waits :
    ]
    token_ref[...] = jnp.zeros_like(token_ref)
    total = keep_ref[...]
    for ref in heard_refs:
        total = total + decode(ref)
    pairs, width = total.shape[0] // 2, total.shape[1]
    rows = con_refs[0].shape[3]
    pitch = con_all.shape[0] // slots
    for slot in range(slots):
        for part in range(2):
            con_all[
                slot * pitch : slot * pitch + rows, part * width : (part + 1) * width
            ] = con_refs[slot][0, 0, part]
    real, imag = total[:pairs], total[pairs:]
    right = jnp.concatenate(
        [jnp.concatenate([real, -imag], axis=1), jnp.concatenate([imag, real], axis=1)], axis=0
    )
    high, low = halves(right)
    left = con_all[...]
    direct = mm_nt(left, high) + mm_nt(left, low)
    lanes = direct_ref.shape[0]
    for slot in range(slots):
        start = pl.multiple_of(jnp.bitwise_xor(me_ref[0], order[slot]) * rows, 8)
        for lane in range(lanes):
            direct_ref[lane, pl.ds(start, rows), :] = direct[
                slot * pitch : slot * pitch + rows, lane * 128 : (lane + 1) * 128
            ]
    group = 128 // NV
    place = lax.broadcasted_iota(jnp.int32, (NC, 128), 1) // NV
    per_part = lanes // 2
    for part in range(2):
        for chunk in range(NC // group):
            for band in range(NV):
                block = jnp.zeros((NC, 128), jnp.float32)
                for step in range(group):
                    e = chunk * group + step
                    piece = direct_ref[part * per_part + band // group, pl.ds(e, NC, stride=NC), :]
                    turn = (NV * (step - band)) % 128
                    if turn:
                        piece = pltpu.roll(piece, turn, 1)
                    block = jnp.where(place == step, piece, block)
                natural_ref[
                    part, band * NC : (band + 1) * NC, chunk * 128 : (chunk + 1) * 128
                ] = block
    pick_rows = row_ref[...]
    count = NT // chunks
    for part in range(2):
        result = None
        for source, pick_cols in (
            (natural_ref[part], col_direct_ref),
            (exch_ref[0, part], col_exch_ref),
        ):
            for piece in halves(source):
                moved = mm(pick_rows, piece).astype(jnp.bfloat16)
                term = mm(moved, pick_cols[...])
                result = term if result is None else result + term
        for chunk in range(chunks):
            at = (2 * chunk + part) * count
            sums_ref[at : at + count, :] = result[chunk * count : (chunk + 1) * count]
    stays = keep_out.shape[0]
    keep_out[...] = sums_ref[0:stays, :]
    encode(sums_ref[stays:, :], go_out)


def tile_call(
    cons, point, keep, heard, exch, me, order, pick_rows, col_direct, col_exch, chunks, after
):
    slots = len(cons)
    _, _, _, rows, width = cons[0][0].shape
    height, tall = keep.shape[0], heard[0].shape[0]
    pitch = -(-rows // 16) * 16
    out_cols = col_direct.shape[1]
    stages = len(heard)
    whole = lambda a: pl.BlockSpec(a.shape, lambda i, me: (0,) * len(a.shape))
    shapes = [
        jax.ShapeDtypeStruct((NT, out_cols), jnp.float32),
        jax.ShapeDtypeStruct((NT + EXP_ROWS, out_cols), jnp.int16),
        TOKEN,
    ]

    def at(known):
        return lambda i, me: (0, block_of(me[0], known, stages, False))

    grid_spec = pltpu.PrefetchScalarGridSpec(
        num_scalar_prefetch=1,
        grid=(1,),
        in_specs=[
            pl.BlockSpec((1, 1, 2, rows, width), lambda i, me, place=place: (place, point, 0, 0, 0))
            for _, place in cons
        ]
        + [pl.BlockSpec((height, width), at(1))]
        + [pl.BlockSpec((tall, width), at(n + 1)) for n in range(stages)]
        + [
            pl.BlockSpec((1,) + exch.shape[1:], lambda i, me: (point, 0, 0, 0)),
            whole(pick_rows),
            whole(col_direct),
            whole(col_exch),
        ]
        + [pl.BlockSpec(memory_space=pl.ANY) for _ in after],
        out_specs=[whole(a) for a in shapes],
        scratch_shapes=[
            pltpu.VMEM((slots * pitch, 2 * width), jnp.bfloat16),
            pltpu.VMEM((height // 128, NC * NC, 128), jnp.float32),
            pltpu.VMEM((2, NT, NT), jnp.float32),
            pltpu.VMEM((2 * NT, out_cols), jnp.float32),
        ],
    )
    return pl.pallas_call(
        lambda *refs: tile_kernel(order, stages, chunks, len(after), *refs),
        grid_spec=grid_spec,
        out_shape=shapes,
        compiler_params=params(),
        cost_estimate=cost(2.8e9, 8e6),
    )(me, *[c for c, _ in cons], keep, *heard, exch, pick_rows, col_direct, col_exch, *after)


def swap(value, axis, size, bit):
    return lax.ppermute(value, axis, [(i, i ^ bit) for i in range(size)])


def halving_order(bits):
    order = [0]
    for bit in reversed(bits):
        order = order + [o ^ bit for o in order]
    return order


def behind(value, token):
    return lax.optimization_barrier((value, token))[0]


def on_device(*args):
    (val_density, con_density, screened, coulomb, trans_here, trans_there, shift_map, ordering) = args
    ga, pair = lax.axis_size("ga"), lax.axis_size("pair")
    points = con_density.shape[1]
    slab = con_density.shape[3]
    width = slab // ga
    me_ga, me_pair = lax.axis_index("ga"), lax.axis_index("pair")
    me = me_ga.astype(jnp.int32).reshape(1)
    ga_bits = [1 << b for b in range(ga.bit_length() - 1)]
    pair_bits = [1 << b for b in range(pair.bit_length() - 1)]
    ga_order = halving_order(ga_bits)
    stages, half = len(ga_bits), ga // 2

    val = jnp.transpose(val_density, (1, 2, 0, 3))
    vals = {0: val}
    for bit in reversed(pair_bits):
        for slot in sorted(vals):
            vals[slot ^ bit] = swap(vals[slot], "pair", pair, bit)

    con = jnp.transpose(behind(con_density, val), (1, 2, 0, 3))
    stay, go, token = shift_call(con, shift_map, me, ga_order, width)
    nearest = ga_bits[0]
    from_near = swap(go, "ga", ga, nearest)

    row_count, col_count = NT // pair, NT // ga
    row_slots = jnp.asarray(halving_order(pair_bits), jnp.int32)
    row_trans = ordering.reshape(pair, row_count)[me_pair ^ row_slots].reshape(-1)
    at_row = ((row_trans // row_count) ^ me_pair) * row_count + row_trans % row_count
    pick_rows = (at_row[:, None] == jnp.arange(NT, dtype=jnp.int32)[None, :]).astype(jnp.bfloat16)
    col_trans = ordering.reshape(ga, col_count)[me_ga ^ jnp.asarray(ga_order, jnp.int32)]
    col_trans = jnp.pad(col_trans, ((0, 0), (0, 64 - col_count)), constant_values=-1).reshape(1, -1)
    real_col = col_trans >= 0
    at_direct = jnp.where(real_col, (col_trans % NC) * NV + col_trans // NC, -1)
    own_col = real_col & (col_trans // row_count == me_pair)
    at_exch = jnp.where(own_col, col_trans % row_count, -1)

    def pick_cols(at, size, scale):
        hot = at == jnp.arange(size, dtype=jnp.int32)[:, None]
        return jnp.where(hot, scale, 0.0).astype(jnp.bfloat16)

    col_direct, col_exch = pick_cols(at_direct, NT, -1.0), pick_cols(at_exch, row_count, 2.0)

    there = jnp.transpose(trans_there, (1, 2, 0, 3))
    here = jnp.transpose(behind(trans_here, vals[pair // 2]), (1, 0, 2))
    heres = {0: here, pair // 2: swap(here, "pair", pair, pair // 2)}
    token = behind(
        token, (there, heres[pair // 2], pick_rows, col_direct, col_exch, from_near)
    )
    gone, keep = [], []
    for q in range(points):
        coded, own, token = x_call(
            [(vals[slot][None], 0) for slot in range(pair)], screened, q, q, me, 4, [token]
        )
        gone.append(coded)
        keep.append(own)
        if q == 0:
            stay, from_near = behind((stay, from_near), token)
            cons = {0: (stay, 0), nearest: (from_near, 0)}
            for place, slot in enumerate(ga_order[1:half], 1):
                both = swap(jnp.stack([stay[place], from_near[place]]), "ga", ga, slot)
                cons[slot], cons[slot ^ nearest] = (both, 0), (both, 1)
    after = [behind(token, [cons[slot][0] for slot in ga_order[:half] if slot & ga_bits[-1]])]
    cons = [cons[slot] for slot in ga_order]

    heard = [[swap(gone[q], "ga", ga, ga_bits[0])] for q in range(points)]
    tiles = [None] * points
    exch = None
    work = [(2 * q + stage, q, stage) for q in range(points) for stage in range(1, stages)]
    work += [(2 * q + stages + (1.2 if q == 0 else 0.8), q, stages) for q in range(points)]
    for _, q, stage in sorted(work):
        if stage < stages:
            columns = (ga >> (stage + 1)) * width
            coded, token = hop_call(keep[q], heard[q], me, stage, columns, after)
            after = [token]
            heard[q].append(swap(coded, "ga", ga, ga_bits[stage]))
            if (q, stage) == (0, 1):
                for bit in reversed(pair_bits[:-1]):
                    for slot in sorted(heres):
                        heres[slot ^ bit] = swap(behind(heres[slot], token), "pair", pair, bit)
            elif exch is None:
                slots = [(heres[slot][None], 0) for slot in range(pair)]
                after = [behind(token, [c for c, _ in cons])]
                exch, token = exchange_call(slots, there, coulomb, after)
                after = [token]
            if (q, stage) == (points - 1, stages - 1):
                own, sent = (jnp.stack(items) for items in zip(*tiles[:-1]))
                early = fold_call(own, swap(behind(sent, token), "pair", pair, pair_bits[0]))
                after = [behind(token, early[0])]
        else:
            *tiles[q], token = tile_call(
                cons, q, keep[q], heard[q], exch, me, ga_order, pick_rows, col_direct,
                col_exch, pair, after,
            )
            after = [token]

    own, sent = (part[None] for part in tiles[-1])
    late = fold_call(own, swap(sent, "pair", pair, pair_bits[0]))
    outs = []
    for own, sent in (early, late):
        for bit in pair_bits[1:-1]:
            own, sent = fold_call(own, swap(sent, "pair", pair, bit))
        total = pack_call(own, swap(sent, "pair", pair, pair_bits[-1]))
        for bit in ga_bits:
            size = total.shape[0] // 2
            total = total[:size] + swap(total[size:], "ga", ga, bit)
        outs.append(total[0])
    out = jnp.concatenate(outs).reshape(points, row_count, 2, 64)[..., :col_count]
    return jnp.transpose(out, (0, 2, 1, 3))


def contract_float(left, right):
    high = lax.Precision.HIGHEST
    real_part = jnp.einsum(
        "nkg,mkg->nkm", left[:, :, 0], right[:, :, 0], precision=high
    ) - jnp.einsum("nkg,mkg->nkm", left[:, :, 1], right[:, :, 1], precision=high)
    imag_part = jnp.einsum(
        "nkg,mkg->nkm", left[:, :, 0], right[:, :, 1], precision=high
    ) + jnp.einsum("nkg,mkg->nkm", left[:, :, 1], right[:, :, 0], precision=high)
    return jnp.stack([real_part, imag_part], axis=2)


def times_cols(rows, weights):
    first = jnp.einsum(
        "nkh,kgh->nkg", rows[:, :, 0], weights[:, 0], preferred_element_type=jnp.float32
    ) - jnp.einsum("nkh,kgh->nkg", rows[:, :, 1], weights[:, 1], preferred_element_type=jnp.float32)
    second = jnp.einsum(
        "nkh,kgh->nkg", rows[:, :, 0], weights[:, 1], preferred_element_type=jnp.float32
    ) + jnp.einsum("nkh,kgh->nkg", rows[:, :, 1], weights[:, 0], preferred_element_type=jnp.float32)
    return jnp.stack([first, second], axis=2)


def on_any_device(
    val_density, con_density, screened, coulomb, trans_here, trans_there, shift_map, ordering
):
    con_count = con_density.shape[0]
    points = con_density.shape[1]
    slab_cols = con_density.shape[3]
    blocks = slab_cols // GBLK
    within = (shift_map % GBLK).reshape(points, blocks, GBLK)
    onehot = (
        within[:, :, :, None] == jnp.arange(GBLK, dtype=jnp.int32)[None, None, None, :]
    ).astype(jnp.bfloat16)
    con_blocks = con_density.reshape(con_count, points, 2, blocks, GBLK)
    shifted = (
        jnp.einsum("bkpnh,kngh->bkpng", con_blocks, onehot, preferred_element_type=jnp.float32)
        .astype(jnp.bfloat16)
        .reshape(con_density.shape)
    )
    whole_here = lax.all_gather(trans_here, "pair", axis=0, tiled=True).astype(jnp.float32)
    weighted = trans_there.astype(jnp.float32) * coulomb[None, :, None, :]
    high = lax.Precision.HIGHEST
    exch_real = jnp.einsum(
        "tg,skg->tks", whole_here[:, 0], weighted[:, :, 0], precision=high
    ) - jnp.einsum("tg,skg->tks", whole_here[:, 1], weighted[:, :, 1], precision=high)
    exch_imag = jnp.einsum(
        "tg,skg->tks", whole_here[:, 0], weighted[:, :, 1], precision=high
    ) + jnp.einsum("tg,skg->tks", whole_here[:, 1], weighted[:, :, 0], precision=high)
    exch_part = jnp.stack([exch_real, exch_imag], axis=2)
    whole_con = lax.all_gather(shifted, "ga", axis=0, tiled=True)
    screened_rows = lax.psum_scatter(
        times_cols(whole_con, screened), "pair", scatter_dimension=0, tiled=True
    )
    direct_part = contract_float(
        lax.all_gather(val_density, "pair", axis=0, tiled=True).astype(jnp.float32), screened_rows
    )
    direct_sum, exch_sum = lax.psum((direct_part, exch_part), "ga")
    direct_full, exch_full = (
        lax.all_gather(direct_sum, "pair", axis=3, tiled=True),
        lax.all_gather(exch_sum, "pair", axis=3, tiled=True),
    )
    row_count = NT // lax.axis_size("pair")
    col_count = NT // lax.axis_size("ga")
    row_trans = lax.dynamic_slice_in_dim(ordering, lax.axis_index("pair") * row_count, row_count, 0)
    col_trans = lax.dynamic_slice_in_dim(ordering, lax.axis_index("ga") * col_count, col_count, 0)
    row_pairs = (row_trans // NC)[:, None] * NV + (col_trans // NC)[None, :]
    col_pairs = (row_trans % NC)[:, None] * NC + (col_trans % NC)[None, :]
    picked = direct_full[row_pairs.reshape(-1)]
    col_mask = (
        col_pairs.reshape(-1)[:, None] == jnp.arange(direct_full.shape[3], dtype=jnp.int32)[None, :]
    ).astype(jnp.float32)
    direct_flat = jnp.sum(picked * col_mask[:, None, None, :], axis=3)
    direct_sel = jnp.transpose(direct_flat.reshape(row_count, col_count, points, 2), (2, 3, 0, 1))
    exch_picked = exch_full[row_trans]
    col_hot = (jnp.arange(NT, dtype=jnp.int32)[:, None] == col_trans[None, :]).astype(jnp.float32)
    exch_sel = jnp.einsum("rkpt,tc->kprc", exch_picked, col_hot, precision=high)
    return 2.0 * exch_sel - direct_sel


def solution(mesh):
    in_specs = (
        P("pair", None, None, "ga"),
        P("ga", None, None, "pair"),
        P(None, None, "ga", "pair"),
        P(None, "ga"),
        P("pair", None, "ga"),
        P("pair", None, None, "ga"),
        P(None, "pair"),
        P(),
    )
    out_specs = P(None, None, "pair", "ga")

    def run(*args):
        ga, pair = mesh.shape["ga"], mesh.shape["pair"]
        con_count, h_count = args[1].shape[0], args[1].shape[3]
        suits = (
            ga & (ga - 1) == 0
            and pair & (pair - 1) == 0
            and ga >= 4
            and pair >= 4
            and NT % (pair * GROUP // 2) == 0
            and h_count % (ga * pair * GBLK) == 0
            and con_count % (8 * ga) == 0
            and args[0].shape[0] % (16 * pair) == 0
            and NT % (16 * pair) == 0
            and NT // ga <= 64
        )
        body = on_device if suits else on_any_device
        return jax.shard_map(
            body, mesh=mesh, in_specs=in_specs, out_specs=out_specs, check_vma=False
        )(*args)

    return run
```

```python
import jax
import jax.numpy as jnp
from jax import lax
from jax.experimental import pallas as pl
from jax.experimental.pallas import tpu as pltpu
from jax.sharding import PartitionSpec as P

NV = 16
NC = 24
GBLK = 128
NT = 384

GROUP = 64
EXP_ROWS = 16
STEPS = 128.0
TOP = 32700.0
MAGIC = 1.5 * 2.0**23
NT_DIMS = (((1,), (1,)), ((), ()))
VMEM = 40 * 1024 * 1024


TOKEN = jax.ShapeDtypeStruct((8, 128), jnp.float32)


def params():
    return pltpu.CompilerParams(vmem_limit_bytes=VMEM)


def cost(flops, moved):
    return pl.CostEstimate(flops=int(flops) // 64, bytes_accessed=int(moved) // 64, transcendentals=0)


def mm(left, right):
    return jnp.dot(left, right, preferred_element_type=jnp.float32)


def mm_nt(left, right):
    return lax.dot_general(left, right, NT_DIMS, preferred_element_type=jnp.float32)


def halves(value):
    high = value.astype(jnp.bfloat16)
    low = (value - high.astype(jnp.float32)).astype(jnp.bfloat16)
    return high, low


def encode(value, out_ref):
    rows, width = value.shape
    groups = rows // GROUP
    parts = value.reshape(groups, GROUP, width)
    largest = jnp.maximum(jnp.max(jnp.abs(parts), axis=1), 1e-30)
    level = jnp.ceil(jnp.log2(largest) * STEPS) + 1.0
    factor = TOP * jnp.exp2(level * (-1.0 / STEPS))
    coded = ((parts * factor[:, None, :] + MAGIC) - MAGIC).astype(jnp.int32)
    out_ref[0:rows, :] = coded.reshape(rows, width).astype(jnp.int16)
    pad = jnp.zeros((EXP_ROWS - groups, width), jnp.int32)
    out_ref[rows : rows + EXP_ROWS, :] = jnp.concatenate(
        [level.astype(jnp.int32), pad], axis=0
    ).astype(jnp.int16)


def decode(ref):
    rows = ref.shape[0] - EXP_ROWS
    width = ref.shape[1]
    groups = rows // GROUP
    level = ref[rows : rows + EXP_ROWS, :].astype(jnp.int32).astype(jnp.float32)[0:groups]
    factor = jnp.exp2(level * (1.0 / STEPS)) * (1.0 / TOP)
    parts = ref[0:rows, :].astype(jnp.int32).astype(jnp.float32).reshape(groups, GROUP, width)
    return (parts * factor[:, None, :]).reshape(rows, width)


def reversed_bits(number, count):
    return sum(((number // (1 << b)) % 2) * (1 << (count - 1 - b)) for b in range(count))


def block_of(me, known, stop, flip):
    number = 0
    for bit in range(known, stop):
        flag = (me // (1 << bit)) % 2
        number = 2 * number + (1 - flag if flip and bit == stop - 1 else flag)
    return number


def shift_kernel(order, me_ref, con_ref, map_ref, *refs):
    *stay_refs, go_ref, token_ref = refs
    half, _, _, rows, width = go_ref.shape
    count = len(order).bit_length() - 1
    token_ref[...] = jnp.zeros_like(token_ref)
    for p, slot in enumerate(order):
        out_ref = stay_refs[p].at[0] if p < half else go_ref.at[p - half]
        first = reversed_bits(jnp.bitwise_xor(me_ref[0], slot), count) * width
        for block in range(width // GBLK):
            cols = pl.ds(pl.multiple_of(first + block * GBLK, GBLK), GBLK)
            within = jnp.bitwise_and(map_ref[0, 0:1, cols], GBLK - 1)
            within = jnp.broadcast_to(within, (rows, GBLK))
            for part in range(2):
                values = con_ref[0, part, :, cols].astype(jnp.float32)
                moved = jnp.take_along_axis(values, within, axis=1)
                out_ref[0, part, :, block * GBLK : (block + 1) * GBLK] = moved.astype(jnp.bfloat16)


def shift_call(con, shift_map, me, order, width):
    points, _, rows, slab = con.shape
    half = len(order) // 2
    counts = [1] * half + [half]
    grid_spec = pltpu.PrefetchScalarGridSpec(
        num_scalar_prefetch=1,
        grid=(points,),
        in_specs=[
            pl.BlockSpec((1, 2, rows, slab), lambda q, me: (q, 0, 0, 0)),
            pl.BlockSpec((1, 1, slab), lambda q, me: (q, 0, 0)),
        ],
        out_specs=[
            pl.BlockSpec((n, 1, 2, rows, width), lambda q, me: (0, q, 0, 0, 0)) for n in counts
        ]
        + [pl.BlockSpec(TOKEN.shape, lambda q, me: (0, 0))],
    )
    return pl.pallas_call(
        lambda *refs: shift_kernel(order, *refs),
        grid_spec=grid_spec,
        out_shape=[
            jax.ShapeDtypeStruct((n, points, 2, rows, width), jnp.bfloat16) for n in counts
        ]
        + [TOKEN],
        compiler_params=params(),
        cost_estimate=cost(8 * con.size, 4 * con.size),
    )(me, con, shift_map.reshape(points, 1, slab))


def x_kernel(slots, waits, me_ref, *refs):
    val_refs, weight_ref = refs[:slots], refs[slots]
    go_ref, keep_ref, token_ref, left_ref = refs[slots + 1 + waits :]
    _, _, _, rows, depth = val_refs[0].shape
    half = slots * rows
    token_ref[...] = jnp.zeros_like(token_ref)
    step = pl.program_id(0)
    halfway = pl.num_programs(0) // 2

    @pl.when(step == 0)
    def _():
        for slot in range(slots):
            real, imag = val_refs[slot][0, 0, 0], val_refs[slot][0, 0, 1]
            top = slice(slot * rows, (slot + 1) * rows)
            low = slice(half + slot * rows, half + (slot + 1) * rows)
            left_ref[top, 0:depth] = real
            left_ref[top, depth : 2 * depth] = -imag
            left_ref[low, 0:depth] = imag
            left_ref[low, depth : 2 * depth] = real

    weight = weight_ref[0].reshape(2 * depth, weight_ref.shape[3])

    @pl.when(step < halfway)
    def _():
        encode(mm(left_ref[...], weight), go_ref)

    @pl.when(step >= halfway)
    def _():
        keep_ref[...] = mm(left_ref[...], weight)


def x_call(vals, screened, place, point, me, steps, after):
    slots = len(vals)
    _, _, _, rows, depth = vals[0][0].shape
    height = 2 * slots * rows
    columns = screened.shape[3] // 2
    half = steps // 2
    width = columns // half
    grid_spec = pltpu.PrefetchScalarGridSpec(
        num_scalar_prefetch=1,
        grid=(steps,),
        in_specs=[
            pl.BlockSpec((1, 1, 2, rows, depth), lambda j, me, slot=slot: (slot, place, 0, 0, 0))
            for _, slot in vals
        ]
        + [
            pl.BlockSpec(
                (1, 2, depth, width),
                lambda j, me: (point, 0, 0, ((me[0] + 1 + j // half) % 2) * half + j % half),
            )
        ]
        + [pl.BlockSpec(memory_space=pl.ANY) for _ in after],
        out_specs=[
            pl.BlockSpec((height + EXP_ROWS, width), lambda j, me: (0, jnp.minimum(j, half - 1))),
            pl.BlockSpec((height, width), lambda j, me: (0, jnp.maximum(j - half, 0))),
            pl.BlockSpec(TOKEN.shape, lambda j, me: (0, 0)),
        ],
        scratch_shapes=[pltpu.VMEM((height, 2 * depth), jnp.bfloat16)],
    )
    return pl.pallas_call(
        lambda *refs: x_kernel(slots, len(after), *refs),
        grid_spec=grid_spec,
        out_shape=[
            jax.ShapeDtypeStruct((height + EXP_ROWS, columns), jnp.int16),
            jax.ShapeDtypeStruct((height, columns), jnp.float32),
            TOKEN,
        ],
        compiler_params=params(),
        cost_estimate=cost(
            2 * height * 2 * depth * 2 * columns, 8 * depth * columns + 6 * height * columns
        ),
    )(me, *[v for v, _ in vals], screened, *after)


def hop_kernel(heard, me_ref, keep_ref, *refs):
    total = keep_ref[...]
    for ref in refs[:heard]:
        total = total + decode(ref)
    out_ref, token_ref = refs[-2:]
    encode(total, out_ref)
    token_ref[...] = jnp.zeros_like(token_ref)


def hop_call(keep, others, me, stage, width, after):
    height, tall = keep.shape[0], others[0].shape[0]
    steps = width // 128

    def at(known):
        return lambda i, me: (0, block_of(me[0], known, stage + 1, True) * steps + i)

    grid_spec = pltpu.PrefetchScalarGridSpec(
        num_scalar_prefetch=1,
        grid=(steps,),
        in_specs=[pl.BlockSpec((height, 128), at(1))]
        + [pl.BlockSpec((tall, 128), at(n + 1)) for n in range(len(others))]
        + [pl.BlockSpec(memory_space=pl.ANY) for _ in after],
        out_specs=[
            pl.BlockSpec((tall, 128), lambda i, me: (0, i)),
            pl.BlockSpec(TOKEN.shape, lambda i, me: (0, 0)),
        ],
    )
    return pl.pallas_call(
        lambda *refs: hop_kernel(len(others), *refs),
        grid_spec=grid_spec,
        out_shape=[jax.ShapeDtypeStruct((tall, width), jnp.int16), TOKEN],
        compiler_params=params(),
        cost_estimate=cost(20 * height * width, 8 * height * width),
    )(me, keep, *others, *after)


def fold_kernel(own_ref, heard_ref, keep_ref, go_ref):
    rows = keep_ref.shape[1]
    for n in range(own_ref.shape[0]):
        total = own_ref[n] + decode(heard_ref.at[n])
        keep_ref[n] = total[:rows]
        encode(total[rows:], go_ref.at[n])


def fold_call(own, heard):
    count, rows, cols = own.shape
    shapes = [
        jax.ShapeDtypeStruct((count, rows // 2, cols), jnp.float32),
        jax.ShapeDtypeStruct((count, rows // 2 + EXP_ROWS, cols), jnp.int16),
    ]
    return pl.pallas_call(
        fold_kernel,
        out_shape=shapes,
        compiler_params=params(),
        cost_estimate=cost(20 * own.size, 10 * own.size),
    )(own, heard)


def pack_kernel(own_ref, heard_ref, out_ref):
    rows = out_ref.shape[2]
    first = lax.broadcasted_iota(jnp.int32, (rows, 128), 1) < 64
    for n in range(own_ref.shape[0]):
        total = own_ref[n] + decode(heard_ref.at[n])
        for block in range(out_ref.shape[0] // 2):
            cols = slice(block * 128, (block + 1) * 128)
            real, imag = total[:rows, cols], total[rows:, cols]
            out_ref[2 * block, n] = jnp.where(first, real, pltpu.roll(imag, 64, 1))
            out_ref[2 * block + 1, n] = jnp.where(first, pltpu.roll(real, 64, 1), imag)


def pack_call(own, heard):
    count, rows, cols = own.shape
    return pl.pallas_call(
        pack_kernel,
        out_shape=jax.ShapeDtypeStruct((cols // 64, count, rows // 2, 128), jnp.float32),
        compiler_params=params(),
        cost_estimate=cost(20 * own.size, 10 * own.size),
    )(own, heard)


def exchange_kernel(slots, waits, *refs):
    here_refs, (there_ref, coulomb_ref) = refs[:slots], refs[slots : slots + 2]
    out_ref, token_ref, left_ref = refs[slots + 2 + waits :]
    _, _, rows, depth = here_refs[0].shape
    token_ref[...] = jnp.zeros_like(token_ref)

    @pl.when(pl.program_id(0) == 0)
    def _():
        for slot in range(slots):
            for part in range(2):
                left_ref[
                    slot * rows : (slot + 1) * rows, part * depth : (part + 1) * depth
                ] = here_refs[slot][0, part]

    factor = coulomb_ref[0]
    real = there_ref[0, 0].astype(jnp.float32) * factor
    imag = there_ref[0, 1].astype(jnp.float32) * factor
    right = jnp.concatenate(
        [jnp.concatenate([real, -imag], axis=1), jnp.concatenate([imag, real], axis=1)], axis=0
    )
    high, low = halves(right)
    left = left_ref[...]
    both = mm_nt(left, high) + mm_nt(left, low)
    cols = both.shape[1] // 2
    for part in range(2):
        out_ref[0, part] = both[:, part * cols : (part + 1) * cols]


def exchange_call(heres, there, coulomb, after):
    slots, rows = len(heres), heres[0][0].shape[2]
    points, _, cols, depth = there.shape
    height = slots * rows
    return pl.pallas_call(
        lambda *refs: exchange_kernel(slots, len(after), *refs),
        grid=(points,),
        in_specs=[
            pl.BlockSpec((1,) + h.shape[1:], lambda q, slot=slot: (slot, 0, 0, 0))
            for h, slot in heres
        ]
        + [
            pl.BlockSpec((1, 2, cols, depth), lambda q: (q, 0, 0, 0)),
            pl.BlockSpec((1, 1, depth), lambda q: (q, 0, 0)),
        ]
        + [pl.BlockSpec(memory_space=pl.ANY) for _ in after],
        out_specs=[
            pl.BlockSpec((1, 2, height, cols), lambda q: (q, 0, 0, 0)),
            pl.BlockSpec(TOKEN.shape, lambda q: (0, 0)),
        ],
        out_shape=[jax.ShapeDtypeStruct((points, 2, height, cols), jnp.float32), TOKEN],
        scratch_shapes=[pltpu.VMEM((height, 2 * depth), jnp.bfloat16)],
        compiler_params=params(),
        cost_estimate=cost(2 * points * height * 2 * cols * 2 * depth * 2, 8 * points * cols * depth),
    )(*[h for h, _ in heres], there, coulomb.reshape(points, 1, depth), *after)


def tile_kernel(order, heard, chunks, waits, me_ref, *refs):
    slots = len(order)
    con_refs, keep_ref = refs[:slots], refs[slots]
    heard_refs = refs[slots + 1 : slots + 1 + heard]
    exch_ref, row_ref, col_direct_ref, col_exch_ref = refs[slots + 1 + heard : slots + 5 + heard]
    keep_out, go_out, token_ref, con_all, direct_ref, natural_ref, sums_ref = refs[
        slots + 5 + heard + waits :
    ]
    token_ref[...] = jnp.zeros_like(token_ref)
    total = keep_ref[...]
    for ref in heard_refs:
        total = total + decode(ref)
    pairs, width = total.shape[0] // 2, total.shape[1]
    rows = con_refs[0].shape[3]
    pitch = con_all.shape[0] // slots
    for slot in range(slots):
        for part in range(2):
            con_all[
                slot * pitch : slot * pitch + rows, part * width : (part + 1) * width
            ] = con_refs[slot][0, 0, part]
    real, imag = total[:pairs], total[pairs:]
    right = jnp.concatenate(
        [jnp.concatenate([real, -imag], axis=1), jnp.concatenate([imag, real], axis=1)], axis=0
    )
    high, low = halves(right)
    left = con_all[...]
    direct = mm_nt(left, high) + mm_nt(left, low)
    lanes = direct_ref.shape[0]
    for slot in range(slots):
        start = pl.multiple_of(jnp.bitwise_xor(me_ref[0], order[slot]) * rows, 8)
        for lane in range(lanes):
            direct_ref[lane, pl.ds(start, rows), :] = direct[
                slot * pitch : slot * pitch + rows, lane * 128 : (lane + 1) * 128
            ]
    group = 128 // NV
    place = lax.broadcasted_iota(jnp.int32, (NC, 128), 1) // NV
    per_part = lanes // 2
    for part in range(2):
        for chunk in range(NC // group):
            for band in range(NV):
                block = jnp.zeros((NC, 128), jnp.float32)
                for step in range(group):
                    e = chunk * group + step
                    piece = direct_ref[part * per_part + band // group, pl.ds(e, NC, stride=NC), :]
                    turn = (NV * (step - band)) % 128
                    if turn:
                        piece = pltpu.roll(piece, turn, 1)
                    block = jnp.where(place == step, piece, block)
                natural_ref[
                    part, band * NC : (band + 1) * NC, chunk * 128 : (chunk + 1) * 128
                ] = block
    pick_rows = row_ref[...]
    count = NT // chunks
    for part in range(2):
        result = None
        for source, pick_cols in (
            (natural_ref[part], col_direct_ref),
            (exch_ref[0, part], col_exch_ref),
        ):
            for piece in halves(source):
                moved = mm(pick_rows, piece).astype(jnp.bfloat16)
                term = mm(moved, pick_cols[...])
                result = term if result is None else result + term
        for chunk in range(chunks):
            at = (2 * chunk + part) * count
            sums_ref[at : at + count, :] = result[chunk * count : (chunk + 1) * count]
    stays = keep_out.shape[0]
    keep_out[...] = sums_ref[0:stays, :]
    encode(sums_ref[stays:, :], go_out)


def tile_call(
    cons, point, keep, heard, exch, me, order, pick_rows, col_direct, col_exch, chunks, after
):
    slots = len(cons)
    _, _, _, rows, width = cons[0][0].shape
    height, tall = keep.shape[0], heard[0].shape[0]
    pitch = -(-rows // 16) * 16
    out_cols = col_direct.shape[1]
    stages = len(heard)
    whole = lambda a: pl.BlockSpec(a.shape, lambda i, me: (0,) * len(a.shape))
    shapes = [
        jax.ShapeDtypeStruct((NT, out_cols), jnp.float32),
        jax.ShapeDtypeStruct((NT + EXP_ROWS, out_cols), jnp.int16),
        TOKEN,
    ]

    def at(known):
        return lambda i, me: (0, block_of(me[0], known, stages, False))

    grid_spec = pltpu.PrefetchScalarGridSpec(
        num_scalar_prefetch=1,
        grid=(1,),
        in_specs=[
            pl.BlockSpec((1, 1, 2, rows, width), lambda i, me, place=place: (place, point, 0, 0, 0))
            for _, place in cons
        ]
        + [pl.BlockSpec((height, width), at(1))]
        + [pl.BlockSpec((tall, width), at(n + 1)) for n in range(stages)]
        + [
            pl.BlockSpec((1,) + exch.shape[1:], lambda i, me: (point, 0, 0, 0)),
            whole(pick_rows),
            whole(col_direct),
            whole(col_exch),
        ]
        + [pl.BlockSpec(memory_space=pl.ANY) for _ in after],
        out_specs=[whole(a) for a in shapes],
        scratch_shapes=[
            pltpu.VMEM((slots * pitch, 2 * width), jnp.bfloat16),
            pltpu.VMEM((height // 128, NC * NC, 128), jnp.float32),
            pltpu.VMEM((2, NT, NT), jnp.float32),
            pltpu.VMEM((2 * NT, out_cols), jnp.float32),
        ],
    )
    return pl.pallas_call(
        lambda *refs: tile_kernel(order, stages, chunks, len(after), *refs),
        grid_spec=grid_spec,
        out_shape=shapes,
        compiler_params=params(),
        cost_estimate=cost(2.8e9, 8e6),
    )(me, *[c for c, _ in cons], keep, *heard, exch, pick_rows, col_direct, col_exch, *after)


def swap(value, axis, size, bit):
    return lax.ppermute(value, axis, [(i, i ^ bit) for i in range(size)])


def halving_order(bits):
    order = [0]
    for bit in reversed(bits):
        order = order + [o ^ bit for o in order]
    return order


def behind(value, token):
    return lax.optimization_barrier((value, token))[0]


def on_device(*args):
    (val_density, con_density, screened, coulomb, trans_here, trans_there, shift_map, ordering) = args
    ga, pair = lax.axis_size("ga"), lax.axis_size("pair")
    points = con_density.shape[1]
    slab = con_density.shape[3]
    width = slab // ga
    me_ga, me_pair = lax.axis_index("ga"), lax.axis_index("pair")
    me = me_ga.astype(jnp.int32).reshape(1)
    ga_bits = [1 << b for b in range(ga.bit_length() - 1)]
    pair_bits = [1 << b for b in range(pair.bit_length() - 1)]
    ga_order = halving_order(ga_bits)
    stages, half = len(ga_bits), ga // 2

    val = jnp.transpose(val_density, (1, 2, 0, 3))
    vals = {0: val}
    for bit in reversed(pair_bits):
        for slot in sorted(vals):
            vals[slot ^ bit] = swap(vals[slot], "pair", pair, bit)

    con = jnp.transpose(behind(con_density, val), (1, 2, 0, 3))
    *stay, go, token = shift_call(con, shift_map, me, ga_order, width)
    nearest = ga_bits[0]
    from_near = swap(go, "ga", ga, nearest)
    cons = {0: (stay[0], 0)}
    for slot, block in zip(ga_order[1:half], stay[1:]):
        cons[slot] = (swap(block, "ga", ga, slot), 0)

    row_count, col_count = NT // pair, NT // ga
    row_slots = jnp.asarray(halving_order(pair_bits), jnp.int32)
    row_trans = ordering.reshape(pair, row_count)[me_pair ^ row_slots].reshape(-1)
    at_row = ((row_trans // row_count) ^ me_pair) * row_count + row_trans % row_count
    pick_rows = (at_row[:, None] == jnp.arange(NT, dtype=jnp.int32)[None, :]).astype(jnp.bfloat16)
    col_trans = ordering.reshape(ga, col_count)[me_ga ^ jnp.asarray(ga_order, jnp.int32)]
    col_trans = jnp.pad(col_trans, ((0, 0), (0, 64 - col_count)), constant_values=-1).reshape(1, -1)
    real_col = col_trans >= 0
    at_direct = jnp.where(real_col, (col_trans % NC) * NV + col_trans // NC, -1)
    own_col = real_col & (col_trans // row_count == me_pair)
    at_exch = jnp.where(own_col, col_trans % row_count, -1)

    def pick_cols(at, size, scale):
        hot = at == jnp.arange(size, dtype=jnp.int32)[:, None]
        return jnp.where(hot, scale, 0.0).astype(jnp.bfloat16)

    col_direct, col_exch = pick_cols(at_direct, NT, -1.0), pick_cols(at_exch, row_count, 2.0)

    there = jnp.transpose(trans_there, (1, 2, 0, 3))
    here = jnp.transpose(behind(trans_here, vals[pair // 2]), (1, 0, 2))
    heres = {0: here, pair // 2: swap(here, "pair", pair, pair // 2)}
    arrived = [cons[slot][0] for slot in ga_order[:half]]
    token = behind(token, (there, pick_rows, col_direct, col_exch, from_near, arrived))
    gone, keep = [], []
    for q in range(points):
        coded, own, token = x_call(
            [(vals[slot][None], 0) for slot in range(pair)], screened, q, q, me, 4, [token]
        )
        gone.append(coded)
        keep.append(own)
        if q == 0:
            from_near = behind(from_near, token)
            for place, slot in enumerate(ga_order[half:]):
                cons[slot] = (from_near, 0)
                if slot != nearest:
                    moved = swap(from_near[place : place + 1], "ga", ga, slot ^ nearest)
                    cons[slot] = (moved, 0)
        elif q == 1:
            token = behind(token, heres[pair // 2])
    after = [behind(token, [cons[slot][0] for slot in ga_order[half:]])]
    cons = [cons[slot] for slot in ga_order]

    heard = [[swap(gone[q], "ga", ga, ga_bits[0])] for q in range(points)]
    tiles = [None] * points
    exch = None
    work = [(2 * q + stage, q, stage) for q in range(points) for stage in range(1, stages)]
    work += [(2 * q + stages + (2.2 if q == 0 else 0.8), q, stages) for q in range(points)]
    for _, q, stage in sorted(work):
        if stage < stages:
            columns = (ga >> (stage + 1)) * width
            if q > 0 and stage == stages - 1:
                after = [behind(after[0], heard[q - 1][-1])]
            coded, token = hop_call(keep[q], heard[q], me, stage, columns, after)
            after = [token]
            heard[q].append(swap(coded, "ga", ga, ga_bits[stage]))
            if (q, stage) == (0, 1):
                for bit in reversed(pair_bits[:-1]):
                    for slot in sorted(heres):
                        heres[slot ^ bit] = swap(behind(heres[slot], token), "pair", pair, bit)
            elif exch is None:
                slots = [(heres[slot][None], 0) for slot in range(pair)]
                after = [behind(token, [c for c, _ in cons])]
                exch, token = exchange_call(slots, there, coulomb, after)
                after = [token]
            if (q, stage) == (points - 1, stages - 1):
                own, sent = (jnp.stack(items) for items in zip(*tiles[:-1]))
                early = fold_call(own, swap(behind(sent, token), "pair", pair, pair_bits[0]))
                after = [behind(token, early[0])]
        else:
            *tiles[q], token = tile_call(
                cons, q, keep[q], heard[q], exch, me, ga_order, pick_rows, col_direct,
                col_exch, pair, after,
            )
            after = [token]

    own, sent = (part[None] for part in tiles[-1])
    late = fold_call(own, swap(sent, "pair", pair, pair_bits[0]))
    outs = []
    for own, sent in (early, late):
        for bit in pair_bits[1:-1]:
            own, sent = fold_call(own, swap(sent, "pair", pair, bit))
        total = pack_call(own, swap(sent, "pair", pair, pair_bits[-1]))
        for bit in ga_bits:
            size = total.shape[0] // 2
            total = total[:size] + swap(total[size:], "ga", ga, bit)
        outs.append(total[0])
    out = jnp.concatenate(outs).reshape(points, row_count, 2, 64)[..., :col_count]
    return jnp.transpose(out, (0, 2, 1, 3))


def contract_float(left, right):
    high = lax.Precision.HIGHEST
    real_part = jnp.einsum(
        "nkg,mkg->nkm", left[:, :, 0], right[:, :, 0], precision=high
    ) - jnp.einsum("nkg,mkg->nkm", left[:, :, 1], right[:, :, 1], precision=high)
    imag_part = jnp.einsum(
        "nkg,mkg->nkm", left[:, :, 0], right[:, :, 1], precision=high
    ) + jnp.einsum("nkg,mkg->nkm", left[:, :, 1], right[:, :, 0], precision=high)
    return jnp.stack([real_part, imag_part], axis=2)


def times_cols(rows, weights):
    first = jnp.einsum(
        "nkh,kgh->nkg", rows[:, :, 0], weights[:, 0], preferred_element_type=jnp.float32
    ) - jnp.einsum("nkh,kgh->nkg", rows[:, :, 1], weights[:, 1], preferred_element_type=jnp.float32)
    second = jnp.einsum(
        "nkh,kgh->nkg", rows[:, :, 0], weights[:, 1], preferred_element_type=jnp.float32
    ) + jnp.einsum("nkh,kgh->nkg", rows[:, :, 1], weights[:, 0], preferred_element_type=jnp.float32)
    return jnp.stack([first, second], axis=2)


def on_any_device(
    val_density, con_density, screened, coulomb, trans_here, trans_there, shift_map, ordering
):
    con_count = con_density.shape[0]
    points = con_density.shape[1]
    slab_cols = con_density.shape[3]
    blocks = slab_cols // GBLK
    within = (shift_map % GBLK).reshape(points, blocks, GBLK)
    onehot = (
        within[:, :, :, None] == jnp.arange(GBLK, dtype=jnp.int32)[None, None, None, :]
    ).astype(jnp.bfloat16)
    con_blocks = con_density.reshape(con_count, points, 2, blocks, GBLK)
    shifted = (
        jnp.einsum("bkpnh,kngh->bkpng", con_blocks, onehot, preferred_element_type=jnp.float32)
        .astype(jnp.bfloat16)
        .reshape(con_density.shape)
    )
    whole_here = lax.all_gather(trans_here, "pair", axis=0, tiled=True).astype(jnp.float32)
    weighted = trans_there.astype(jnp.float32) * coulomb[None, :, None, :]
    high = lax.Precision.HIGHEST
    exch_real = jnp.einsum(
        "tg,skg->tks", whole_here[:, 0], weighted[:, :, 0], precision=high
    ) - jnp.einsum("tg,skg->tks", whole_here[:, 1], weighted[:, :, 1], precision=high)
    exch_imag = jnp.einsum(
        "tg,skg->tks", whole_here[:, 0], weighted[:, :, 1], precision=high
    ) + jnp.einsum("tg,skg->tks", whole_here[:, 1], weighted[:, :, 0], precision=high)
    exch_part = jnp.stack([exch_real, exch_imag], axis=2)
    whole_con = lax.all_gather(shifted, "ga", axis=0, tiled=True)
    screened_rows = lax.psum_scatter(
        times_cols(whole_con, screened), "pair", scatter_dimension=0, tiled=True
    )
    direct_part = contract_float(
        lax.all_gather(val_density, "pair", axis=0, tiled=True).astype(jnp.float32), screened_rows
    )
    direct_sum, exch_sum = lax.psum((direct_part, exch_part), "ga")
    direct_full, exch_full = (
        lax.all_gather(direct_sum, "pair", axis=3, tiled=True),
        lax.all_gather(exch_sum, "pair", axis=3, tiled=True),
    )
    row_count = NT // lax.axis_size("pair")
    col_count = NT // lax.axis_size("ga")
    row_trans = lax.dynamic_slice_in_dim(ordering, lax.axis_index("pair") * row_count, row_count, 0)
    col_trans = lax.dynamic_slice_in_dim(ordering, lax.axis_index("ga") * col_count, col_count, 0)
    row_pairs = (row_trans // NC)[:, None] * NV + (col_trans // NC)[None, :]
    col_pairs = (row_trans % NC)[:, None] * NC + (col_trans % NC)[None, :]
    picked = direct_full[row_pairs.reshape(-1)]
    col_mask = (
        col_pairs.reshape(-1)[:, None] == jnp.arange(direct_full.shape[3], dtype=jnp.int32)[None, :]
    ).astype(jnp.float32)
    direct_flat = jnp.sum(picked * col_mask[:, None, None, :], axis=3)
    direct_sel = jnp.transpose(direct_flat.reshape(row_count, col_count, points, 2), (2, 3, 0, 1))
    exch_picked = exch_full[row_trans]
    col_hot = (jnp.arange(NT, dtype=jnp.int32)[:, None] == col_trans[None, :]).astype(jnp.float32)
    exch_sel = jnp.einsum("rkpt,tc->kprc", exch_picked, col_hot, precision=high)
    return 2.0 * exch_sel - direct_sel


def solution(mesh):
    in_specs = (
        P("pair", None, None, "ga"),
        P("ga", None, None, "pair"),
        P(None, None, "ga", "pair"),
        P(None, "ga"),
        P("pair", None, "ga"),
        P("pair", None, None, "ga"),
        P(None, "pair"),
        P(),
    )
    out_specs = P(None, None, "pair", "ga")

    def run(*args):
        ga, pair = mesh.shape["ga"], mesh.shape["pair"]
        con_count, h_count = args[1].shape[0], args[1].shape[3]
        suits = (
            ga & (ga - 1) == 0
            and pair & (pair - 1) == 0
            and ga >= 4
            and pair >= 4
            and NT % (pair * GROUP // 2) == 0
            and h_count % (ga * pair * GBLK) == 0
            and con_count % (8 * ga) == 0
            and args[0].shape[0] % (16 * pair) == 0
            and NT % (16 * pair) == 0
            and NT // ga <= 64
        )
        body = on_device if suits else on_any_device
        return jax.shard_map(
            body, mesh=mesh, in_specs=in_specs, out_specs=out_specs, check_vma=False
        )(*args)

    return run
```

```python
import jax
import jax.numpy as jnp
from jax import lax
from jax.experimental import pallas as pl
from jax.experimental.pallas import tpu as pltpu
from jax.sharding import PartitionSpec as P

NV = 16
NC = 24
GBLK = 128
NT = 384

GROUP = 64
EXP_ROWS = 16
SMALL = 32
STEPS = 128.0
TOP = 32700.0
MAGIC = 1.5 * 2.0**23
NT_DIMS = (((1,), (1,)), ((), ()))
VMEM = 40 * 1024 * 1024


TOKEN = jax.ShapeDtypeStruct((8, 128), jnp.float32)


def params():
    return pltpu.CompilerParams(vmem_limit_bytes=VMEM)


def cost(flops, moved):
    return pl.CostEstimate(flops=int(flops) // 64, bytes_accessed=int(moved) // 64, transcendentals=0)


def mm(left, right):
    return jnp.dot(left, right, preferred_element_type=jnp.float32)


def mm_nt(left, right):
    return lax.dot_general(left, right, NT_DIMS, preferred_element_type=jnp.float32)


def halves(value):
    high = value.astype(jnp.bfloat16)
    low = (value - high.astype(jnp.float32)).astype(jnp.bfloat16)
    return high, low


def exp_rows(rows, group):
    return -(-(rows // group) // 16) * 16


def encode(value, out_ref, group=GROUP):
    rows, width = value.shape
    groups = rows // group
    parts = value.reshape(groups, group, width)
    largest = jnp.maximum(jnp.max(jnp.abs(parts), axis=1), 1e-30)
    level = jnp.ceil(jnp.log2(largest) * STEPS) + 1.0
    factor = TOP * jnp.exp2(level * (-1.0 / STEPS))
    coded = ((parts * factor[:, None, :] + MAGIC) - MAGIC).astype(jnp.int32)
    out_ref[0:rows, :] = coded.reshape(rows, width).astype(jnp.int16)
    extra = exp_rows(rows, group)
    level = level.astype(jnp.int32)
    if extra > groups:
        pad = jnp.zeros((extra - groups, width), jnp.int32)
        level = jnp.concatenate([level, pad], axis=0)
    out_ref[rows : rows + extra, :] = level.astype(jnp.int16)


def decode(ref, rows=None, group=GROUP):
    rows = ref.shape[0] - EXP_ROWS if rows is None else rows
    width = ref.shape[1]
    groups = rows // group
    extra = exp_rows(rows, group)
    level = ref[rows : rows + extra, :].astype(jnp.int32).astype(jnp.float32)[0:groups]
    factor = jnp.exp2(level * (1.0 / STEPS)) * (1.0 / TOP)
    parts = ref[0:rows, :].astype(jnp.int32).astype(jnp.float32).reshape(groups, group, width)
    return (parts * factor[:, None, :]).reshape(rows, width)


def reversed_bits(number, count):
    return sum(((number // (1 << b)) % 2) * (1 << (count - 1 - b)) for b in range(count))


def block_of(me, known, stop, flip):
    number = 0
    for bit in range(known, stop):
        flag = (me // (1 << bit)) % 2
        number = 2 * number + (1 - flag if flip and bit == stop - 1 else flag)
    return number


def shift_kernel(order, me_ref, con_ref, map_ref, *refs):
    *stay_refs, go_ref, token_ref = refs
    half, _, _, rows, width = go_ref.shape
    count = len(order).bit_length() - 1
    token_ref[...] = jnp.zeros_like(token_ref)
    for p, slot in enumerate(order):
        out_ref = stay_refs[p].at[0] if p < half else go_ref.at[p - half]
        first = reversed_bits(jnp.bitwise_xor(me_ref[0], slot), count) * width
        for block in range(width // GBLK):
            cols = pl.ds(pl.multiple_of(first + block * GBLK, GBLK), GBLK)
            within = jnp.bitwise_and(map_ref[0, 0:1, cols], GBLK - 1)
            within = jnp.broadcast_to(within, (rows, GBLK))
            for part in range(2):
                values = con_ref[0, part, :, cols].astype(jnp.float32)
                moved = jnp.take_along_axis(values, within, axis=1)
                out_ref[0, part, :, block * GBLK : (block + 1) * GBLK] = moved.astype(jnp.bfloat16)


def shift_call(con, shift_map, me, order, width):
    points, _, rows, slab = con.shape
    half = len(order) // 2
    counts = [1] * half + [half]
    grid_spec = pltpu.PrefetchScalarGridSpec(
        num_scalar_prefetch=1,
        grid=(points,),
        in_specs=[
            pl.BlockSpec((1, 2, rows, slab), lambda q, me: (q, 0, 0, 0)),
            pl.BlockSpec((1, 1, slab), lambda q, me: (q, 0, 0)),
        ],
        out_specs=[
            pl.BlockSpec((n, 1, 2, rows, width), lambda q, me: (0, q, 0, 0, 0)) for n in counts
        ]
        + [pl.BlockSpec(TOKEN.shape, lambda q, me: (0, 0))],
    )
    return pl.pallas_call(
        lambda *refs: shift_kernel(order, *refs),
        grid_spec=grid_spec,
        out_shape=[
            jax.ShapeDtypeStruct((n, points, 2, rows, width), jnp.bfloat16) for n in counts
        ]
        + [TOKEN],
        compiler_params=params(),
        cost_estimate=cost(8 * con.size, 4 * con.size),
    )(me, con, shift_map.reshape(points, 1, slab))


def x_kernel(slots, waits, me_ref, *refs):
    val_refs, weight_ref = refs[:slots], refs[slots]
    go_ref, keep_ref, token_ref, left_ref = refs[slots + 1 + waits :]
    _, _, _, rows, depth = val_refs[0].shape
    half = slots * rows
    token_ref[...] = jnp.zeros_like(token_ref)
    step = pl.program_id(0)
    halfway = pl.num_programs(0) // 2

    @pl.when(step == 0)
    def _():
        for slot in range(slots):
            real, imag = val_refs[slot][0, 0, 0], val_refs[slot][0, 0, 1]
            top = slice(slot * rows, (slot + 1) * rows)
            low = slice(half + slot * rows, half + (slot + 1) * rows)
            left_ref[top, 0:depth] = real
            left_ref[top, depth : 2 * depth] = -imag
            left_ref[low, 0:depth] = imag
            left_ref[low, depth : 2 * depth] = real

    weight = weight_ref[0].reshape(2 * depth, weight_ref.shape[3])

    @pl.when(step < halfway)
    def _():
        encode(mm(left_ref[...], weight), go_ref)

    @pl.when(step >= halfway)
    def _():
        keep_ref[...] = mm(left_ref[...], weight)


def x_call(vals, screened, place, point, me, steps, after):
    slots = len(vals)
    _, _, _, rows, depth = vals[0][0].shape
    height = 2 * slots * rows
    columns = screened.shape[3] // 2
    half = steps // 2
    width = columns // half
    grid_spec = pltpu.PrefetchScalarGridSpec(
        num_scalar_prefetch=1,
        grid=(steps,),
        in_specs=[
            pl.BlockSpec((1, 1, 2, rows, depth), lambda j, me, slot=slot: (slot, place, 0, 0, 0))
            for _, slot in vals
        ]
        + [
            pl.BlockSpec(
                (1, 2, depth, width),
                lambda j, me: (point, 0, 0, ((me[0] + 1 + j // half) % 2) * half + j % half),
            )
        ]
        + [pl.BlockSpec(memory_space=pl.ANY) for _ in after],
        out_specs=[
            pl.BlockSpec((height + EXP_ROWS, width), lambda j, me: (0, jnp.minimum(j, half - 1))),
            pl.BlockSpec((height, width), lambda j, me: (0, jnp.maximum(j - half, 0))),
            pl.BlockSpec(TOKEN.shape, lambda j, me: (0, 0)),
        ],
        scratch_shapes=[pltpu.VMEM((height, 2 * depth), jnp.bfloat16)],
    )
    return pl.pallas_call(
        lambda *refs: x_kernel(slots, len(after), *refs),
        grid_spec=grid_spec,
        out_shape=[
            jax.ShapeDtypeStruct((height + EXP_ROWS, columns), jnp.int16),
            jax.ShapeDtypeStruct((height, columns), jnp.float32),
            TOKEN,
        ],
        compiler_params=params(),
        cost_estimate=cost(
            2 * height * 2 * depth * 2 * columns, 8 * depth * columns + 6 * height * columns
        ),
    )(me, *[v for v, _ in vals], screened, *after)


def hop_kernel(heard, me_ref, keep_ref, *refs):
    total = keep_ref[...]
    for ref in refs[:heard]:
        total = total + decode(ref)
    out_ref, token_ref = refs[-2:]
    encode(total, out_ref)
    token_ref[...] = jnp.zeros_like(token_ref)


def hop_call(keep, others, me, stage, width, after):
    height, tall = keep.shape[0], others[0].shape[0]
    steps = width // 128

    def at(known):
        return lambda i, me: (0, block_of(me[0], known, stage + 1, True) * steps + i)

    grid_spec = pltpu.PrefetchScalarGridSpec(
        num_scalar_prefetch=1,
        grid=(steps,),
        in_specs=[pl.BlockSpec((height, 128), at(1))]
        + [pl.BlockSpec((tall, 128), at(n + 1)) for n in range(len(others))]
        + [pl.BlockSpec(memory_space=pl.ANY) for _ in after],
        out_specs=[
            pl.BlockSpec((tall, 128), lambda i, me: (0, i)),
            pl.BlockSpec(TOKEN.shape, lambda i, me: (0, 0)),
        ],
    )
    return pl.pallas_call(
        lambda *refs: hop_kernel(len(others), *refs),
        grid_spec=grid_spec,
        out_shape=[jax.ShapeDtypeStruct((tall, width), jnp.int16), TOKEN],
        compiler_params=params(),
        cost_estimate=cost(20 * height * width, 8 * height * width),
    )(me, keep, *others, *after)


def fold_kernel(own_ref, heard_ref, keep_ref, go_ref):
    rows = keep_ref.shape[1]
    for n in range(own_ref.shape[0]):
        total = own_ref[n] + decode(heard_ref.at[n])
        keep_ref[n] = total[:rows]
        encode(total[rows:], go_ref.at[n])


def fold_call(own, heard):
    count, rows, cols = own.shape
    shapes = [
        jax.ShapeDtypeStruct((count, rows // 2, cols), jnp.float32),
        jax.ShapeDtypeStruct((count, rows // 2 + EXP_ROWS, cols), jnp.int16),
    ]
    return pl.pallas_call(
        fold_kernel,
        out_shape=shapes,
        compiler_params=params(),
        cost_estimate=cost(20 * own.size, 10 * own.size),
    )(own, heard)


def split_sums(sums_ref, keep_ref, go_ref):
    half, points, rows, width = keep_ref.shape
    keep_ref[...] = sums_ref[0:half]
    encode(sums_ref[half:].reshape(half * points * rows, width), go_ref, SMALL)


def split_shapes(slots, points, rows):
    count = slots // 2 * points * rows
    return [
        jax.ShapeDtypeStruct((slots // 2, points, rows, 128), jnp.float32),
        jax.ShapeDtypeStruct((count + exp_rows(count, SMALL), 128), jnp.int16),
    ]


def pack_kernel(*refs):
    *refs, keep_ref, go_ref, sums_ref = refs
    slots, points, rows, _ = sums_ref.shape
    first = lax.broadcasted_iota(jnp.int32, (rows, 128), 1) < 64
    for n in range(points):
        total = refs[n][...] + decode(refs[points + n])
        for block in range(slots // 2):
            cols = slice(block * 128, (block + 1) * 128)
            real, imag = total[:rows, cols], total[rows:, cols]
            sums_ref[2 * block, n] = jnp.where(first, real, pltpu.roll(imag, 64, 1))
            sums_ref[2 * block + 1, n] = jnp.where(first, pltpu.roll(real, 64, 1), imag)
    split_sums(sums_ref, keep_ref, go_ref)


def pack_call(owns, heards):
    rows, cols = owns[0].shape
    shape = (cols // 64, len(owns), rows // 2)
    return pl.pallas_call(
        pack_kernel,
        out_shape=split_shapes(*shape),
        scratch_shapes=[pltpu.VMEM(shape + (128,), jnp.float32)],
        compiler_params=params(),
        cost_estimate=cost(60 * owns[0].size, 30 * owns[0].size),
    )(*owns, *heards)


def merge_kernel(own_ref, heard_ref, *refs):
    slots, points, rows, width = own_ref.shape
    count = slots * points * rows
    sums_ref = refs[-1]
    heard = decode(heard_ref, count, SMALL)
    sums_ref[...] = own_ref[...] + heard.reshape(slots, points, rows, width)
    if slots > 1:
        split_sums(sums_ref, *refs[:-1])


def merge_call(own, heard):
    last = own.shape[0] == 1
    sums = jax.ShapeDtypeStruct(own.shape, jnp.float32)
    return pl.pallas_call(
        merge_kernel,
        out_shape=sums if last else split_shapes(*own.shape[:3]),
        scratch_shapes=[] if last else [pltpu.VMEM(own.shape, jnp.float32)],
        compiler_params=params(),
        cost_estimate=cost(20 * own.size, 10 * own.size),
    )(own, heard)


def exchange_kernel(slots, waits, *refs):
    here_refs, (there_ref, coulomb_ref) = refs[:slots], refs[slots : slots + 2]
    out_ref, token_ref, left_ref = refs[slots + 2 + waits :]
    _, _, rows, depth = here_refs[0].shape
    token_ref[...] = jnp.zeros_like(token_ref)

    @pl.when(pl.program_id(0) == 0)
    def _():
        for slot in range(slots):
            for part in range(2):
                left_ref[
                    slot * rows : (slot + 1) * rows, part * depth : (part + 1) * depth
                ] = here_refs[slot][0, part]

    factor = coulomb_ref[0]
    real = there_ref[0, 0].astype(jnp.float32) * factor
    imag = there_ref[0, 1].astype(jnp.float32) * factor
    right = jnp.concatenate(
        [jnp.concatenate([real, -imag], axis=1), jnp.concatenate([imag, real], axis=1)], axis=0
    )
    high, low = halves(right)
    left = left_ref[...]
    both = mm_nt(left, high) + mm_nt(left, low)
    cols = both.shape[1] // 2
    for part in range(2):
        out_ref[0, part] = both[:, part * cols : (part + 1) * cols]


def exchange_call(heres, there, coulomb, after):
    slots, rows = len(heres), heres[0][0].shape[2]
    points, _, cols, depth = there.shape
    height = slots * rows
    return pl.pallas_call(
        lambda *refs: exchange_kernel(slots, len(after), *refs),
        grid=(points,),
        in_specs=[
            pl.BlockSpec((1,) + h.shape[1:], lambda q, slot=slot: (slot, 0, 0, 0))
            for h, slot in heres
        ]
        + [
            pl.BlockSpec((1, 2, cols, depth), lambda q: (q, 0, 0, 0)),
            pl.BlockSpec((1, 1, depth), lambda q: (q, 0, 0)),
        ]
        + [pl.BlockSpec(memory_space=pl.ANY) for _ in after],
        out_specs=[
            pl.BlockSpec((1, 2, height, cols), lambda q: (q, 0, 0, 0)),
            pl.BlockSpec(TOKEN.shape, lambda q: (0, 0)),
        ],
        out_shape=[jax.ShapeDtypeStruct((points, 2, height, cols), jnp.float32), TOKEN],
        scratch_shapes=[pltpu.VMEM((height, 2 * depth), jnp.bfloat16)],
        compiler_params=params(),
        cost_estimate=cost(2 * points * height * 2 * cols * 2 * depth * 2, 8 * points * cols * depth),
    )(*[h for h, _ in heres], there, coulomb.reshape(points, 1, depth), *after)


def tile_kernel(order, heard, chunks, waits, me_ref, *refs):
    slots = len(order)
    con_refs, keep_ref = refs[:slots], refs[slots]
    heard_refs = refs[slots + 1 : slots + 1 + heard]
    exch_ref, row_ref, col_direct_ref, col_exch_ref = refs[slots + 1 + heard : slots + 5 + heard]
    keep_out, go_out, token_ref, con_all, direct_ref, natural_ref, sums_ref = refs[
        slots + 5 + heard + waits :
    ]
    token_ref[...] = jnp.zeros_like(token_ref)
    total = keep_ref[...]
    for ref in heard_refs:
        total = total + decode(ref)
    pairs, width = total.shape[0] // 2, total.shape[1]
    rows = con_refs[0].shape[3]
    pitch = con_all.shape[0] // slots
    for slot in range(slots):
        for part in range(2):
            con_all[
                slot * pitch : slot * pitch + rows, part * width : (part + 1) * width
            ] = con_refs[slot][0, 0, part]
    real, imag = total[:pairs], total[pairs:]
    right = jnp.concatenate(
        [jnp.concatenate([real, -imag], axis=1), jnp.concatenate([imag, real], axis=1)], axis=0
    )
    high, low = halves(right)
    left = con_all[...]
    direct = mm_nt(left, high) + mm_nt(left, low)
    lanes = direct_ref.shape[0]
    for slot in range(slots):
        start = pl.multiple_of(jnp.bitwise_xor(me_ref[0], order[slot]) * rows, 8)
        for lane in range(lanes):
            direct_ref[lane, pl.ds(start, rows), :] = direct[
                slot * pitch : slot * pitch + rows, lane * 128 : (lane + 1) * 128
            ]
    group = 128 // NV
    place = lax.broadcasted_iota(jnp.int32, (NC, 128), 1) // NV
    per_part = lanes // 2
    for part in range(2):
        for chunk in range(NC // group):
            for band in range(NV):
                block = jnp.zeros((NC, 128), jnp.float32)
                for step in range(group):
                    e = chunk * group + step
                    piece = direct_ref[part * per_part + band // group, pl.ds(e, NC, stride=NC), :]
                    turn = (NV * (step - band)) % 128
                    if turn:
                        piece = pltpu.roll(piece, turn, 1)
                    block = jnp.where(place == step, piece, block)
                natural_ref[
                    part, band * NC : (band + 1) * NC, chunk * 128 : (chunk + 1) * 128
                ] = block
    pick_rows = row_ref[...]
    count = NT // chunks
    for part in range(2):
        result = None
        for source, pick_cols in (
            (natural_ref[part], col_direct_ref),
            (exch_ref[0, part], col_exch_ref),
        ):
            for piece in halves(source):
                moved = mm(pick_rows, piece).astype(jnp.bfloat16)
                term = mm(moved, pick_cols[...])
                result = term if result is None else result + term
        for chunk in range(chunks):
            at = (2 * chunk + part) * count
            sums_ref[at : at + count, :] = result[chunk * count : (chunk + 1) * count]
    stays = keep_out.shape[0]
    keep_out[...] = sums_ref[0:stays, :]
    encode(sums_ref[stays:, :], go_out)


def tile_call(
    cons, point, keep, heard, exch, me, order, pick_rows, col_direct, col_exch, chunks, after
):
    slots = len(cons)
    _, _, _, rows, width = cons[0][0].shape
    height, tall = keep.shape[0], heard[0].shape[0]
    pitch = -(-rows // 16) * 16
    out_cols = col_direct.shape[1]
    stages = len(heard)
    whole = lambda a: pl.BlockSpec(a.shape, lambda i, me: (0,) * len(a.shape))
    shapes = [
        jax.ShapeDtypeStruct((NT, out_cols), jnp.float32),
        jax.ShapeDtypeStruct((NT + EXP_ROWS, out_cols), jnp.int16),
        TOKEN,
    ]

    def at(known):
        return lambda i, me: (0, block_of(me[0], known, stages, False))

    grid_spec = pltpu.PrefetchScalarGridSpec(
        num_scalar_prefetch=1,
        grid=(1,),
        in_specs=[
            pl.BlockSpec((1, 1, 2, rows, width), lambda i, me, place=place: (place, point, 0, 0, 0))
            for _, place in cons
        ]
        + [pl.BlockSpec((height, width), at(1))]
        + [pl.BlockSpec((tall, width), at(n + 1)) for n in range(stages)]
        + [
            pl.BlockSpec((1,) + exch.shape[1:], lambda i, me: (point, 0, 0, 0)),
            whole(pick_rows),
            whole(col_direct),
            whole(col_exch),
        ]
        + [pl.BlockSpec(memory_space=pl.ANY) for _ in after],
        out_specs=[whole(a) for a in shapes],
        scratch_shapes=[
            pltpu.VMEM((slots * pitch, 2 * width), jnp.bfloat16),
            pltpu.VMEM((height // 128, NC * NC, 128), jnp.float32),
            pltpu.VMEM((2, NT, NT), jnp.float32),
            pltpu.VMEM((2 * NT, out_cols), jnp.float32),
        ],
    )
    return pl.pallas_call(
        lambda *refs: tile_kernel(order, stages, chunks, len(after), *refs),
        grid_spec=grid_spec,
        out_shape=shapes,
        compiler_params=params(),
        cost_estimate=cost(2.8e9, 8e6),
    )(me, *[c for c, _ in cons], keep, *heard, exch, pick_rows, col_direct, col_exch, *after)


def swap(value, axis, size, bit):
    return lax.ppermute(value, axis, [(i, i ^ bit) for i in range(size)])


def halving_order(bits):
    order = [0]
    for bit in reversed(bits):
        order = order + [o ^ bit for o in order]
    return order


def behind(value, token):
    return lax.optimization_barrier((value, token))[0]


def on_device(*args):
    (val_density, con_density, screened, coulomb, trans_here, trans_there, shift_map, ordering) = args
    ga, pair = lax.axis_size("ga"), lax.axis_size("pair")
    points = con_density.shape[1]
    slab = con_density.shape[3]
    width = slab // ga
    me_ga, me_pair = lax.axis_index("ga"), lax.axis_index("pair")
    me = me_ga.astype(jnp.int32).reshape(1)
    ga_bits = [1 << b for b in range(ga.bit_length() - 1)]
    pair_bits = [1 << b for b in range(pair.bit_length() - 1)]
    ga_order = halving_order(ga_bits)
    stages, half = len(ga_bits), ga // 2

    val = jnp.transpose(val_density, (1, 2, 0, 3))
    vals = {0: val}
    for bit in reversed(pair_bits):
        for slot in sorted(vals):
            vals[slot ^ bit] = swap(vals[slot], "pair", pair, bit)

    con = jnp.transpose(behind(con_density, val), (1, 2, 0, 3))
    *stay, go, token = shift_call(con, shift_map, me, ga_order, width)
    nearest = ga_bits[0]
    from_near = swap(go, "ga", ga, nearest)
    cons = {0: (stay[0], 0)}
    for slot, block in zip(ga_order[1:half], stay[1:]):
        cons[slot] = (swap(block, "ga", ga, slot), 0)

    row_count, col_count = NT // pair, NT // ga
    row_slots = jnp.asarray(halving_order(pair_bits), jnp.int32)
    row_trans = ordering.reshape(pair, row_count)[me_pair ^ row_slots].reshape(-1)
    at_row = ((row_trans // row_count) ^ me_pair) * row_count + row_trans % row_count
    pick_rows = (at_row[:, None] == jnp.arange(NT, dtype=jnp.int32)[None, :]).astype(jnp.bfloat16)
    col_trans = ordering.reshape(ga, col_count)[me_ga ^ jnp.asarray(ga_order, jnp.int32)]
    col_trans = jnp.pad(col_trans, ((0, 0), (0, 64 - col_count)), constant_values=-1).reshape(1, -1)
    real_col = col_trans >= 0
    at_direct = jnp.where(real_col, (col_trans % NC) * NV + col_trans // NC, -1)
    own_col = real_col & (col_trans // row_count == me_pair)
    at_exch = jnp.where(own_col, col_trans % row_count, -1)

    def pick_cols(at, size, scale):
        hot = at == jnp.arange(size, dtype=jnp.int32)[:, None]
        return jnp.where(hot, scale, 0.0).astype(jnp.bfloat16)

    col_direct, col_exch = pick_cols(at_direct, NT, -1.0), pick_cols(at_exch, row_count, 2.0)

    there = jnp.transpose(trans_there, (1, 2, 0, 3))
    here = jnp.transpose(behind(trans_here, vals[pair // 2]), (1, 0, 2))
    heres = {0: here, pair // 2: swap(here, "pair", pair, pair // 2)}
    arrived = [cons[slot][0] for slot in ga_order[:half]]
    token = behind(token, (there, pick_rows, col_direct, col_exch, from_near, arrived))
    gone, keep = [], []
    for q in range(points):
        coded, own, token = x_call(
            [(vals[slot][None], 0) for slot in range(pair)], screened, q, q, me, 4, [token]
        )
        gone.append(coded)
        keep.append(own)
        if q == 0:
            from_near = behind(from_near, token)
            for place, slot in enumerate(ga_order[half:]):
                cons[slot] = (from_near, 0)
                if slot != nearest:
                    moved = swap(from_near[place : place + 1], "ga", ga, slot ^ nearest)
                    cons[slot] = (moved, 0)
        elif q == 1:
            token = behind(token, heres[pair // 2])
    after = [behind(token, [cons[slot][0] for slot in ga_order[half:]])]
    cons = [cons[slot] for slot in ga_order]

    heard = [[swap(gone[q], "ga", ga, ga_bits[0])] for q in range(points)]
    tiles = [None] * points
    exch = None
    work = [(2 * q + stage, q, stage) for q in range(points) for stage in range(1, stages)]
    work += [(2 * q + stages + 2.2, q, stages) for q in range(points)]
    for _, q, stage in sorted(work):
        if stage < stages:
            columns = (ga >> (stage + 1)) * width
            if q > 0 and stage == stages - 1:
                after = [behind(after[0], heard[q - 1][-1])]
            coded, token = hop_call(keep[q], heard[q], me, stage, columns, after)
            after = [token]
            heard[q].append(swap(coded, "ga", ga, ga_bits[stage]))
            if (q, stage) == (0, 1):
                for bit in reversed(pair_bits[:-1]):
                    for slot in sorted(heres):
                        heres[slot ^ bit] = swap(behind(heres[slot], token), "pair", pair, bit)
            elif exch is None:
                slots = [(heres[slot][None], 0) for slot in range(pair)]
                after = [behind(token, [c for c, _ in cons])]
                exch, token = exchange_call(slots, there, coulomb, after)
                after = [token]
        else:
            if q == 1:
                after = [behind(after[0], tiles[0][1])]
            own, sent, token = tile_call(
                cons, q, keep[q], heard[q], exch, me, ga_order, pick_rows, col_direct,
                col_exch, pair, after,
            )
            after = [token]
            for bit in pair_bits[:-1]:
                own, sent = fold_call(own[None], swap(sent[None], "pair", pair, bit))
                own, sent = own[0], sent[0]
            tiles[q] = own, swap(sent, "pair", pair, pair_bits[-1])

    own, sent = pack_call(*zip(*tiles))
    for bit in ga_bits[:-1]:
        own, sent = merge_call(own, swap(sent, "ga", ga, bit))
    total = merge_call(own, swap(sent, "ga", ga, ga_bits[-1]))[0]
    out = total.reshape(points, row_count, 2, 64)[..., :col_count]
    return jnp.transpose(out, (0, 2, 1, 3))


def contract_float(left, right):
    high = lax.Precision.HIGHEST
    real_part = jnp.einsum(
        "nkg,mkg->nkm", left[:, :, 0], right[:, :, 0], precision=high
    ) - jnp.einsum("nkg,mkg->nkm", left[:, :, 1], right[:, :, 1], precision=high)
    imag_part = jnp.einsum(
        "nkg,mkg->nkm", left[:, :, 0], right[:, :, 1], precision=high
    ) + jnp.einsum("nkg,mkg->nkm", left[:, :, 1], right[:, :, 0], precision=high)
    return jnp.stack([real_part, imag_part], axis=2)


def times_cols(rows, weights):
    first = jnp.einsum(
        "nkh,kgh->nkg", rows[:, :, 0], weights[:, 0], preferred_element_type=jnp.float32
    ) - jnp.einsum("nkh,kgh->nkg", rows[:, :, 1], weights[:, 1], preferred_element_type=jnp.float32)
    second = jnp.einsum(
        "nkh,kgh->nkg", rows[:, :, 0], weights[:, 1], preferred_element_type=jnp.float32
    ) + jnp.einsum("nkh,kgh->nkg", rows[:, :, 1], weights[:, 0], preferred_element_type=jnp.float32)
    return jnp.stack([first, second], axis=2)


def on_any_device(
    val_density, con_density, screened, coulomb, trans_here, trans_there, shift_map, ordering
):
    con_count = con_density.shape[0]
    points = con_density.shape[1]
    slab_cols = con_density.shape[3]
    blocks = slab_cols // GBLK
    within = (shift_map % GBLK).reshape(points, blocks, GBLK)
    onehot = (
        within[:, :, :, None] == jnp.arange(GBLK, dtype=jnp.int32)[None, None, None, :]
    ).astype(jnp.bfloat16)
    con_blocks = con_density.reshape(con_count, points, 2, blocks, GBLK)
    shifted = (
        jnp.einsum("bkpnh,kngh->bkpng", con_blocks, onehot, preferred_element_type=jnp.float32)
        .astype(jnp.bfloat16)
        .reshape(con_density.shape)
    )
    whole_here = lax.all_gather(trans_here, "pair", axis=0, tiled=True).astype(jnp.float32)
    weighted = trans_there.astype(jnp.float32) * coulomb[None, :, None, :]
    high = lax.Precision.HIGHEST
    exch_real = jnp.einsum(
        "tg,skg->tks", whole_here[:, 0], weighted[:, :, 0], precision=high
    ) - jnp.einsum("tg,skg->tks", whole_here[:, 1], weighted[:, :, 1], precision=high)
    exch_imag = jnp.einsum(
        "tg,skg->tks", whole_here[:, 0], weighted[:, :, 1], precision=high
    ) + jnp.einsum("tg,skg->tks", whole_here[:, 1], weighted[:, :, 0], precision=high)
    exch_part = jnp.stack([exch_real, exch_imag], axis=2)
    whole_con = lax.all_gather(shifted, "ga", axis=0, tiled=True)
    screened_rows = lax.psum_scatter(
        times_cols(whole_con, screened), "pair", scatter_dimension=0, tiled=True
    )
    direct_part = contract_float(
        lax.all_gather(val_density, "pair", axis=0, tiled=True).astype(jnp.float32), screened_rows
    )
    direct_sum, exch_sum = lax.psum((direct_part, exch_part), "ga")
    direct_full, exch_full = (
        lax.all_gather(direct_sum, "pair", axis=3, tiled=True),
        lax.all_gather(exch_sum, "pair", axis=3, tiled=True),
    )
    row_count = NT // lax.axis_size("pair")
    col_count = NT // lax.axis_size("ga")
    row_trans = lax.dynamic_slice_in_dim(ordering, lax.axis_index("pair") * row_count, row_count, 0)
    col_trans = lax.dynamic_slice_in_dim(ordering, lax.axis_index("ga") * col_count, col_count, 0)
    row_pairs = (row_trans // NC)[:, None] * NV + (col_trans // NC)[None, :]
    col_pairs = (row_trans % NC)[:, None] * NC + (col_trans % NC)[None, :]
    picked = direct_full[row_pairs.reshape(-1)]
    col_mask = (
        col_pairs.reshape(-1)[:, None] == jnp.arange(direct_full.shape[3], dtype=jnp.int32)[None, :]
    ).astype(jnp.float32)
    direct_flat = jnp.sum(picked * col_mask[:, None, None, :], axis=3)
    direct_sel = jnp.transpose(direct_flat.reshape(row_count, col_count, points, 2), (2, 3, 0, 1))
    exch_picked = exch_full[row_trans]
    col_hot = (jnp.arange(NT, dtype=jnp.int32)[:, None] == col_trans[None, :]).astype(jnp.float32)
    exch_sel = jnp.einsum("rkpt,tc->kprc", exch_picked, col_hot, precision=high)
    return 2.0 * exch_sel - direct_sel


def solution(mesh):
    in_specs = (
        P("pair", None, None, "ga"),
        P("ga", None, None, "pair"),
        P(None, None, "ga", "pair"),
        P(None, "ga"),
        P("pair", None, "ga"),
        P("pair", None, None, "ga"),
        P(None, "pair"),
        P(),
    )
    out_specs = P(None, None, "pair", "ga")

    def run(*args):
        ga, pair = mesh.shape["ga"], mesh.shape["pair"]
        con_count, h_count = args[1].shape[0], args[1].shape[3]
        suits = (
            ga & (ga - 1) == 0
            and pair & (pair - 1) == 0
            and ga >= 4
            and pair >= 4
            and NT % (pair * GROUP // 2) == 0
            and h_count % (ga * pair * GBLK) == 0
            and con_count % (8 * ga) == 0
            and args[0].shape[0] % (16 * pair) == 0
            and NT % (16 * pair) == 0
            and NT // ga <= 64
            and args[1].shape[1] * NT % (pair * SMALL) == 0
        )
        body = on_device if suits else on_any_device
        return jax.shard_map(
            body, mesh=mesh, in_specs=in_specs, out_specs=out_specs, check_vma=False
        )(*args)

    return run
```

```python
import jax
import jax.numpy as jnp
from jax import lax
from jax.experimental import pallas as pl
from jax.experimental.pallas import tpu as pltpu
from jax.sharding import PartitionSpec as P

NV = 16
NC = 24
GBLK = 128
NT = 384

GROUP = 64
EXP_ROWS = 16
SMALL = 32
STEPS = 128.0
TOP = 32700.0
MAGIC = 1.5 * 2.0**23
NT_DIMS = (((1,), (1,)), ((), ()))
VMEM = 40 * 1024 * 1024


TOKEN = jax.ShapeDtypeStruct((8, 128), jnp.float32)


def params():
    return pltpu.CompilerParams(vmem_limit_bytes=VMEM)


def cost(flops, moved):
    return pl.CostEstimate(flops=int(flops) // 64, bytes_accessed=int(moved) // 64, transcendentals=0)


def mm(left, right):
    return jnp.dot(left, right, preferred_element_type=jnp.float32)


def mm_nt(left, right):
    return lax.dot_general(left, right, NT_DIMS, preferred_element_type=jnp.float32)


def halves(value):
    high = value.astype(jnp.bfloat16)
    low = (value - high.astype(jnp.float32)).astype(jnp.bfloat16)
    return high, low


def exp_rows(rows, group):
    return -(-(rows // group) // 16) * 16


def encode(value, out_ref, group=GROUP):
    rows, width = value.shape
    groups = rows // group
    parts = value.reshape(groups, group, width)
    largest = jnp.maximum(jnp.max(jnp.abs(parts), axis=1), 1e-30)
    level = jnp.ceil(jnp.log2(largest) * STEPS) + 1.0
    factor = TOP * jnp.exp2(level * (-1.0 / STEPS))
    coded = ((parts * factor[:, None, :] + MAGIC) - MAGIC).astype(jnp.int32)
    out_ref[0:rows, :] = coded.reshape(rows, width).astype(jnp.int16)
    extra = exp_rows(rows, group)
    level = level.astype(jnp.int32)
    if extra > groups:
        pad = jnp.zeros((extra - groups, width), jnp.int32)
        level = jnp.concatenate([level, pad], axis=0)
    out_ref[rows : rows + extra, :] = level.astype(jnp.int16)


def decode(ref, rows=None, group=GROUP):
    rows = ref.shape[0] - EXP_ROWS if rows is None else rows
    width = ref.shape[1]
    groups = rows // group
    extra = exp_rows(rows, group)
    level = ref[rows : rows + extra, :].astype(jnp.int32).astype(jnp.float32)[0:groups]
    factor = jnp.exp2(level * (1.0 / STEPS)) * (1.0 / TOP)
    parts = ref[0:rows, :].astype(jnp.int32).astype(jnp.float32).reshape(groups, group, width)
    return (parts * factor[:, None, :]).reshape(rows, width)


def reversed_bits(number, count):
    return sum(((number // (1 << b)) % 2) * (1 << (count - 1 - b)) for b in range(count))


def block_of(me, known, stop, flip):
    number = 0
    for bit in range(known, stop):
        flag = (me // (1 << bit)) % 2
        number = 2 * number + (1 - flag if flip and bit == stop - 1 else flag)
    return number


def shift_kernel(order, me_ref, con_ref, map_ref, *refs):
    *stay_refs, go_ref, token_ref = refs
    half, _, _, rows, width = go_ref.shape
    count = len(order).bit_length() - 1
    token_ref[...] = jnp.zeros_like(token_ref)
    for p, slot in enumerate(order):
        out_ref = stay_refs[p].at[0] if p < half else go_ref.at[p - half]
        first = reversed_bits(jnp.bitwise_xor(me_ref[0], slot), count) * width
        for block in range(width // GBLK):
            cols = pl.ds(pl.multiple_of(first + block * GBLK, GBLK), GBLK)
            within = jnp.bitwise_and(map_ref[0, 0:1, cols], GBLK - 1)
            within = jnp.broadcast_to(within, (rows, GBLK))
            for part in range(2):
                values = con_ref[0, part, :, cols].astype(jnp.float32)
                moved = jnp.take_along_axis(values, within, axis=1)
                out_ref[0, part, :, block * GBLK : (block + 1) * GBLK] = moved.astype(jnp.bfloat16)


def shift_call(con, shift_map, me, order, width):
    points, _, rows, slab = con.shape
    half = len(order) // 2
    counts = [1] * half + [half]
    grid_spec = pltpu.PrefetchScalarGridSpec(
        num_scalar_prefetch=1,
        grid=(points,),
        in_specs=[
            pl.BlockSpec((1, 2, rows, slab), lambda q, me: (q, 0, 0, 0)),
            pl.BlockSpec((1, 1, slab), lambda q, me: (q, 0, 0)),
        ],
        out_specs=[
            pl.BlockSpec((n, 1, 2, rows, width), lambda q, me: (0, q, 0, 0, 0)) for n in counts
        ]
        + [pl.BlockSpec(TOKEN.shape, lambda q, me: (0, 0))],
    )
    return pl.pallas_call(
        lambda *refs: shift_kernel(order, *refs),
        grid_spec=grid_spec,
        out_shape=[
            jax.ShapeDtypeStruct((n, points, 2, rows, width), jnp.bfloat16) for n in counts
        ]
        + [TOKEN],
        compiler_params=params(),
        cost_estimate=cost(8 * con.size, 4 * con.size),
    )(me, con, shift_map.reshape(points, 1, slab))


def x_kernel(slots, waits, me_ref, *refs):
    val_refs, weight_ref = refs[:slots], refs[slots]
    go_ref, keep_ref, token_ref, left_ref = refs[slots + 1 + waits :]
    _, _, _, rows, depth = val_refs[0].shape
    half = slots * rows
    token_ref[...] = jnp.zeros_like(token_ref)
    step = pl.program_id(0)
    halfway = pl.num_programs(0) // 2

    @pl.when(step == 0)
    def _():
        for slot in range(slots):
            real, imag = val_refs[slot][0, 0, 0], val_refs[slot][0, 0, 1]
            top = slice(slot * rows, (slot + 1) * rows)
            low = slice(half + slot * rows, half + (slot + 1) * rows)
            left_ref[top, 0:depth] = real
            left_ref[top, depth : 2 * depth] = -imag
            left_ref[low, 0:depth] = imag
            left_ref[low, depth : 2 * depth] = real

    weight = weight_ref[0].reshape(2 * depth, weight_ref.shape[3])

    @pl.when(step < halfway)
    def _():
        encode(mm(left_ref[...], weight), go_ref)

    @pl.when(step >= halfway)
    def _():
        keep_ref[...] = mm(left_ref[...], weight)


def x_call(vals, screened, place, point, me, steps, after):
    slots = len(vals)
    _, _, _, rows, depth = vals[0][0].shape
    height = 2 * slots * rows
    columns = screened.shape[3] // 2
    half = steps // 2
    width = columns // half
    grid_spec = pltpu.PrefetchScalarGridSpec(
        num_scalar_prefetch=1,
        grid=(steps,),
        in_specs=[
            pl.BlockSpec((1, 1, 2, rows, depth), lambda j, me, slot=slot: (slot, place, 0, 0, 0))
            for _, slot in vals
        ]
        + [
            pl.BlockSpec(
                (1, 2, depth, width),
                lambda j, me: (point, 0, 0, ((me[0] + 1 + j // half) % 2) * half + j % half),
            )
        ]
        + [pl.BlockSpec(memory_space=pl.ANY) for _ in after],
        out_specs=[
            pl.BlockSpec((height + EXP_ROWS, width), lambda j, me: (0, jnp.minimum(j, half - 1))),
            pl.BlockSpec((height, width), lambda j, me: (0, jnp.maximum(j - half, 0))),
            pl.BlockSpec(TOKEN.shape, lambda j, me: (0, 0)),
        ],
        scratch_shapes=[pltpu.VMEM((height, 2 * depth), jnp.bfloat16)],
    )
    return pl.pallas_call(
        lambda *refs: x_kernel(slots, len(after), *refs),
        grid_spec=grid_spec,
        out_shape=[
            jax.ShapeDtypeStruct((height + EXP_ROWS, columns), jnp.int16),
            jax.ShapeDtypeStruct((height, columns), jnp.float32),
            TOKEN,
        ],
        compiler_params=params(),
        cost_estimate=cost(
            2 * height * 2 * depth * 2 * columns, 8 * depth * columns + 6 * height * columns
        ),
    )(me, *[v for v, _ in vals], screened, *after)


def hop_kernel(heard, me_ref, keep_ref, *refs):
    total = keep_ref[...]
    for ref in refs[:heard]:
        total = total + decode(ref)
    out_ref, token_ref = refs[-2:]
    encode(total, out_ref)
    token_ref[...] = jnp.zeros_like(token_ref)


def hop_call(keep, others, me, stage, width, after):
    height, tall = keep.shape[0], others[0].shape[0]
    steps = width // 128

    def at(known):
        return lambda i, me: (0, block_of(me[0], known, stage + 1, True) * steps + i)

    grid_spec = pltpu.PrefetchScalarGridSpec(
        num_scalar_prefetch=1,
        grid=(steps,),
        in_specs=[pl.BlockSpec((height, 128), at(1))]
        + [pl.BlockSpec((tall, 128), at(n + 1)) for n in range(len(others))]
        + [pl.BlockSpec(memory_space=pl.ANY) for _ in after],
        out_specs=[
            pl.BlockSpec((tall, 128), lambda i, me: (0, i)),
            pl.BlockSpec(TOKEN.shape, lambda i, me: (0, 0)),
        ],
    )
    return pl.pallas_call(
        lambda *refs: hop_kernel(len(others), *refs),
        grid_spec=grid_spec,
        out_shape=[jax.ShapeDtypeStruct((tall, width), jnp.int16), TOKEN],
        compiler_params=params(),
        cost_estimate=cost(20 * height * width, 8 * height * width),
    )(me, keep, *others, *after)


def fold_kernel(own_ref, heard_ref, keep_ref, go_ref):
    rows = keep_ref.shape[1]
    for n in range(own_ref.shape[0]):
        total = own_ref[n] + decode(heard_ref.at[n])
        keep_ref[n] = total[:rows]
        encode(total[rows:], go_ref.at[n])


def fold_call(own, heard):
    count, rows, cols = own.shape
    shapes = [
        jax.ShapeDtypeStruct((count, rows // 2, cols), jnp.float32),
        jax.ShapeDtypeStruct((count, rows // 2 + EXP_ROWS, cols), jnp.int16),
    ]
    return pl.pallas_call(
        fold_kernel,
        out_shape=shapes,
        compiler_params=params(),
        cost_estimate=cost(20 * own.size, 10 * own.size),
    )(own, heard)


def split_sums(sums_ref, keep_ref, go_ref):
    half, points, rows, width = keep_ref.shape
    keep_ref[...] = sums_ref[0:half]
    encode(sums_ref[half:].reshape(half * points * rows, width), go_ref, SMALL)


def split_shapes(slots, points, rows):
    count = slots // 2 * points * rows
    return [
        jax.ShapeDtypeStruct((slots // 2, points, rows, 128), jnp.float32),
        jax.ShapeDtypeStruct((count + exp_rows(count, SMALL), 128), jnp.int16),
    ]


def pack_kernel(*refs):
    *refs, keep_ref, go_ref, sums_ref = refs
    slots, points, rows, _ = sums_ref.shape
    first = lax.broadcasted_iota(jnp.int32, (rows, 128), 1) < 64
    for n in range(points):
        total = refs[n][...] + decode(refs[points + n])
        for block in range(slots // 2):
            cols = slice(block * 128, (block + 1) * 128)
            real, imag = total[:rows, cols], total[rows:, cols]
            sums_ref[2 * block, n] = jnp.where(first, real, pltpu.roll(imag, 64, 1))
            sums_ref[2 * block + 1, n] = jnp.where(first, pltpu.roll(real, 64, 1), imag)
    split_sums(sums_ref, keep_ref, go_ref)


def pack_call(owns, heards):
    rows, cols = owns[0].shape
    shape = (cols // 64, len(owns), rows // 2)
    return pl.pallas_call(
        pack_kernel,
        out_shape=split_shapes(*shape),
        scratch_shapes=[pltpu.VMEM(shape + (128,), jnp.float32)],
        compiler_params=params(),
        cost_estimate=cost(60 * owns[0].size, 30 * owns[0].size),
    )(*owns, *heards)


def merge_kernel(own_ref, heard_ref, *refs):
    slots, points, rows, width = own_ref.shape
    count = slots * points * rows
    sums_ref = refs[-1]
    heard = decode(heard_ref, count, SMALL)
    sums_ref[...] = own_ref[...] + heard.reshape(slots, points, rows, width)
    if slots > 1:
        split_sums(sums_ref, *refs[:-1])


def merge_call(own, heard):
    last = own.shape[0] == 1
    sums = jax.ShapeDtypeStruct(own.shape, jnp.float32)
    return pl.pallas_call(
        merge_kernel,
        out_shape=sums if last else split_shapes(*own.shape[:3]),
        scratch_shapes=[] if last else [pltpu.VMEM(own.shape, jnp.float32)],
        compiler_params=params(),
        cost_estimate=cost(20 * own.size, 10 * own.size),
    )(own, heard)


def exchange_kernel(slots, waits, *refs):
    here_refs, (there_ref, coulomb_ref) = refs[:slots], refs[slots : slots + 2]
    out_ref, token_ref, left_ref = refs[slots + 2 + waits :]
    _, _, rows, depth = here_refs[0].shape
    token_ref[...] = jnp.zeros_like(token_ref)

    @pl.when(pl.program_id(0) == 0)
    def _():
        for slot in range(slots):
            for part in range(2):
                left_ref[
                    slot * rows : (slot + 1) * rows, part * depth : (part + 1) * depth
                ] = here_refs[slot][0, part]

    factor = coulomb_ref[0]
    real = there_ref[0, 0].astype(jnp.float32) * factor
    imag = there_ref[0, 1].astype(jnp.float32) * factor
    right = jnp.concatenate(
        [jnp.concatenate([real, -imag], axis=1), jnp.concatenate([imag, real], axis=1)], axis=0
    )
    high, low = halves(right)
    left = left_ref[...]
    both = mm_nt(left, high) + mm_nt(left, low)
    cols = both.shape[1] // 2
    for part in range(2):
        out_ref[0, part] = both[:, part * cols : (part + 1) * cols]


def exchange_call(heres, there, coulomb, after):
    slots, rows = len(heres), heres[0][0].shape[2]
    points, _, cols, depth = there.shape
    height = slots * rows
    return pl.pallas_call(
        lambda *refs: exchange_kernel(slots, len(after), *refs),
        grid=(points,),
        in_specs=[
            pl.BlockSpec((1,) + h.shape[1:], lambda q, slot=slot: (slot, 0, 0, 0))
            for h, slot in heres
        ]
        + [
            pl.BlockSpec((1, 2, cols, depth), lambda q: (q, 0, 0, 0)),
            pl.BlockSpec((1, 1, depth), lambda q: (q, 0, 0)),
        ]
        + [pl.BlockSpec(memory_space=pl.ANY) for _ in after],
        out_specs=[
            pl.BlockSpec((1, 2, height, cols), lambda q: (q, 0, 0, 0)),
            pl.BlockSpec(TOKEN.shape, lambda q: (0, 0)),
        ],
        out_shape=[jax.ShapeDtypeStruct((points, 2, height, cols), jnp.float32), TOKEN],
        scratch_shapes=[pltpu.VMEM((height, 2 * depth), jnp.bfloat16)],
        compiler_params=params(),
        cost_estimate=cost(2 * points * height * 2 * cols * 2 * depth * 2, 8 * points * cols * depth),
    )(*[h for h, _ in heres], there, coulomb.reshape(points, 1, depth), *after)


def tile_kernel(order, heard, chunks, waits, me_ref, *refs):
    slots = len(order)
    con_refs, keep_ref = refs[:slots], refs[slots]
    heard_refs = refs[slots + 1 : slots + 1 + heard]
    exch_ref, row_ref, col_direct_ref, col_exch_ref = refs[slots + 1 + heard : slots + 5 + heard]
    keep_out, go_out, token_ref, con_all, direct_ref, natural_ref, sums_ref = refs[
        slots + 5 + heard + waits :
    ]
    token_ref[...] = jnp.zeros_like(token_ref)
    total = keep_ref[...]
    for ref in heard_refs:
        total = total + decode(ref)
    pairs, width = total.shape[0] // 2, total.shape[1]
    rows = con_refs[0].shape[3]
    pitch = con_all.shape[0] // slots
    for slot in range(slots):
        for part in range(2):
            con_all[
                slot * pitch : slot * pitch + rows, part * width : (part + 1) * width
            ] = con_refs[slot][0, 0, part]
    real, imag = total[:pairs], total[pairs:]
    right = jnp.concatenate(
        [jnp.concatenate([real, -imag], axis=1), jnp.concatenate([imag, real], axis=1)], axis=0
    )
    high, low = halves(right)
    left = con_all[...]
    direct = mm_nt(left, high) + mm_nt(left, low)
    lanes = direct_ref.shape[0]
    for slot in range(slots):
        start = pl.multiple_of(jnp.bitwise_xor(me_ref[0], order[slot]) * rows, 8)
        for lane in range(lanes):
            direct_ref[lane, pl.ds(start, rows), :] = direct[
                slot * pitch : slot * pitch + rows, lane * 128 : (lane + 1) * 128
            ]
    group = 128 // NV
    place = lax.broadcasted_iota(jnp.int32, (NC, 128), 1) // NV
    per_part = lanes // 2
    for part in range(2):
        for chunk in range(NC // group):
            for band in range(NV):
                block = jnp.zeros((NC, 128), jnp.float32)
                for step in range(group):
                    e = chunk * group + step
                    piece = direct_ref[part * per_part + band // group, pl.ds(e, NC, stride=NC), :]
                    turn = (NV * (step - band)) % 128
                    if turn:
                        piece = pltpu.roll(piece, turn, 1)
                    block = jnp.where(place == step, piece, block)
                natural_ref[
                    part, band * NC : (band + 1) * NC, chunk * 128 : (chunk + 1) * 128
                ] = block
    pick_rows = row_ref[...]
    count = NT // chunks
    for part in range(2):
        result = None
        for source, pick_cols in (
            (natural_ref[part], col_direct_ref),
            (exch_ref[0, part], col_exch_ref),
        ):
            for piece in halves(source):
                moved = mm(pick_rows, piece).astype(jnp.bfloat16)
                term = mm(moved, pick_cols[...])
                result = term if result is None else result + term
        for chunk in range(chunks):
            at = (2 * chunk + part) * count
            sums_ref[at : at + count, :] = result[chunk * count : (chunk + 1) * count]
    stays = keep_out.shape[0]
    keep_out[...] = sums_ref[0:stays, :]
    encode(sums_ref[stays:, :], go_out)


def tile_call(
    cons, point, keep, heard, exch, me, order, pick_rows, col_direct, col_exch, chunks, after
):
    slots = len(cons)
    _, _, _, rows, width = cons[0][0].shape
    height, tall = keep.shape[0], heard[0].shape[0]
    pitch = -(-rows // 16) * 16
    out_cols = col_direct.shape[1]
    stages = len(heard)
    whole = lambda a: pl.BlockSpec(a.shape, lambda i, me: (0,) * len(a.shape))
    shapes = [
        jax.ShapeDtypeStruct((NT, out_cols), jnp.float32),
        jax.ShapeDtypeStruct((NT + EXP_ROWS, out_cols), jnp.int16),
        TOKEN,
    ]

    def at(known):
        return lambda i, me: (0, block_of(me[0], known, stages, False))

    grid_spec = pltpu.PrefetchScalarGridSpec(
        num_scalar_prefetch=1,
        grid=(1,),
        in_specs=[
            pl.BlockSpec((1, 1, 2, rows, width), lambda i, me, place=place: (place, point, 0, 0, 0))
            for _, place in cons
        ]
        + [pl.BlockSpec((height, width), at(1))]
        + [pl.BlockSpec((tall, width), at(n + 1)) for n in range(stages)]
        + [
            pl.BlockSpec((1,) + exch.shape[1:], lambda i, me: (point, 0, 0, 0)),
            whole(pick_rows),
            whole(col_direct),
            whole(col_exch),
        ]
        + [pl.BlockSpec(memory_space=pl.ANY) for _ in after],
        out_specs=[whole(a) for a in shapes],
        scratch_shapes=[
            pltpu.VMEM((slots * pitch, 2 * width), jnp.bfloat16),
            pltpu.VMEM((height // 128, NC * NC, 128), jnp.float32),
            pltpu.VMEM((2, NT, NT), jnp.float32),
            pltpu.VMEM((2 * NT, out_cols), jnp.float32),
        ],
    )
    return pl.pallas_call(
        lambda *refs: tile_kernel(order, stages, chunks, len(after), *refs),
        grid_spec=grid_spec,
        out_shape=shapes,
        compiler_params=params(),
        cost_estimate=cost(2.8e9, 8e6),
    )(me, *[c for c, _ in cons], keep, *heard, exch, pick_rows, col_direct, col_exch, *after)


def swap(value, axis, size, bit):
    return lax.ppermute(value, axis, [(i, i ^ bit) for i in range(size)])


def halving_order(bits):
    order = [0]
    for bit in reversed(bits):
        order = order + [o ^ bit for o in order]
    return order


def behind(value, token):
    return lax.optimization_barrier((value, token))[0]


def on_device(*args):
    (val_density, con_density, screened, coulomb, trans_here, trans_there, shift_map, ordering) = args
    ga, pair = lax.axis_size("ga"), lax.axis_size("pair")
    points = con_density.shape[1]
    slab = con_density.shape[3]
    width = slab // ga
    me_ga, me_pair = lax.axis_index("ga"), lax.axis_index("pair")
    me = me_ga.astype(jnp.int32).reshape(1)
    ga_bits = [1 << b for b in range(ga.bit_length() - 1)]
    pair_bits = [1 << b for b in range(pair.bit_length() - 1)]
    ga_order = halving_order(ga_bits)
    stages, half = len(ga_bits), ga // 2

    val = jnp.transpose(val_density, (1, 2, 0, 3))
    vals = {0: (val[None], 0)}
    for bit in reversed(pair_bits):
        known = sorted(vals)
        got = swap(
            jnp.concatenate([vals[r][0][vals[r][1] :][:1] for r in known]), "pair", pair, bit
        )
        for place, slot in enumerate(known):
            vals[slot ^ bit] = (got, place)

    con = jnp.transpose(behind(con_density, val), (1, 2, 0, 3))
    *stay, go, token = shift_call(con, shift_map, me, ga_order, width)
    nearest = ga_bits[0]
    from_near = swap(go, "ga", ga, nearest)
    cons = {0: (stay[0], 0)}
    for slot, block in zip(ga_order[1:half], stay[1:]):
        if slot & ga_bits[-1]:
            cons[slot] = (swap(block, "ga", ga, slot), 0)

    row_count, col_count = NT // pair, NT // ga
    row_slots = jnp.asarray(halving_order(pair_bits), jnp.int32)
    row_trans = ordering.reshape(pair, row_count)[me_pair ^ row_slots].reshape(-1)
    at_row = ((row_trans // row_count) ^ me_pair) * row_count + row_trans % row_count
    pick_rows = (at_row[:, None] == jnp.arange(NT, dtype=jnp.int32)[None, :]).astype(jnp.bfloat16)
    col_trans = ordering.reshape(ga, col_count)[me_ga ^ jnp.asarray(ga_order, jnp.int32)]
    col_trans = jnp.pad(col_trans, ((0, 0), (0, 64 - col_count)), constant_values=-1).reshape(1, -1)
    real_col = col_trans >= 0
    at_direct = jnp.where(real_col, (col_trans % NC) * NV + col_trans // NC, -1)
    own_col = real_col & (col_trans // row_count == me_pair)
    at_exch = jnp.where(own_col, col_trans % row_count, -1)

    def pick_cols(at, size, scale):
        hot = at == jnp.arange(size, dtype=jnp.int32)[:, None]
        return jnp.where(hot, scale, 0.0).astype(jnp.bfloat16)

    col_direct, col_exch = pick_cols(at_direct, NT, -1.0), pick_cols(at_exch, row_count, 2.0)

    there = jnp.transpose(trans_there, (1, 2, 0, 3))
    arrived = [block for block, _ in cons.values()]
    token = behind(token, (there, pick_rows, col_direct, col_exch, arrived))
    order = [("x", 0, 0), ("x", 1, 0), ("hop", 0, 1)] + [("x", q, 0) for q in range(2, points)]
    hops = [(2 * q + s, q, s) for q in range(points) for s in range(1, stages)]
    order += [("hop", q, s) for _, q, s in sorted(hops) if (q, s) != (0, 1)]
    order += [("tile", q, stages) for q in range(points)]
    gone, keep, heard = [], [], []
    tiles = [None] * points
    for kind, q, stage in order:
        if kind == "x":
            if q == 2:
                token = behind(token, [c for c, _ in cons])
            coded, own, token = x_call(
                [vals[slot] for slot in range(pair)], screened, q, q, me, 4, [token]
            )
            keep.append(own)
            heard.append([swap(coded, "ga", ga, ga_bits[0])])
            if q == 0:
                stay, from_near = behind((stay, from_near), token)
                cons[nearest] = (from_near, 0)
                for place, slot in enumerate(ga_order[1:half], 1):
                    sent = from_near[place : place + 1]
                    if slot in cons:
                        cons[slot ^ nearest] = (swap(sent, "ga", ga, slot), 0)
                    else:
                        both = swap(jnp.concatenate([stay[place], sent]), "ga", ga, slot)
                        cons[slot], cons[slot ^ nearest] = (both, 0), (both, 1)
                cons = [cons[slot] for slot in ga_order]
        elif kind == "hop":
            columns = (ga >> (stage + 1)) * width
            if q > 0 and stage == stages - 1:
                token = behind(token, heard[q - 1][-1])
            coded, token = hop_call(keep[q], heard[q], me, stage, columns, [token])
            heard[q].append(swap(coded, "ga", ga, ga_bits[stage]))
            if (q, stage) == (0, 1):
                heres = {0: jnp.transpose(behind(trans_here, token), (1, 0, 2))}
                for bit in reversed(pair_bits):
                    for slot in sorted(heres):
                        heres[slot ^ bit] = swap(heres[slot], "pair", pair, bit)
            if (q, stage) == (1, 1):
                slots = [(heres[slot][None], 0) for slot in range(pair)]
                exch, token = exchange_call(slots, there, coulomb, [token])
        else:
            own, sent, token = tile_call(
                cons, q, keep[q], heard[q], exch, me, ga_order, pick_rows, col_direct,
                col_exch, pair, [token],
            )
            for bit in pair_bits[:-1]:
                own, sent = fold_call(own[None], swap(sent[None], "pair", pair, bit))
                own, sent = own[0], sent[0]
            tiles[q] = own, swap(sent, "pair", pair, pair_bits[-1])

    own, sent = pack_call(*zip(*tiles))
    for bit in ga_bits[:-1]:
        own, sent = merge_call(own, swap(sent, "ga", ga, bit))
    total = merge_call(own, swap(sent, "ga", ga, ga_bits[-1]))[0]
    out = total.reshape(points, row_count, 2, 64)[..., :col_count]
    return jnp.transpose(out, (0, 2, 1, 3))


def contract_float(left, right):
    high = lax.Precision.HIGHEST
    real_part = jnp.einsum(
        "nkg,mkg->nkm", left[:, :, 0], right[:, :, 0], precision=high
    ) - jnp.einsum("nkg,mkg->nkm", left[:, :, 1], right[:, :, 1], precision=high)
    imag_part = jnp.einsum(
        "nkg,mkg->nkm", left[:, :, 0], right[:, :, 1], precision=high
    ) + jnp.einsum("nkg,mkg->nkm", left[:, :, 1], right[:, :, 0], precision=high)
    return jnp.stack([real_part, imag_part], axis=2)


def times_cols(rows, weights):
    first = jnp.einsum(
        "nkh,kgh->nkg", rows[:, :, 0], weights[:, 0], preferred_element_type=jnp.float32
    ) - jnp.einsum("nkh,kgh->nkg", rows[:, :, 1], weights[:, 1], preferred_element_type=jnp.float32)
    second = jnp.einsum(
        "nkh,kgh->nkg", rows[:, :, 0], weights[:, 1], preferred_element_type=jnp.float32
    ) + jnp.einsum("nkh,kgh->nkg", rows[:, :, 1], weights[:, 0], preferred_element_type=jnp.float32)
    return jnp.stack([first, second], axis=2)


def on_any_device(
    val_density, con_density, screened, coulomb, trans_here, trans_there, shift_map, ordering
):
    con_count = con_density.shape[0]
    points = con_density.shape[1]
    slab_cols = con_density.shape[3]
    blocks = slab_cols // GBLK
    within = (shift_map % GBLK).reshape(points, blocks, GBLK)
    onehot = (
        within[:, :, :, None] == jnp.arange(GBLK, dtype=jnp.int32)[None, None, None, :]
    ).astype(jnp.bfloat16)
    con_blocks = con_density.reshape(con_count, points, 2, blocks, GBLK)
    shifted = (
        jnp.einsum("bkpnh,kngh->bkpng", con_blocks, onehot, preferred_element_type=jnp.float32)
        .astype(jnp.bfloat16)
        .reshape(con_density.shape)
    )
    whole_here = lax.all_gather(trans_here, "pair", axis=0, tiled=True).astype(jnp.float32)
    weighted = trans_there.astype(jnp.float32) * coulomb[None, :, None, :]
    high = lax.Precision.HIGHEST
    exch_real = jnp.einsum(
        "tg,skg->tks", whole_here[:, 0], weighted[:, :, 0], precision=high
    ) - jnp.einsum("tg,skg->tks", whole_here[:, 1], weighted[:, :, 1], precision=high)
    exch_imag = jnp.einsum(
        "tg,skg->tks", whole_here[:, 0], weighted[:, :, 1], precision=high
    ) + jnp.einsum("tg,skg->tks", whole_here[:, 1], weighted[:, :, 0], precision=high)
    exch_part = jnp.stack([exch_real, exch_imag], axis=2)
    whole_con = lax.all_gather(shifted, "ga", axis=0, tiled=True)
    screened_rows = lax.psum_scatter(
        times_cols(whole_con, screened), "pair", scatter_dimension=0, tiled=True
    )
    direct_part = contract_float(
        lax.all_gather(val_density, "pair", axis=0, tiled=True).astype(jnp.float32), screened_rows
    )
    direct_sum, exch_sum = lax.psum((direct_part, exch_part), "ga")
    direct_full, exch_full = (
        lax.all_gather(direct_sum, "pair", axis=3, tiled=True),
        lax.all_gather(exch_sum, "pair", axis=3, tiled=True),
    )
    row_count = NT // lax.axis_size("pair")
    col_count = NT // lax.axis_size("ga")
    row_trans = lax.dynamic_slice_in_dim(ordering, lax.axis_index("pair") * row_count, row_count, 0)
    col_trans = lax.dynamic_slice_in_dim(ordering, lax.axis_index("ga") * col_count, col_count, 0)
    row_pairs = (row_trans // NC)[:, None] * NV + (col_trans // NC)[None, :]
    col_pairs = (row_trans % NC)[:, None] * NC + (col_trans % NC)[None, :]
    picked = direct_full[row_pairs.reshape(-1)]
    col_mask = (
        col_pairs.reshape(-1)[:, None] == jnp.arange(direct_full.shape[3], dtype=jnp.int32)[None, :]
    ).astype(jnp.float32)
    direct_flat = jnp.sum(picked * col_mask[:, None, None, :], axis=3)
    direct_sel = jnp.transpose(direct_flat.reshape(row_count, col_count, points, 2), (2, 3, 0, 1))
    exch_picked = exch_full[row_trans]
    col_hot = (jnp.arange(NT, dtype=jnp.int32)[:, None] == col_trans[None, :]).astype(jnp.float32)
    exch_sel = jnp.einsum("rkpt,tc->kprc", exch_picked, col_hot, precision=high)
    return 2.0 * exch_sel - direct_sel


def solution(mesh):
    in_specs = (
        P("pair", None, None, "ga"),
        P("ga", None, None, "pair"),
        P(None, None, "ga", "pair"),
        P(None, "ga"),
        P("pair", None, "ga"),
        P("pair", None, None, "ga"),
        P(None, "pair"),
        P(),
    )
    out_specs = P(None, None, "pair", "ga")

    def run(*args):
        ga, pair = mesh.shape["ga"], mesh.shape["pair"]
        con_count, h_count = args[1].shape[0], args[1].shape[3]
        suits = (
            ga & (ga - 1) == 0
            and pair & (pair - 1) == 0
            and ga >= 4
            and pair >= 4
            and NT % (pair * GROUP // 2) == 0
            and h_count % (ga * pair * GBLK) == 0
            and con_count % (8 * ga) == 0
            and args[0].shape[0] % (16 * pair) == 0
            and NT % (16 * pair) == 0
            and NT // ga <= 64
            and args[1].shape[1] * NT % (pair * SMALL) == 0
        )
        body = on_device if suits else on_any_device
        return jax.shard_map(
            body, mesh=mesh, in_specs=in_specs, out_specs=out_specs, check_vma=False
        )(*args)

    return run
```

```python
import jax
import jax.numpy as jnp
from jax import lax
from jax.experimental import pallas as pl
from jax.experimental.pallas import tpu as pltpu
from jax.sharding import PartitionSpec as P

NV = 16
NC = 24
GBLK = 128
NT = 384

GROUP = 64
EXP_ROWS = 16
SMALL = 32
STEPS = 128.0
TOP = 32700.0
MAGIC = 1.5 * 2.0**23
NT_DIMS = (((1,), (1,)), ((), ()))
VMEM = 40 * 1024 * 1024


TOKEN = jax.ShapeDtypeStruct((8, 128), jnp.float32)


def params():
    return pltpu.CompilerParams(vmem_limit_bytes=VMEM)


def cost(flops, moved):
    return pl.CostEstimate(flops=int(flops) // 64, bytes_accessed=int(moved) // 64, transcendentals=0)


def mm(left, right):
    return jnp.dot(left, right, preferred_element_type=jnp.float32)


def mm_nt(left, right):
    return lax.dot_general(left, right, NT_DIMS, preferred_element_type=jnp.float32)


def halves(value):
    high = value.astype(jnp.bfloat16)
    low = (value - high.astype(jnp.float32)).astype(jnp.bfloat16)
    return high, low


def exp_rows(rows, group):
    return -(-(rows // group) // 16) * 16


def encode(value, out_ref, group=GROUP):
    rows, width = value.shape
    groups = rows // group
    parts = value.reshape(groups, group, width)
    largest = jnp.maximum(jnp.max(jnp.abs(parts), axis=1), 1e-30)
    level = jnp.ceil(jnp.log2(largest) * STEPS) + 1.0
    factor = TOP * jnp.exp2(level * (-1.0 / STEPS))
    coded = ((parts * factor[:, None, :] + MAGIC) - MAGIC).astype(jnp.int32)
    out_ref[0:rows, :] = coded.reshape(rows, width).astype(jnp.int16)
    extra = exp_rows(rows, group)
    level = level.astype(jnp.int32)
    if extra > groups:
        pad = jnp.zeros((extra - groups, width), jnp.int32)
        level = jnp.concatenate([level, pad], axis=0)
    out_ref[rows : rows + extra, :] = level.astype(jnp.int16)


def decode(ref, rows=None, group=GROUP):
    rows = ref.shape[0] - EXP_ROWS if rows is None else rows
    width = ref.shape[1]
    groups = rows // group
    extra = exp_rows(rows, group)
    level = ref[rows : rows + extra, :].astype(jnp.int32).astype(jnp.float32)[0:groups]
    factor = jnp.exp2(level * (1.0 / STEPS)) * (1.0 / TOP)
    parts = ref[0:rows, :].astype(jnp.int32).astype(jnp.float32).reshape(groups, group, width)
    return (parts * factor[:, None, :]).reshape(rows, width)


def reversed_bits(number, count):
    return sum(((number // (1 << b)) % 2) * (1 << (count - 1 - b)) for b in range(count))


def block_of(me, known, stop, flip):
    number = 0
    for bit in range(known, stop):
        flag = (me // (1 << bit)) % 2
        number = 2 * number + (1 - flag if flip and bit == stop - 1 else flag)
    return number


def shift_kernel(order, me_ref, con_ref, map_ref, *refs):
    *stay_refs, go_ref, token_ref = refs
    half, _, _, rows, width = go_ref.shape
    count = len(order).bit_length() - 1
    token_ref[...] = jnp.zeros_like(token_ref)
    for p, slot in enumerate(order):
        out_ref = stay_refs[p].at[0] if p < half else go_ref.at[p - half]
        first = reversed_bits(jnp.bitwise_xor(me_ref[0], slot), count) * width
        for block in range(width // GBLK):
            cols = pl.ds(pl.multiple_of(first + block * GBLK, GBLK), GBLK)
            within = jnp.bitwise_and(map_ref[0, 0:1, cols], GBLK - 1)
            within = jnp.broadcast_to(within, (rows, GBLK))
            for part in range(2):
                values = con_ref[0, part, :, cols].astype(jnp.float32)
                moved = jnp.take_along_axis(values, within, axis=1)
                out_ref[0, part, :, block * GBLK : (block + 1) * GBLK] = moved.astype(jnp.bfloat16)


def shift_call(con, shift_map, me, order, width):
    points, _, rows, slab = con.shape
    half = len(order) // 2
    counts = [1] * half + [half]
    grid_spec = pltpu.PrefetchScalarGridSpec(
        num_scalar_prefetch=1,
        grid=(points,),
        in_specs=[
            pl.BlockSpec((1, 2, rows, slab), lambda q, me: (q, 0, 0, 0)),
            pl.BlockSpec((1, 1, slab), lambda q, me: (q, 0, 0)),
        ],
        out_specs=[
            pl.BlockSpec((n, 1, 2, rows, width), lambda q, me: (0, q, 0, 0, 0)) for n in counts
        ]
        + [pl.BlockSpec(TOKEN.shape, lambda q, me: (0, 0))],
    )
    return pl.pallas_call(
        lambda *refs: shift_kernel(order, *refs),
        grid_spec=grid_spec,
        out_shape=[
            jax.ShapeDtypeStruct((n, points, 2, rows, width), jnp.bfloat16) for n in counts
        ]
        + [TOKEN],
        compiler_params=params(),
        cost_estimate=cost(8 * con.size, 4 * con.size),
    )(me, con, shift_map.reshape(points, 1, slab))


def x_kernel(slots, waits, me_ref, *refs):
    val_refs, weight_ref = refs[:slots], refs[slots]
    go_ref, keep_ref, token_ref, left_ref = refs[slots + 1 + waits :]
    _, _, _, rows, depth = val_refs[0].shape
    half = slots * rows
    token_ref[...] = jnp.zeros_like(token_ref)
    step = pl.program_id(0)
    halfway = pl.num_programs(0) // 2

    @pl.when(step == 0)
    def _():
        for slot in range(slots):
            real, imag = val_refs[slot][0, 0, 0], val_refs[slot][0, 0, 1]
            top = slice(slot * rows, (slot + 1) * rows)
            low = slice(half + slot * rows, half + (slot + 1) * rows)
            left_ref[top, 0:depth] = real
            left_ref[top, depth : 2 * depth] = -imag
            left_ref[low, 0:depth] = imag
            left_ref[low, depth : 2 * depth] = real

    weight = weight_ref[0].reshape(2 * depth, weight_ref.shape[3])

    @pl.when(step < halfway)
    def _():
        encode(mm(left_ref[...], weight), go_ref)

    @pl.when(step >= halfway)
    def _():
        keep_ref[...] = mm(left_ref[...], weight)


def x_call(vals, screened, place, point, me, steps, after):
    slots = len(vals)
    _, _, _, rows, depth = vals[0][0].shape
    height = 2 * slots * rows
    columns = screened.shape[3] // 2
    half = steps // 2
    width = columns // half
    grid_spec = pltpu.PrefetchScalarGridSpec(
        num_scalar_prefetch=1,
        grid=(steps,),
        in_specs=[
            pl.BlockSpec((1, 1, 2, rows, depth), lambda j, me, slot=slot: (slot, place, 0, 0, 0))
            for _, slot in vals
        ]
        + [
            pl.BlockSpec(
                (1, 2, depth, width),
                lambda j, me: (point, 0, 0, ((me[0] + 1 + j // half) % 2) * half + j % half),
            )
        ]
        + [pl.BlockSpec(memory_space=pl.ANY) for _ in after],
        out_specs=[
            pl.BlockSpec((height + EXP_ROWS, width), lambda j, me: (0, jnp.minimum(j, half - 1))),
            pl.BlockSpec((height, width), lambda j, me: (0, jnp.maximum(j - half, 0))),
            pl.BlockSpec(TOKEN.shape, lambda j, me: (0, 0)),
        ],
        scratch_shapes=[pltpu.VMEM((height, 2 * depth), jnp.bfloat16)],
    )
    return pl.pallas_call(
        lambda *refs: x_kernel(slots, len(after), *refs),
        grid_spec=grid_spec,
        out_shape=[
            jax.ShapeDtypeStruct((height + EXP_ROWS, columns), jnp.int16),
            jax.ShapeDtypeStruct((height, columns), jnp.float32),
            TOKEN,
        ],
        compiler_params=params(),
        cost_estimate=cost(
            2 * height * 2 * depth * 2 * columns, 8 * depth * columns + 6 * height * columns
        ),
    )(me, *[v for v, _ in vals], screened, *after)


def hop_kernel(heard, me_ref, keep_ref, *refs):
    total = keep_ref[...]
    for ref in refs[:heard]:
        total = total + decode(ref)
    out_ref, token_ref = refs[-2:]
    encode(total, out_ref)
    token_ref[...] = jnp.zeros_like(token_ref)


def hop_call(keep, others, me, stage, width, after):
    height, tall = keep.shape[0], others[0].shape[0]
    steps = width // 128

    def at(known):
        return lambda i, me: (0, block_of(me[0], known, stage + 1, True) * steps + i)

    grid_spec = pltpu.PrefetchScalarGridSpec(
        num_scalar_prefetch=1,
        grid=(steps,),
        in_specs=[pl.BlockSpec((height, 128), at(1))]
        + [pl.BlockSpec((tall, 128), at(n + 1)) for n in range(len(others))]
        + [pl.BlockSpec(memory_space=pl.ANY) for _ in after],
        out_specs=[
            pl.BlockSpec((tall, 128), lambda i, me: (0, i)),
            pl.BlockSpec(TOKEN.shape, lambda i, me: (0, 0)),
        ],
    )
    return pl.pallas_call(
        lambda *refs: hop_kernel(len(others), *refs),
        grid_spec=grid_spec,
        out_shape=[jax.ShapeDtypeStruct((tall, width), jnp.int16), TOKEN],
        compiler_params=params(),
        cost_estimate=cost(20 * height * width, 8 * height * width),
    )(me, keep, *others, *after)


def fold_kernel(own_ref, heard_ref, keep_ref, go_ref):
    rows = keep_ref.shape[1]
    for n in range(own_ref.shape[0]):
        total = own_ref[n] + decode(heard_ref.at[n])
        keep_ref[n] = total[:rows]
        encode(total[rows:], go_ref.at[n])


def fold_call(own, heard):
    count, rows, cols = own.shape
    shapes = [
        jax.ShapeDtypeStruct((count, rows // 2, cols), jnp.float32),
        jax.ShapeDtypeStruct((count, rows // 2 + EXP_ROWS, cols), jnp.int16),
    ]
    return pl.pallas_call(
        fold_kernel,
        out_shape=shapes,
        compiler_params=params(),
        cost_estimate=cost(20 * own.size, 10 * own.size),
    )(own, heard)


def split_sums(sums_ref, keep_ref, go_ref):
    half, points, rows, width = keep_ref.shape
    keep_ref[...] = sums_ref[0:half]
    encode(sums_ref[half:].reshape(half * points * rows, width), go_ref, SMALL)


def split_shapes(slots, points, rows):
    count = slots // 2 * points * rows
    return [
        jax.ShapeDtypeStruct((slots // 2, points, rows, 128), jnp.float32),
        jax.ShapeDtypeStruct((count + exp_rows(count, SMALL), 128), jnp.int16),
    ]


def pack_kernel(*refs):
    *refs, keep_ref, go_ref, sums_ref = refs
    slots, points, rows, _ = sums_ref.shape
    width = refs[0].shape[1]
    count = width // slots
    first = lax.broadcasted_iota(jnp.int32, (rows, 128), 1) < 64
    for n in range(points):
        total = refs[n][...] + decode(refs[points + n])
        for slot in range(slots):
            tile, lane = divmod(slot * count, 128)
            reach = min(width, (tile + (1 if lane + count <= 128 else 2)) * 128)
            piece = total[:, tile * 128 : reach]
            if lane:
                piece = pltpu.roll(piece, reach - tile * 128 - lane, 1)
            real, imag = piece[:rows, :128], piece[rows:, :128]
            sums_ref[slot, n] = jnp.where(first, real, pltpu.roll(imag, 64, 1))
    split_sums(sums_ref, keep_ref, go_ref)


def pack_call(owns, heards, slots):
    rows, cols = owns[0].shape
    shape = (slots, len(owns), rows // 2)
    return pl.pallas_call(
        pack_kernel,
        out_shape=split_shapes(*shape),
        scratch_shapes=[pltpu.VMEM(shape + (128,), jnp.float32)],
        compiler_params=params(),
        cost_estimate=cost(60 * owns[0].size, 30 * owns[0].size),
    )(*owns, *heards)


def merge_kernel(own_ref, heard_ref, *refs):
    slots, points, rows, width = own_ref.shape
    count = slots * points * rows
    sums_ref = refs[-1]
    heard = decode(heard_ref, count, SMALL)
    sums_ref[...] = own_ref[...] + heard.reshape(slots, points, rows, width)
    if slots > 1:
        split_sums(sums_ref, *refs[:-1])


def merge_call(own, heard):
    last = own.shape[0] == 1
    sums = jax.ShapeDtypeStruct(own.shape, jnp.float32)
    return pl.pallas_call(
        merge_kernel,
        out_shape=sums if last else split_shapes(*own.shape[:3]),
        scratch_shapes=[] if last else [pltpu.VMEM(own.shape, jnp.float32)],
        compiler_params=params(),
        cost_estimate=cost(20 * own.size, 10 * own.size),
    )(own, heard)


def exchange_kernel(slots, waits, *refs):
    here_refs, (there_ref, coulomb_ref) = refs[:slots], refs[slots : slots + 2]
    out_ref, token_ref, left_ref = refs[slots + 2 + waits :]
    _, _, rows, depth = here_refs[0].shape
    token_ref[...] = jnp.zeros_like(token_ref)

    @pl.when(pl.program_id(0) == 0)
    def _():
        for slot in range(slots):
            for part in range(2):
                left_ref[
                    slot * rows : (slot + 1) * rows, part * depth : (part + 1) * depth
                ] = here_refs[slot][0, part]

    factor = coulomb_ref[0]
    real = there_ref[0, 0].astype(jnp.float32) * factor
    imag = there_ref[0, 1].astype(jnp.float32) * factor
    right = jnp.concatenate(
        [jnp.concatenate([real, -imag], axis=1), jnp.concatenate([imag, real], axis=1)], axis=0
    )
    high, low = halves(right)
    left = left_ref[...]
    both = mm_nt(left, high) + mm_nt(left, low)
    cols = both.shape[1] // 2
    for part in range(2):
        out_ref[0, part] = both[:, part * cols : (part + 1) * cols]


def exchange_call(heres, there, coulomb, after):
    slots, rows = len(heres), heres[0][0].shape[2]
    points, _, cols, depth = there.shape
    height = slots * rows
    return pl.pallas_call(
        lambda *refs: exchange_kernel(slots, len(after), *refs),
        grid=(points,),
        in_specs=[
            pl.BlockSpec((1,) + h.shape[1:], lambda q, slot=slot: (slot, 0, 0, 0))
            for h, slot in heres
        ]
        + [
            pl.BlockSpec((1, 2, cols, depth), lambda q: (q, 0, 0, 0)),
            pl.BlockSpec((1, 1, depth), lambda q: (q, 0, 0)),
        ]
        + [pl.BlockSpec(memory_space=pl.ANY) for _ in after],
        out_specs=[
            pl.BlockSpec((1, 2, height, cols), lambda q: (q, 0, 0, 0)),
            pl.BlockSpec(TOKEN.shape, lambda q: (0, 0)),
        ],
        out_shape=[jax.ShapeDtypeStruct((points, 2, height, cols), jnp.float32), TOKEN],
        scratch_shapes=[pltpu.VMEM((height, 2 * depth), jnp.bfloat16)],
        compiler_params=params(),
        cost_estimate=cost(2 * points * height * 2 * cols * 2 * depth * 2, 8 * points * cols * depth),
    )(*[h for h, _ in heres], there, coulomb.reshape(points, 1, depth), *after)


def tile_kernel(order, heard, chunks, waits, me_ref, *refs):
    slots = len(order)
    con_refs, keep_ref = refs[:slots], refs[slots]
    heard_refs = refs[slots + 1 : slots + 1 + heard]
    exch_ref, row_ref, col_direct_ref, col_exch_ref = refs[slots + 1 + heard : slots + 5 + heard]
    keep_out, go_out, token_ref, con_all, direct_ref, natural_ref, sums_ref = refs[
        slots + 5 + heard + waits :
    ]
    token_ref[...] = jnp.zeros_like(token_ref)
    total = keep_ref[...]
    for ref in heard_refs:
        total = total + decode(ref)
    pairs, width = total.shape[0] // 2, total.shape[1]
    rows = con_refs[0].shape[3]
    pitch = con_all.shape[0] // slots
    for slot in range(slots):
        for part in range(2):
            con_all[
                slot * pitch : slot * pitch + rows, part * width : (part + 1) * width
            ] = con_refs[slot][0, 0, part]
    real, imag = total[:pairs], total[pairs:]
    right = jnp.concatenate(
        [jnp.concatenate([real, -imag], axis=1), jnp.concatenate([imag, real], axis=1)], axis=0
    )
    high, low = halves(right)
    left = con_all[...]
    direct = mm_nt(left, high) + mm_nt(left, low)
    lanes = direct_ref.shape[0]
    for slot in range(slots):
        start = pl.multiple_of(jnp.bitwise_xor(me_ref[0], order[slot]) * rows, 8)
        for lane in range(lanes):
            direct_ref[lane, pl.ds(start, rows), :] = direct[
                slot * pitch : slot * pitch + rows, lane * 128 : (lane + 1) * 128
            ]
    group = 128 // NV
    place = lax.broadcasted_iota(jnp.int32, (NC, 128), 1) // NV
    per_part = lanes // 2
    for part in range(2):
        for chunk in range(NC // group):
            for band in range(NV):
                block = jnp.zeros((NC, 128), jnp.float32)
                for step in range(group):
                    e = chunk * group + step
                    piece = direct_ref[part * per_part + band // group, pl.ds(e, NC, stride=NC), :]
                    turn = (NV * (step - band)) % 128
                    if turn:
                        piece = pltpu.roll(piece, turn, 1)
                    block = jnp.where(place == step, piece, block)
                natural_ref[
                    part, band * NC : (band + 1) * NC, chunk * 128 : (chunk + 1) * 128
                ] = block
    pick_rows = row_ref[...]
    count = NT // chunks
    for part in range(2):
        result = None
        for source, pick_cols in (
            (natural_ref[part], col_direct_ref),
            (exch_ref[0, part], col_exch_ref),
        ):
            for piece in halves(source):
                moved = mm(pick_rows, piece).astype(jnp.bfloat16)
                term = mm(moved, pick_cols[...])
                result = term if result is None else result + term
        for chunk in range(chunks):
            at = (2 * chunk + part) * count
            sums_ref[at : at + count, :] = result[chunk * count : (chunk + 1) * count]
    stays = keep_out.shape[0]
    keep_out[...] = sums_ref[0:stays, :]
    encode(sums_ref[stays:, :], go_out)


def tile_call(
    cons, point, keep, heard, exch, me, order, pick_rows, col_direct, col_exch, chunks, after
):
    slots = len(cons)
    _, _, _, rows, width = cons[0][0].shape
    height, tall = keep.shape[0], heard[0].shape[0]
    pitch = -(-rows // 16) * 16
    out_cols = col_direct.shape[1]
    stages = len(heard)
    whole = lambda a: pl.BlockSpec(a.shape, lambda i, me: (0,) * len(a.shape))
    shapes = [
        jax.ShapeDtypeStruct((NT, out_cols), jnp.float32),
        jax.ShapeDtypeStruct((NT + EXP_ROWS, out_cols), jnp.int16),
        TOKEN,
    ]

    def at(known):
        return lambda i, me: (0, block_of(me[0], known, stages, False))

    grid_spec = pltpu.PrefetchScalarGridSpec(
        num_scalar_prefetch=1,
        grid=(1,),
        in_specs=[
            pl.BlockSpec((1, 1, 2, rows, width), lambda i, me, place=place: (place, point, 0, 0, 0))
            for _, place in cons
        ]
        + [pl.BlockSpec((height, width), at(1))]
        + [pl.BlockSpec((tall, width), at(n + 1)) for n in range(stages)]
        + [
            pl.BlockSpec((1,) + exch.shape[1:], lambda i, me: (point, 0, 0, 0)),
            whole(pick_rows),
            whole(col_direct),
            whole(col_exch),
        ]
        + [pl.BlockSpec(memory_space=pl.ANY) for _ in after],
        out_specs=[whole(a) for a in shapes],
        scratch_shapes=[
            pltpu.VMEM((slots * pitch, 2 * width), jnp.bfloat16),
            pltpu.VMEM((height // 128, NC * NC, 128), jnp.float32),
            pltpu.VMEM((2, NT, NT), jnp.float32),
            pltpu.VMEM((2 * NT, out_cols), jnp.float32),
        ],
    )
    return pl.pallas_call(
        lambda *refs: tile_kernel(order, stages, chunks, len(after), *refs),
        grid_spec=grid_spec,
        out_shape=shapes,
        compiler_params=params(),
        cost_estimate=cost(2.8e9, 8e6),
    )(me, *[c for c, _ in cons], keep, *heard, exch, pick_rows, col_direct, col_exch, *after)


def swap(value, axis, size, bit):
    return lax.ppermute(value, axis, [(i, i ^ bit) for i in range(size)])


def halving_order(bits):
    order = [0]
    for bit in reversed(bits):
        order = order + [o ^ bit for o in order]
    return order


def behind(value, token):
    return lax.optimization_barrier((value, token))[0]


def on_device(*args):
    (val_density, con_density, screened, coulomb, trans_here, trans_there, shift_map, ordering) = args
    ga, pair = lax.axis_size("ga"), lax.axis_size("pair")
    points = con_density.shape[1]
    slab = con_density.shape[3]
    width = slab // ga
    me_ga, me_pair = lax.axis_index("ga"), lax.axis_index("pair")
    me = me_ga.astype(jnp.int32).reshape(1)
    ga_bits = [1 << b for b in range(ga.bit_length() - 1)]
    pair_bits = [1 << b for b in range(pair.bit_length() - 1)]
    ga_order = halving_order(ga_bits)
    stages, half = len(ga_bits), ga // 2

    val = jnp.transpose(val_density, (1, 2, 0, 3))
    vals = {0: (val[None], 0)}
    for bit in reversed(pair_bits):
        known = sorted(vals)
        got = swap(
            jnp.concatenate([vals[r][0][vals[r][1] :][:1] for r in known]), "pair", pair, bit
        )
        for place, slot in enumerate(known):
            vals[slot ^ bit] = (got, place)

    con = jnp.transpose(behind(con_density, val), (1, 2, 0, 3))
    *stay, go, token = shift_call(con, shift_map, me, ga_order, width)
    nearest = ga_bits[0]
    from_near = swap(go, "ga", ga, nearest)
    cons = {0: (stay[0], 0)}
    for slot, block in zip(ga_order[1:half], stay[1:]):
        if slot & ga_bits[-1]:
            cons[slot] = (swap(block, "ga", ga, slot), 0)

    row_count, col_count = NT // pair, NT // ga
    row_slots = jnp.asarray(halving_order(pair_bits), jnp.int32)
    row_trans = ordering.reshape(pair, row_count)[me_pair ^ row_slots].reshape(-1)
    at_row = ((row_trans // row_count) ^ me_pair) * row_count + row_trans % row_count
    pick_rows = (at_row[:, None] == jnp.arange(NT, dtype=jnp.int32)[None, :]).astype(jnp.bfloat16)
    col_trans = ordering.reshape(ga, col_count)[me_ga ^ jnp.asarray(ga_order, jnp.int32)]
    col_trans = col_trans.reshape(1, -1)
    at_direct = (col_trans % NC) * NV + col_trans // NC
    at_exch = jnp.where(col_trans // row_count == me_pair, col_trans % row_count, -1)

    def pick_cols(at, size, scale):
        hot = at == jnp.arange(size, dtype=jnp.int32)[:, None]
        return jnp.where(hot, scale, 0.0).astype(jnp.bfloat16)

    col_direct, col_exch = pick_cols(at_direct, NT, -1.0), pick_cols(at_exch, row_count, 2.0)

    there = jnp.transpose(trans_there, (1, 2, 0, 3))
    arrived = [block for block, _ in cons.values()]
    token = behind(token, (there, pick_rows, col_direct, col_exch, arrived))
    order = [("x", q, 0) for q in range(points)]
    hops = [(2 * q + s, q, s) for q in range(points) for s in range(1, stages)]
    order += [("hop", q, s) for _, q, s in sorted(hops)]
    order += [("tile", q, stages) for q in range(points)]
    gone, keep, heard = [], [], []
    tiles = [None] * points
    for kind, q, stage in order:
        if kind == "x":
            coded, own, token = x_call(
                [vals[slot] for slot in range(pair)], screened, q, q, me, 4, [token]
            )
            keep.append(own)
            heard.append([swap(coded, "ga", ga, ga_bits[0])])
            if q == 0:
                stay, from_near = behind((stay, from_near), token)
                cons[nearest] = (from_near, 0)
                for place, slot in enumerate(ga_order[1:half], 1):
                    sent = from_near[place : place + 1]
                    if slot in cons:
                        cons[slot ^ nearest] = (swap(sent, "ga", ga, slot), 0)
                    else:
                        both = swap(jnp.concatenate([stay[place], sent]), "ga", ga, slot)
                        cons[slot], cons[slot ^ nearest] = (both, 0), (both, 1)
                cons = [cons[slot] for slot in ga_order]
        elif kind == "hop":
            columns = (ga >> (stage + 1)) * width
            if (q, stage) == (0, 1):
                token = behind(token, [c for c, _ in cons])
            if q > 0 and stage == stages - 1:
                token = behind(token, heard[q - 1][-1])
            coded, token = hop_call(keep[q], heard[q], me, stage, columns, [token])
            heard[q].append(swap(coded, "ga", ga, ga_bits[stage]))
            if (q, stage) == (0, 1):
                heres = {0: jnp.transpose(behind(trans_here, token), (1, 0, 2))}
                for bit in reversed(pair_bits):
                    for slot in sorted(heres):
                        heres[slot ^ bit] = swap(heres[slot], "pair", pair, bit)
            if (q, stage) == (1, 1):
                slots = [(heres[slot][None], 0) for slot in range(pair)]
                exch, token = exchange_call(slots, there, coulomb, [token])
        else:
            own, sent, token = tile_call(
                cons, q, keep[q], heard[q], exch, me, ga_order, pick_rows, col_direct,
                col_exch, pair, [token],
            )
            for bit in pair_bits[:-1]:
                own, sent = fold_call(own[None], swap(sent[None], "pair", pair, bit))
                own, sent = own[0], sent[0]
            tiles[q] = own, swap(sent, "pair", pair, pair_bits[-1])

    own, sent = pack_call(*zip(*tiles), ga)
    for bit in ga_bits[:-1]:
        own, sent = merge_call(own, swap(sent, "ga", ga, bit))
    total = merge_call(own, swap(sent, "ga", ga, ga_bits[-1]))[0]
    out = total.reshape(points, row_count, 2, 64)[..., :col_count]
    return jnp.transpose(out, (0, 2, 1, 3))


def contract_float(left, right):
    high = lax.Precision.HIGHEST
    real_part = jnp.einsum(
        "nkg,mkg->nkm", left[:, :, 0], right[:, :, 0], precision=high
    ) - jnp.einsum("nkg,mkg->nkm", left[:, :, 1], right[:, :, 1], precision=high)
    imag_part = jnp.einsum(
        "nkg,mkg->nkm", left[:, :, 0], right[:, :, 1], precision=high
    ) + jnp.einsum("nkg,mkg->nkm", left[:, :, 1], right[:, :, 0], precision=high)
    return jnp.stack([real_part, imag_part], axis=2)


def times_cols(rows, weights):
    first = jnp.einsum(
        "nkh,kgh->nkg", rows[:, :, 0], weights[:, 0], preferred_element_type=jnp.float32
    ) - jnp.einsum("nkh,kgh->nkg", rows[:, :, 1], weights[:, 1], preferred_element_type=jnp.float32)
    second = jnp.einsum(
        "nkh,kgh->nkg", rows[:, :, 0], weights[:, 1], preferred_element_type=jnp.float32
    ) + jnp.einsum("nkh,kgh->nkg", rows[:, :, 1], weights[:, 0], preferred_element_type=jnp.float32)
    return jnp.stack([first, second], axis=2)


def on_any_device(
    val_density, con_density, screened, coulomb, trans_here, trans_there, shift_map, ordering
):
    con_count = con_density.shape[0]
    points = con_density.shape[1]
    slab_cols = con_density.shape[3]
    blocks = slab_cols // GBLK
    within = (shift_map % GBLK).reshape(points, blocks, GBLK)
    onehot = (
        within[:, :, :, None] == jnp.arange(GBLK, dtype=jnp.int32)[None, None, None, :]
    ).astype(jnp.bfloat16)
    con_blocks = con_density.reshape(con_count, points, 2, blocks, GBLK)
    shifted = (
        jnp.einsum("bkpnh,kngh->bkpng", con_blocks, onehot, preferred_element_type=jnp.float32)
        .astype(jnp.bfloat16)
        .reshape(con_density.shape)
    )
    whole_here = lax.all_gather(trans_here, "pair", axis=0, tiled=True).astype(jnp.float32)
    weighted = trans_there.astype(jnp.float32) * coulomb[None, :, None, :]
    high = lax.Precision.HIGHEST
    exch_real = jnp.einsum(
        "tg,skg->tks", whole_here[:, 0], weighted[:, :, 0], precision=high
    ) - jnp.einsum("tg,skg->tks", whole_here[:, 1], weighted[:, :, 1], precision=high)
    exch_imag = jnp.einsum(
        "tg,skg->tks", whole_here[:, 0], weighted[:, :, 1], precision=high
    ) + jnp.einsum("tg,skg->tks", whole_here[:, 1], weighted[:, :, 0], precision=high)
    exch_part = jnp.stack([exch_real, exch_imag], axis=2)
    whole_con = lax.all_gather(shifted, "ga", axis=0, tiled=True)
    screened_rows = lax.psum_scatter(
        times_cols(whole_con, screened), "pair", scatter_dimension=0, tiled=True
    )
    direct_part = contract_float(
        lax.all_gather(val_density, "pair", axis=0, tiled=True).astype(jnp.float32), screened_rows
    )
    direct_sum, exch_sum = lax.psum((direct_part, exch_part), "ga")
    direct_full, exch_full = (
        lax.all_gather(direct_sum, "pair", axis=3, tiled=True),
        lax.all_gather(exch_sum, "pair", axis=3, tiled=True),
    )
    row_count = NT // lax.axis_size("pair")
    col_count = NT // lax.axis_size("ga")
    row_trans = lax.dynamic_slice_in_dim(ordering, lax.axis_index("pair") * row_count, row_count, 0)
    col_trans = lax.dynamic_slice_in_dim(ordering, lax.axis_index("ga") * col_count, col_count, 0)
    row_pairs = (row_trans // NC)[:, None] * NV + (col_trans // NC)[None, :]
    col_pairs = (row_trans % NC)[:, None] * NC + (col_trans % NC)[None, :]
    picked = direct_full[row_pairs.reshape(-1)]
    col_mask = (
        col_pairs.reshape(-1)[:, None] == jnp.arange(direct_full.shape[3], dtype=jnp.int32)[None, :]
    ).astype(jnp.float32)
    direct_flat = jnp.sum(picked * col_mask[:, None, None, :], axis=3)
    direct_sel = jnp.transpose(direct_flat.reshape(row_count, col_count, points, 2), (2, 3, 0, 1))
    exch_picked = exch_full[row_trans]
    col_hot = (jnp.arange(NT, dtype=jnp.int32)[:, None] == col_trans[None, :]).astype(jnp.float32)
    exch_sel = jnp.einsum("rkpt,tc->kprc", exch_picked, col_hot, precision=high)
    return 2.0 * exch_sel - direct_sel


def solution(mesh):
    in_specs = (
        P("pair", None, None, "ga"),
        P("ga", None, None, "pair"),
        P(None, None, "ga", "pair"),
        P(None, "ga"),
        P("pair", None, "ga"),
        P("pair", None, None, "ga"),
        P(None, "pair"),
        P(),
    )
    out_specs = P(None, None, "pair", "ga")

    def run(*args):
        ga, pair = mesh.shape["ga"], mesh.shape["pair"]
        con_count, h_count = args[1].shape[0], args[1].shape[3]
        suits = (
            ga & (ga - 1) == 0
            and pair & (pair - 1) == 0
            and ga >= 4
            and pair >= 4
            and NT % (pair * GROUP // 2) == 0
            and h_count % (ga * pair * GBLK) == 0
            and con_count % (8 * ga) == 0
            and args[0].shape[0] % (16 * pair) == 0
            and NT % (16 * pair) == 0
            and NT // ga <= 64
            and args[1].shape[1] * NT % (pair * SMALL) == 0
        )
        body = on_device if suits else on_any_device
        return jax.shard_map(
            body, mesh=mesh, in_specs=in_specs, out_specs=out_specs, check_vma=False
        )(*args)

    return run
```

```python
import jax
import jax.numpy as jnp
from jax import lax
from jax.experimental import pallas as pl
from jax.experimental.pallas import tpu as pltpu
from jax.sharding import PartitionSpec as P

NV = 16
NC = 24
GBLK = 128
NT = 384

GROUP = 64
EXP_ROWS = 16
SMALL = 32
STEPS = 128.0
TOP = 32700.0
MAGIC = 1.5 * 2.0**23
NT_DIMS = (((1,), (1,)), ((), ()))
VMEM = 40 * 1024 * 1024


TOKEN = jax.ShapeDtypeStruct((8, 128), jnp.float32)


def params():
    return pltpu.CompilerParams(vmem_limit_bytes=VMEM)


def cost(flops, moved):
    return pl.CostEstimate(flops=int(flops) // 64, bytes_accessed=int(moved) // 64, transcendentals=0)


def mm(left, right):
    return jnp.dot(left, right, preferred_element_type=jnp.float32)


def mm_nt(left, right):
    return lax.dot_general(left, right, NT_DIMS, preferred_element_type=jnp.float32)


def halves(value):
    high = value.astype(jnp.bfloat16)
    low = (value - high.astype(jnp.float32)).astype(jnp.bfloat16)
    return high, low


def exp_rows(rows, group):
    return -(-(rows // group) // 16) * 16


def encode(value, out_ref, group=GROUP):
    rows, width = value.shape
    groups = rows // group
    parts = value.reshape(groups, group, width)
    largest = jnp.maximum(jnp.max(jnp.abs(parts), axis=1), 1e-30)
    level = jnp.ceil(jnp.log2(largest) * STEPS) + 1.0
    factor = TOP * jnp.exp2(level * (-1.0 / STEPS))
    coded = ((parts * factor[:, None, :] + MAGIC) - MAGIC).astype(jnp.int32)
    out_ref[0:rows, :] = coded.reshape(rows, width).astype(jnp.int16)
    extra = exp_rows(rows, group)
    level = level.astype(jnp.int32)
    if extra > groups:
        pad = jnp.zeros((extra - groups, width), jnp.int32)
        level = jnp.concatenate([level, pad], axis=0)
    out_ref[rows : rows + extra, :] = level.astype(jnp.int16)


def decode(ref, rows=None, group=GROUP):
    rows = ref.shape[0] - EXP_ROWS if rows is None else rows
    width = ref.shape[1]
    groups = rows // group
    extra = exp_rows(rows, group)
    level = ref[rows : rows + extra, :].astype(jnp.int32).astype(jnp.float32)[0:groups]
    factor = jnp.exp2(level * (1.0 / STEPS)) * (1.0 / TOP)
    parts = ref[0:rows, :].astype(jnp.int32).astype(jnp.float32).reshape(groups, group, width)
    return (parts * factor[:, None, :]).reshape(rows, width)


def reversed_bits(number, count):
    return sum(((number // (1 << b)) % 2) * (1 << (count - 1 - b)) for b in range(count))


def block_of(me, known, stop, flip):
    number = 0
    for bit in range(known, stop):
        flag = (me // (1 << bit)) % 2
        number = 2 * number + (1 - flag if flip and bit == stop - 1 else flag)
    return number


def shift_kernel(order, me_ref, con_ref, map_ref, *refs):
    *stay_refs, go_ref, token_ref = refs
    half, _, _, rows, width = go_ref.shape
    count = len(order).bit_length() - 1
    token_ref[...] = jnp.zeros_like(token_ref)
    for p, slot in enumerate(order):
        out_ref = stay_refs[p].at[0] if p < half else go_ref.at[p - half]
        first = reversed_bits(jnp.bitwise_xor(me_ref[0], slot), count) * width
        for block in range(width // GBLK):
            cols = pl.ds(pl.multiple_of(first + block * GBLK, GBLK), GBLK)
            within = jnp.bitwise_and(map_ref[0, 0:1, cols], GBLK - 1)
            within = jnp.broadcast_to(within, (rows, GBLK))
            for part in range(2):
                values = con_ref[0, part, :, cols].astype(jnp.float32)
                moved = jnp.take_along_axis(values, within, axis=1)
                out_ref[0, part, :, block * GBLK : (block + 1) * GBLK] = moved.astype(jnp.bfloat16)


def shift_call(con, shift_map, me, order, width):
    points, _, rows, slab = con.shape
    half = len(order) // 2
    counts = [1] * half + [half]
    grid_spec = pltpu.PrefetchScalarGridSpec(
        num_scalar_prefetch=1,
        grid=(points,),
        in_specs=[
            pl.BlockSpec((1, 2, rows, slab), lambda q, me: (q, 0, 0, 0)),
            pl.BlockSpec((1, 1, slab), lambda q, me: (q, 0, 0)),
        ],
        out_specs=[
            pl.BlockSpec((n, 1, 2, rows, width), lambda q, me: (0, q, 0, 0, 0)) for n in counts
        ]
        + [pl.BlockSpec(TOKEN.shape, lambda q, me: (0, 0))],
    )
    return pl.pallas_call(
        lambda *refs: shift_kernel(order, *refs),
        grid_spec=grid_spec,
        out_shape=[
            jax.ShapeDtypeStruct((n, points, 2, rows, width), jnp.bfloat16) for n in counts
        ]
        + [TOKEN],
        compiler_params=params(),
        cost_estimate=cost(8 * con.size, 4 * con.size),
    )(me, con, shift_map.reshape(points, 1, slab))


def x_kernel(slots, waits, me_ref, *refs):
    val_refs, weight_ref = refs[:slots], refs[slots]
    go_ref, keep_ref, token_ref, left_ref = refs[slots + 1 + waits :]
    _, _, _, rows, depth = val_refs[0].shape
    half = slots * rows
    token_ref[...] = jnp.zeros_like(token_ref)
    step = pl.program_id(0)
    halfway = pl.num_programs(0) // 2

    @pl.when(step == 0)
    def _():
        for slot in range(slots):
            real, imag = val_refs[slot][0, 0, 0], val_refs[slot][0, 0, 1]
            top = slice(slot * rows, (slot + 1) * rows)
            low = slice(half + slot * rows, half + (slot + 1) * rows)
            left_ref[top, 0:depth] = real
            left_ref[top, depth : 2 * depth] = -imag
            left_ref[low, 0:depth] = imag
            left_ref[low, depth : 2 * depth] = real

    weight = weight_ref[0].reshape(2 * depth, weight_ref.shape[3])

    @pl.when(step < halfway)
    def _():
        encode(mm(left_ref[...], weight), go_ref)

    @pl.when(step >= halfway)
    def _():
        keep_ref[...] = mm(left_ref[...], weight)


def x_call(vals, screened, place, point, me, steps, after):
    slots = len(vals)
    _, _, _, rows, depth = vals[0][0].shape
    height = 2 * slots * rows
    columns = screened.shape[3] // 2
    half = steps // 2
    width = columns // half
    grid_spec = pltpu.PrefetchScalarGridSpec(
        num_scalar_prefetch=1,
        grid=(steps,),
        in_specs=[
            pl.BlockSpec((1, 1, 2, rows, depth), lambda j, me, slot=slot: (slot, place, 0, 0, 0))
            for _, slot in vals
        ]
        + [
            pl.BlockSpec(
                (1, 2, depth, width),
                lambda j, me: (point, 0, 0, ((me[0] + 1 + j // half) % 2) * half + j % half),
            )
        ]
        + [pl.BlockSpec(memory_space=pl.ANY) for _ in after],
        out_specs=[
            pl.BlockSpec((height + EXP_ROWS, width), lambda j, me: (0, jnp.minimum(j, half - 1))),
            pl.BlockSpec((height, width), lambda j, me: (0, jnp.maximum(j - half, 0))),
            pl.BlockSpec(TOKEN.shape, lambda j, me: (0, 0)),
        ],
        scratch_shapes=[pltpu.VMEM((height, 2 * depth), jnp.bfloat16)],
    )
    return pl.pallas_call(
        lambda *refs: x_kernel(slots, len(after), *refs),
        grid_spec=grid_spec,
        out_shape=[
            jax.ShapeDtypeStruct((height + EXP_ROWS, columns), jnp.int16),
            jax.ShapeDtypeStruct((height, columns), jnp.float32),
            TOKEN,
        ],
        compiler_params=params(),
        cost_estimate=cost(
            2 * height * 2 * depth * 2 * columns, 8 * depth * columns + 6 * height * columns
        ),
    )(me, *[v for v, _ in vals], screened, *after)


def hop_kernel(heard, me_ref, keep_ref, *refs):
    total = keep_ref[...]
    for ref in refs[:heard]:
        total = total + decode(ref)
    out_ref, token_ref = refs[-2:]
    encode(total, out_ref)
    token_ref[...] = jnp.zeros_like(token_ref)


def hop_call(keep, others, me, stage, width, after):
    height, tall = keep.shape[0], others[0].shape[0]
    steps = width // 128

    def at(known):
        return lambda i, me: (0, block_of(me[0], known, stage + 1, True) * steps + i)

    grid_spec = pltpu.PrefetchScalarGridSpec(
        num_scalar_prefetch=1,
        grid=(steps,),
        in_specs=[pl.BlockSpec((height, 128), at(1))]
        + [pl.BlockSpec((tall, 128), at(n + 1)) for n in range(len(others))]
        + [pl.BlockSpec(memory_space=pl.ANY) for _ in after],
        out_specs=[
            pl.BlockSpec((tall, 128), lambda i, me: (0, i)),
            pl.BlockSpec(TOKEN.shape, lambda i, me: (0, 0)),
        ],
    )
    return pl.pallas_call(
        lambda *refs: hop_kernel(len(others), *refs),
        grid_spec=grid_spec,
        out_shape=[jax.ShapeDtypeStruct((tall, width), jnp.int16), TOKEN],
        compiler_params=params(),
        cost_estimate=cost(20 * height * width, 8 * height * width),
    )(me, keep, *others, *after)


def fold_kernel(own_ref, heard_ref, keep_ref, go_ref):
    rows = keep_ref.shape[1]
    for n in range(own_ref.shape[0]):
        total = own_ref[n] + decode(heard_ref.at[n])
        keep_ref[n] = total[:rows]
        encode(total[rows:], go_ref.at[n])


def fold_call(own, heard):
    count, rows, cols = own.shape
    shapes = [
        jax.ShapeDtypeStruct((count, rows // 2, cols), jnp.float32),
        jax.ShapeDtypeStruct((count, rows // 2 + EXP_ROWS, cols), jnp.int16),
    ]
    return pl.pallas_call(
        fold_kernel,
        out_shape=shapes,
        compiler_params=params(),
        cost_estimate=cost(20 * own.size, 10 * own.size),
    )(own, heard)


def split_sums(sums_ref, keep_ref, go_ref):
    half, points, rows, width = keep_ref.shape
    keep_ref[...] = sums_ref[0:half]
    encode(sums_ref[half:].reshape(half * points * rows, width), go_ref, SMALL)


def split_shapes(slots, points, rows):
    count = slots // 2 * points * rows
    return [
        jax.ShapeDtypeStruct((slots // 2, points, rows, 128), jnp.float32),
        jax.ShapeDtypeStruct((count + exp_rows(count, SMALL), 128), jnp.int16),
    ]


def pack_point(own_ref, heard_ref, out_ref):
    slots, rows, _ = out_ref.shape
    width = own_ref.shape[1]
    count = width // slots
    first = lax.broadcasted_iota(jnp.int32, (rows, 128), 1) < 64
    total = own_ref[...] + decode(heard_ref)
    for slot in range(slots):
        tile, lane = divmod(slot * count, 128)
        reach = min(width, (tile + (1 if lane + count <= 128 else 2)) * 128)
        piece = total[:, tile * 128 : reach]
        if lane:
            piece = pltpu.roll(piece, reach - tile * 128 - lane, 1)
        real, imag = piece[:rows, :128], piece[rows:, :128]
        out_ref[slot] = jnp.where(first, real, pltpu.roll(imag, 64, 1))


def pack_call(own, heard, slots):
    rows, cols = own.shape
    return pl.pallas_call(
        pack_point,
        out_shape=jax.ShapeDtypeStruct((slots, rows // 2, 128), jnp.float32),
        compiler_params=params(),
        cost_estimate=cost(20 * own.size, 10 * own.size),
    )(own, heard)


def gather_kernel(own_ref, heard_ref, *refs):
    *packed_refs, keep_ref, go_ref, sums_ref = refs
    for n, ref in enumerate(packed_refs):
        sums_ref[:, n] = ref[...]
    pack_point(own_ref, heard_ref, sums_ref.at[:, len(packed_refs)])
    split_sums(sums_ref, keep_ref, go_ref)


def gather_call(own, heard, packed):
    slots, rows, _ = packed[0].shape
    shape = (slots, len(packed) + 1, rows)
    return pl.pallas_call(
        gather_kernel,
        out_shape=split_shapes(*shape),
        scratch_shapes=[pltpu.VMEM(shape + (128,), jnp.float32)],
        compiler_params=params(),
        cost_estimate=cost(60 * own.size, 30 * own.size),
    )(own, heard, *packed)


def merge_kernel(own_ref, heard_ref, *refs):
    slots, points, rows, width = own_ref.shape
    count = slots * points * rows
    sums_ref = refs[-1]
    heard = decode(heard_ref, count, SMALL)
    sums_ref[...] = own_ref[...] + heard.reshape(slots, points, rows, width)
    if slots > 1:
        split_sums(sums_ref, *refs[:-1])


def merge_call(own, heard):
    last = own.shape[0] == 1
    sums = jax.ShapeDtypeStruct(own.shape, jnp.float32)
    return pl.pallas_call(
        merge_kernel,
        out_shape=sums if last else split_shapes(*own.shape[:3]),
        scratch_shapes=[] if last else [pltpu.VMEM(own.shape, jnp.float32)],
        compiler_params=params(),
        cost_estimate=cost(20 * own.size, 10 * own.size),
    )(own, heard)


def exchange_kernel(slots, waits, *refs):
    here_refs, (there_ref, coulomb_ref) = refs[:slots], refs[slots : slots + 2]
    out_ref, token_ref, left_ref = refs[slots + 2 + waits :]
    _, _, rows, depth = here_refs[0].shape
    token_ref[...] = jnp.zeros_like(token_ref)

    @pl.when(pl.program_id(0) == 0)
    def _():
        for slot in range(slots):
            for part in range(2):
                left_ref[
                    slot * rows : (slot + 1) * rows, part * depth : (part + 1) * depth
                ] = here_refs[slot][0, part]

    factor = coulomb_ref[0]
    real = there_ref[0, 0].astype(jnp.float32) * factor
    imag = there_ref[0, 1].astype(jnp.float32) * factor
    right = jnp.concatenate(
        [jnp.concatenate([real, -imag], axis=1), jnp.concatenate([imag, real], axis=1)], axis=0
    )
    high, low = halves(right)
    left = left_ref[...]
    both = mm_nt(left, high) + mm_nt(left, low)
    cols = both.shape[1] // 2
    for part in range(2):
        out_ref[0, part] = both[:, part * cols : (part + 1) * cols]


def exchange_call(heres, there, coulomb, after):
    slots, rows = len(heres), heres[0][0].shape[2]
    points, _, cols, depth = there.shape
    height = slots * rows
    return pl.pallas_call(
        lambda *refs: exchange_kernel(slots, len(after), *refs),
        grid=(points,),
        in_specs=[
            pl.BlockSpec((1,) + h.shape[1:], lambda q, slot=slot: (slot, 0, 0, 0))
            for h, slot in heres
        ]
        + [
            pl.BlockSpec((1, 2, cols, depth), lambda q: (q, 0, 0, 0)),
            pl.BlockSpec((1, 1, depth), lambda q: (q, 0, 0)),
        ]
        + [pl.BlockSpec(memory_space=pl.ANY) for _ in after],
        out_specs=[
            pl.BlockSpec((1, 2, height, cols), lambda q: (q, 0, 0, 0)),
            pl.BlockSpec(TOKEN.shape, lambda q: (0, 0)),
        ],
        out_shape=[jax.ShapeDtypeStruct((points, 2, height, cols), jnp.float32), TOKEN],
        scratch_shapes=[pltpu.VMEM((height, 2 * depth), jnp.bfloat16)],
        compiler_params=params(),
        cost_estimate=cost(2 * points * height * 2 * cols * 2 * depth * 2, 8 * points * cols * depth),
    )(*[h for h, _ in heres], there, coulomb.reshape(points, 1, depth), *after)


def tile_kernel(order, heard, chunks, waits, me_ref, *refs):
    slots = len(order)
    con_refs, keep_ref = refs[:slots], refs[slots]
    heard_refs = refs[slots + 1 : slots + 1 + heard]
    exch_ref, row_ref, col_direct_ref, col_exch_ref = refs[slots + 1 + heard : slots + 5 + heard]
    keep_out, go_out, token_ref, con_all, direct_ref, natural_ref, sums_ref = refs[
        slots + 5 + heard + waits :
    ]
    token_ref[...] = jnp.zeros_like(token_ref)
    total = keep_ref[...]
    for ref in heard_refs:
        total = total + decode(ref)
    pairs, width = total.shape[0] // 2, total.shape[1]
    rows = con_refs[0].shape[3]
    pitch = con_all.shape[0] // slots
    for slot in range(slots):
        for part in range(2):
            con_all[
                slot * pitch : slot * pitch + rows, part * width : (part + 1) * width
            ] = con_refs[slot][0, 0, part]
    real, imag = total[:pairs], total[pairs:]
    right = jnp.concatenate(
        [jnp.concatenate([real, -imag], axis=1), jnp.concatenate([imag, real], axis=1)], axis=0
    )
    high, low = halves(right)
    left = con_all[...]
    direct = mm_nt(left, high) + mm_nt(left, low)
    lanes = direct_ref.shape[0]
    for slot in range(slots):
        start = pl.multiple_of(jnp.bitwise_xor(me_ref[0], order[slot]) * rows, 8)
        for lane in range(lanes):
            direct_ref[lane, pl.ds(start, rows), :] = direct[
                slot * pitch : slot * pitch + rows, lane * 128 : (lane + 1) * 128
            ]
    group = 128 // NV
    place = lax.broadcasted_iota(jnp.int32, (NC, 128), 1) // NV
    per_part = lanes // 2
    for part in range(2):
        for chunk in range(NC // group):
            for band in range(NV):
                block = jnp.zeros((NC, 128), jnp.float32)
                for step in range(group):
                    e = chunk * group + step
                    piece = direct_ref[part * per_part + band // group, pl.ds(e, NC, stride=NC), :]
                    turn = (NV * (step - band)) % 128
                    if turn:
                        piece = pltpu.roll(piece, turn, 1)
                    block = jnp.where(place == step, piece, block)
                natural_ref[
                    part, band * NC : (band + 1) * NC, chunk * 128 : (chunk + 1) * 128
                ] = block
    pick_rows = row_ref[...]
    count = NT // chunks
    for part in range(2):
        result = None
        for source, pick_cols in (
            (natural_ref[part], col_direct_ref),
            (exch_ref[0, part], col_exch_ref),
        ):
            for piece in halves(source):
                moved = mm(pick_rows, piece).astype(jnp.bfloat16)
                term = mm(moved, pick_cols[...])
                result = term if result is None else result + term
        for chunk in range(chunks):
            at = (2 * chunk + part) * count
            sums_ref[at : at + count, :] = result[chunk * count : (chunk + 1) * count]
    stays = keep_out.shape[0]
    keep_out[...] = sums_ref[0:stays, :]
    encode(sums_ref[stays:, :], go_out)


def tile_call(
    cons, point, keep, heard, exch, me, order, pick_rows, col_direct, col_exch, chunks, after
):
    slots = len(cons)
    _, _, _, rows, width = cons[0][0].shape
    height, tall = keep.shape[0], heard[0].shape[0]
    pitch = -(-rows // 16) * 16
    out_cols = col_direct.shape[1]
    stages = len(heard)
    whole = lambda a: pl.BlockSpec(a.shape, lambda i, me: (0,) * len(a.shape))
    shapes = [
        jax.ShapeDtypeStruct((NT, out_cols), jnp.float32),
        jax.ShapeDtypeStruct((NT + EXP_ROWS, out_cols), jnp.int16),
        TOKEN,
    ]

    def at(known):
        return lambda i, me: (0, block_of(me[0], known, stages, False))

    grid_spec = pltpu.PrefetchScalarGridSpec(
        num_scalar_prefetch=1,
        grid=(1,),
        in_specs=[
            pl.BlockSpec((1, 1, 2, rows, width), lambda i, me, place=place: (place, point, 0, 0, 0))
            for _, place in cons
        ]
        + [pl.BlockSpec((height, width), at(1))]
        + [pl.BlockSpec((tall, width), at(n + 1)) for n in range(stages)]
        + [
            pl.BlockSpec((1,) + exch.shape[1:], lambda i, me: (point, 0, 0, 0)),
            whole(pick_rows),
            whole(col_direct),
            whole(col_exch),
        ]
        + [pl.BlockSpec(memory_space=pl.ANY) for _ in after],
        out_specs=[whole(a) for a in shapes],
        scratch_shapes=[
            pltpu.VMEM((slots * pitch, 2 * width), jnp.bfloat16),
            pltpu.VMEM((height // 128, NC * NC, 128), jnp.float32),
            pltpu.VMEM((2, NT, NT), jnp.float32),
            pltpu.VMEM((2 * NT, out_cols), jnp.float32),
        ],
    )
    return pl.pallas_call(
        lambda *refs: tile_kernel(order, stages, chunks, len(after), *refs),
        grid_spec=grid_spec,
        out_shape=shapes,
        compiler_params=params(),
        cost_estimate=cost(2.8e9, 8e6),
    )(me, *[c for c, _ in cons], keep, *heard, exch, pick_rows, col_direct, col_exch, *after)


def swap(value, axis, size, bit):
    return lax.ppermute(value, axis, [(i, i ^ bit) for i in range(size)])


def halving_order(bits):
    order = [0]
    for bit in reversed(bits):
        order = order + [o ^ bit for o in order]
    return order


def behind(value, token):
    return lax.optimization_barrier((value, token))[0]


def on_device(*args):
    (val_density, con_density, screened, coulomb, trans_here, trans_there, shift_map, ordering) = args
    ga, pair = lax.axis_size("ga"), lax.axis_size("pair")
    points = con_density.shape[1]
    slab = con_density.shape[3]
    width = slab // ga
    me_ga, me_pair = lax.axis_index("ga"), lax.axis_index("pair")
    me = me_ga.astype(jnp.int32).reshape(1)
    ga_bits = [1 << b for b in range(ga.bit_length() - 1)]
    pair_bits = [1 << b for b in range(pair.bit_length() - 1)]
    ga_order = halving_order(ga_bits)
    stages, half = len(ga_bits), ga // 2

    val = jnp.transpose(val_density, (1, 2, 0, 3))
    vals = {0: (val[None], 0)}
    for bit in reversed(pair_bits):
        known = sorted(vals)
        got = swap(
            jnp.concatenate([vals[r][0][vals[r][1] :][:1] for r in known]), "pair", pair, bit
        )
        for place, slot in enumerate(known):
            vals[slot ^ bit] = (got, place)

    con = jnp.transpose(behind(con_density, val), (1, 2, 0, 3))
    *stay, go, token = shift_call(con, shift_map, me, ga_order, width)
    nearest = ga_bits[0]
    from_near = swap(go, "ga", ga, nearest)
    cons = {0: (stay[0], 0)}
    for slot, block in zip(ga_order[1:half], stay[1:]):
        if slot & ga_bits[-1]:
            cons[slot] = (swap(block, "ga", ga, slot), 0)

    row_count, col_count = NT // pair, NT // ga
    row_slots = jnp.asarray(halving_order(pair_bits), jnp.int32)
    row_trans = ordering.reshape(pair, row_count)[me_pair ^ row_slots].reshape(-1)
    at_row = ((row_trans // row_count) ^ me_pair) * row_count + row_trans % row_count
    pick_rows = (at_row[:, None] == jnp.arange(NT, dtype=jnp.int32)[None, :]).astype(jnp.bfloat16)
    col_trans = ordering.reshape(ga, col_count)[me_ga ^ jnp.asarray(ga_order, jnp.int32)]
    col_trans = col_trans.reshape(1, -1)
    at_direct = (col_trans % NC) * NV + col_trans // NC
    at_exch = jnp.where(col_trans // row_count == me_pair, col_trans % row_count, -1)

    def pick_cols(at, size, scale):
        hot = at == jnp.arange(size, dtype=jnp.int32)[:, None]
        return jnp.where(hot, scale, 0.0).astype(jnp.bfloat16)

    col_direct, col_exch = pick_cols(at_direct, NT, -1.0), pick_cols(at_exch, row_count, 2.0)

    there = jnp.transpose(trans_there, (1, 2, 0, 3))
    arrived = [block for block, _ in cons.values()]
    token = behind(token, (there, pick_rows, col_direct, col_exch, arrived))
    order = [("x", q, 0) for q in range(points)]
    hops = [(2 * q + s, q, s) for q in range(points) for s in range(1, stages)]
    order += [("hop", q, s) for _, q, s in sorted(hops)]
    order += [("tile", q, stages) for q in range(points)]
    gone, keep, heard = [], [], []
    tiles = [None] * points
    for kind, q, stage in order:
        if kind == "x":
            coded, own, token = x_call(
                [vals[slot] for slot in range(pair)], screened, q, q, me, 4, [token]
            )
            keep.append(own)
            heard.append([swap(coded, "ga", ga, ga_bits[0])])
            if q == 0:
                stay, from_near = behind((stay, from_near), token)
                cons[nearest] = (from_near, 0)
                for place, slot in enumerate(ga_order[1:half], 1):
                    sent = from_near[place : place + 1]
                    if slot in cons:
                        cons[slot ^ nearest] = (swap(sent, "ga", ga, slot), 0)
                    else:
                        both = swap(jnp.concatenate([stay[place], sent]), "ga", ga, slot)
                        cons[slot], cons[slot ^ nearest] = (both, 0), (both, 1)
                cons = [cons[slot] for slot in ga_order]
        elif kind == "hop":
            columns = (ga >> (stage + 1)) * width
            if (q, stage) == (0, 1):
                token = behind(token, [c for c, _ in cons])
            if q > 0 and stage == stages - 1:
                token = behind(token, heard[q - 1][-1])
            coded, token = hop_call(keep[q], heard[q], me, stage, columns, [token])
            heard[q].append(swap(coded, "ga", ga, ga_bits[stage]))
            if (q, stage) == (0, 1):
                heres = {0: jnp.transpose(behind(trans_here, token), (1, 0, 2))}
                for bit in reversed(pair_bits):
                    for slot in sorted(heres):
                        heres[slot ^ bit] = swap(heres[slot], "pair", pair, bit)
            if (q, stage) == (1, 1):
                slots = [(heres[slot][None], 0) for slot in range(pair)]
                exch, token = exchange_call(slots, there, coulomb, [token])
        else:
            own, sent, token = tile_call(
                cons, q, keep[q], heard[q], exch, me, ga_order, pick_rows, col_direct,
                col_exch, pair, [token],
            )
            for bit in pair_bits[:-1]:
                own, sent = fold_call(own[None], swap(sent[None], "pair", pair, bit))
                own, sent = own[0], sent[0]
            tiles[q] = own, swap(sent, "pair", pair, pair_bits[-1])

    own, sent = gather_call(*tiles[-1], [pack_call(*tile, ga) for tile in tiles[:-1]])
    for bit in ga_bits[:-1]:
        own, sent = merge_call(own, swap(sent, "ga", ga, bit))
    total = merge_call(own, swap(sent, "ga", ga, ga_bits[-1]))[0]
    out = total.reshape(points, row_count, 2, 64)[..., :col_count]
    return jnp.transpose(out, (0, 2, 1, 3))


def contract_float(left, right):
    high = lax.Precision.HIGHEST
    real_part = jnp.einsum(
        "nkg,mkg->nkm", left[:, :, 0], right[:, :, 0], precision=high
    ) - jnp.einsum("nkg,mkg->nkm", left[:, :, 1], right[:, :, 1], precision=high)
    imag_part = jnp.einsum(
        "nkg,mkg->nkm", left[:, :, 0], right[:, :, 1], precision=high
    ) + jnp.einsum("nkg,mkg->nkm", left[:, :, 1], right[:, :, 0], precision=high)
    return jnp.stack([real_part, imag_part], axis=2)


def times_cols(rows, weights):
    first = jnp.einsum(
        "nkh,kgh->nkg", rows[:, :, 0], weights[:, 0], preferred_element_type=jnp.float32
    ) - jnp.einsum("nkh,kgh->nkg", rows[:, :, 1], weights[:, 1], preferred_element_type=jnp.float32)
    second = jnp.einsum(
        "nkh,kgh->nkg", rows[:, :, 0], weights[:, 1], preferred_element_type=jnp.float32
    ) + jnp.einsum("nkh,kgh->nkg", rows[:, :, 1], weights[:, 0], preferred_element_type=jnp.float32)
    return jnp.stack([first, second], axis=2)


def on_any_device(
    val_density, con_density, screened, coulomb, trans_here, trans_there, shift_map, ordering
):
    con_count = con_density.shape[0]
    points = con_density.shape[1]
    slab_cols = con_density.shape[3]
    blocks = slab_cols // GBLK
    within = (shift_map % GBLK).reshape(points, blocks, GBLK)
    onehot = (
        within[:, :, :, None] == jnp.arange(GBLK, dtype=jnp.int32)[None, None, None, :]
    ).astype(jnp.bfloat16)
    con_blocks = con_density.reshape(con_count, points, 2, blocks, GBLK)
    shifted = (
        jnp.einsum("bkpnh,kngh->bkpng", con_blocks, onehot, preferred_element_type=jnp.float32)
        .astype(jnp.bfloat16)
        .reshape(con_density.shape)
    )
    whole_here = lax.all_gather(trans_here, "pair", axis=0, tiled=True).astype(jnp.float32)
    weighted = trans_there.astype(jnp.float32) * coulomb[None, :, None, :]
    high = lax.Precision.HIGHEST
    exch_real = jnp.einsum(
        "tg,skg->tks", whole_here[:, 0], weighted[:, :, 0], precision=high
    ) - jnp.einsum("tg,skg->tks", whole_here[:, 1], weighted[:, :, 1], precision=high)
    exch_imag = jnp.einsum(
        "tg,skg->tks", whole_here[:, 0], weighted[:, :, 1], precision=high
    ) + jnp.einsum("tg,skg->tks", whole_here[:, 1], weighted[:, :, 0], precision=high)
    exch_part = jnp.stack([exch_real, exch_imag], axis=2)
    whole_con = lax.all_gather(shifted, "ga", axis=0, tiled=True)
    screened_rows = lax.psum_scatter(
        times_cols(whole_con, screened), "pair", scatter_dimension=0, tiled=True
    )
    direct_part = contract_float(
        lax.all_gather(val_density, "pair", axis=0, tiled=True).astype(jnp.float32), screened_rows
    )
    direct_sum, exch_sum = lax.psum((direct_part, exch_part), "ga")
    direct_full, exch_full = (
        lax.all_gather(direct_sum, "pair", axis=3, tiled=True),
        lax.all_gather(exch_sum, "pair", axis=3, tiled=True),
    )
    row_count = NT // lax.axis_size("pair")
    col_count = NT // lax.axis_size("ga")
    row_trans = lax.dynamic_slice_in_dim(ordering, lax.axis_index("pair") * row_count, row_count, 0)
    col_trans = lax.dynamic_slice_in_dim(ordering, lax.axis_index("ga") * col_count, col_count, 0)
    row_pairs = (row_trans // NC)[:, None] * NV + (col_trans // NC)[None, :]
    col_pairs = (row_trans % NC)[:, None] * NC + (col_trans % NC)[None, :]
    picked = direct_full[row_pairs.reshape(-1)]
    col_mask = (
        col_pairs.reshape(-1)[:, None] == jnp.arange(direct_full.shape[3], dtype=jnp.int32)[None, :]
    ).astype(jnp.float32)
    direct_flat = jnp.sum(picked * col_mask[:, None, None, :], axis=3)
    direct_sel = jnp.transpose(direct_flat.reshape(row_count, col_count, points, 2), (2, 3, 0, 1))
    exch_picked = exch_full[row_trans]
    col_hot = (jnp.arange(NT, dtype=jnp.int32)[:, None] == col_trans[None, :]).astype(jnp.float32)
    exch_sel = jnp.einsum("rkpt,tc->kprc", exch_picked, col_hot, precision=high)
    return 2.0 * exch_sel - direct_sel


def solution(mesh):
    in_specs = (
        P("pair", None, None, "ga"),
        P("ga", None, None, "pair"),
        P(None, None, "ga", "pair"),
        P(None, "ga"),
        P("pair", None, "ga"),
        P("pair", None, None, "ga"),
        P(None, "pair"),
        P(),
    )
    out_specs = P(None, None, "pair", "ga")

    def run(*args):
        ga, pair = mesh.shape["ga"], mesh.shape["pair"]
        con_count, h_count = args[1].shape[0], args[1].shape[3]
        suits = (
            ga & (ga - 1) == 0
            and pair & (pair - 1) == 0
            and ga >= 4
            and pair >= 4
            and NT % (pair * GROUP // 2) == 0
            and h_count % (ga * pair * GBLK) == 0
            and con_count % (8 * ga) == 0
            and args[0].shape[0] % (16 * pair) == 0
            and NT % (16 * pair) == 0
            and NT // ga <= 64
            and args[1].shape[1] * NT % (pair * SMALL) == 0
        )
        body = on_device if suits else on_any_device
        return jax.shard_map(
            body, mesh=mesh, in_specs=in_specs, out_specs=out_specs, check_vma=False
        )(*args)

    return run
```
